32 devices in a mesh: section: 2 (over x), batch: 16 (over z, y, core).
Axes of the slice: x: 2, y: 2, z: 4, core: 2. Of those that a mesh axis runs over, the one named last changes fastest.
Arguments:
- frames: bfloat16 [6144, 4, 84, 84], P('batch'), may hold values from 0 to 1
- next_frames: bfloat16 [6144, 4, 84, 84], P('batch'), may hold values from 0 to 1
- actions: int32 [6144], P('batch'), may hold values from 0 to 17
- next_actions: int32 [6144], P('batch'), may hold values from 0 to 17
- lengths: int32 [6144], P('batch'), may hold values from 1 to 3
- terminal: int32 [6144], P('batch'), may hold values 0 or 1
- rewards: float32 [6144, 3], P('batch'), may hold values from -1 to 1
- discounts: float32 [6144, 3], P('batch'), may hold values from 0.85 to 0.999
- owners: int32 [6144, 1], P('batch'), may hold values from 0 to 15; in each aligned block of 384 rows (0 to 383, 384 to 767, ...) at most 25 rows name the same one
- conv_one_weight: bfloat16 [32, 4, 8, 8], replicated, may hold values from -0.375 to 0.375
- conv_one_offset: bfloat16 [32], replicated, may hold values from -1 to 1
- conv_two_weight: bfloat16 [64, 32, 4, 4], replicated, may hold values from -0.25 to 0.25
- conv_two_offset: bfloat16 [64], replicated, may hold values from -1 to 1
- conv_three_weight: bfloat16 [64, 64, 3, 3], replicated, may hold values from -0.25 to 0.25
- conv_three_offset: bfloat16 [64], replicated, may hold values from -1 to 1
- dense_one_weight: bfloat16 [3136, 512], replicated, may hold values from -0.109375 to 0.109375
- dense_one_offset: bfloat16 [512], replicated, may hold values from -1 to 1
- dense_two_weight: bfloat16 [512, 918], replicated, may hold values from -0.75 to 0.75
- dense_two_offset: bfloat16 [918], replicated, may hold values from -1.5 to 1.5
- target_conv_one_weight: bfloat16 [32, 4, 8, 8], replicated, may hold values from -0.375 to 0.375
- target_conv_one_offset: bfloat16 [32], replicated, may hold values from -1 to 1
- target_conv_two_weight: bfloat16 [64, 32, 4, 4], replicated, may hold values from -0.25 to 0.25
- target_conv_two_offset: bfloat16 [64], replicated, may hold values from -1 to 1
- target_conv_three_weight: bfloat16 [64, 64, 3, 3], replicated, may hold values from -0.25 to 0.25
- target_conv_three_offset: bfloat16 [64], replicated, may hold values from -1 to 1
- target_dense_one_weight: bfloat16 [3136, 512], replicated, may hold values from -0.109375 to 0.109375
- target_dense_one_offset: bfloat16 [512], replicated, may hold values from -1 to 1
- target_dense_two_weight: bfloat16 [512, 918], replicated, may hold values from -0.75 to 0.75
- target_dense_two_offset: bfloat16 [918], replicated, may hold values from -1.5 to 1.5
Outputs:
- mean_loss: float32 [], replicated
- frames_grad: bfloat16 [6144, 4, 84, 84], P('batch', 'section')
- grad_conv_one_weight: float32 [32, 4, 8, 8], P('section')
- grad_conv_one_offset: float32 [32], P('section')
- grad_conv_two_weight: float32 [64, 32, 4, 4], P('section')
- grad_conv_two_offset: float32 [64], P('section')
- grad_conv_three_weight: float32 [64, 64, 3, 3], P('section')
- grad_conv_three_offset: float32 [64], P('section')
- grad_dense_one_weight: float32 [3136, 512], P('section')
- grad_dense_one_offset: float32 [512], P('section')
- grad_dense_two_weight: float32 [512, 918], P('section')
- grad_dense_two_offset: float32 [918], P('section')
- priority_table: float32 [16, 16, 25], P('batch', 'section')
The draws below stay inside these ranges and needn't reach their ends.
Inputs may be any that keep to these rules, and one draw needn't show every extreme that they name: `owners`: within the transitions of one device (an aligned block of 384) no owner is named more than 25 times, a bound that some block reaches.
All inputs are finite; a program needn't handle non-finite values. No bound on the sum of `terminal` on one device may be relied on, other than what follows from the above.
Results may differ from the reference program's by a relative error of at most 0.012.
Values may be sent and summed in bfloat16 or wider, within the bound.
A program may use at most 448 MiB of HBM per device.

```python
import math
import jax
import jax.numpy as jnp
import numpy as np
from jax import lax

FRAME = 84
STACK = 4
C1 = 32
C2 = 64
C3 = 64
HID = 512
ACTIONS = 18
ATOMS = 51
NSTEP = 3
TRANS_DEV = 384
FLAT = 3136
TRANS = 6144
CAP = 25
N_BATCH = 16


def set_ends(drawn, rng, least, top_value):
    dims = drawn.shape
    index_at = [jax.random.randint(jax.random.fold_in(rng, axis), (), 0, dims[axis]) for axis in range(len(dims))]
    drawn = drawn.at[tuple(index_at)].set(least)
    longest = dims.index(max(dims))
    index_at[longest] = (index_at[longest] + 1) % dims[longest]
    return drawn.at[tuple(index_at)].set(top_value)


def block_scale(own_key, shape, shards, low, top_value):
    gain, own = 1.0, jax.random.fold_in(own_key, 6)
    for dim, shards_of in shards:
        steps = jnp.exp(jax.random.uniform(jax.random.fold_in(own, dim), (shards_of,), jnp.float32, low / len(shards), top_value / len(shards)))
        gain = gain * jnp.repeat(steps, shape[dim] // shards_of).reshape([-1 if axis == dim else 1 for axis in range(len(shape))])
    return gain


def shared_out(key, own, number, rows, number_of, top, reach, slope):
    sequence = jax.random.permutation(key, number_of)
    packed, common = portions_of(number_of, rows * top, reach, slope, True), portions_of(number_of, rows * top, reach, slope, False)
    places = jnp.arange(number_of)

    def named(tallies, rotation):
        used = int((tallies > 0).sum())
        fixed = max(1, used // 4)
        moved = fixed + (places - fixed + rotation * (used - fixed)) % max(1, number_of - fixed)
        return jnp.zeros((number_of,), jnp.int32).at[sequence[jnp.where(places < fixed, places, moved)]].set(jnp.asarray(tallies, jnp.int32))

    tallies = jnp.where(number % 4 == 0, named(packed, number // 4), named(common, number - number // 4 - 1))
    mixed = jax.random.permutation(jax.random.fold_in(own, 3), number_of)
    giver, receiver = mixed[0:number_of // 2 * 2:2], mixed[1:number_of // 2 * 2:2]
    room = jnp.minimum(tallies[giver] - 1, reach - tallies[receiver]) // 2
    room = jnp.where((giver == sequence[0]) | (receiver == sequence[0]) | (tallies[receiver] == 0), 0, jnp.maximum(room, 0))
    moved = jax.random.randint(jax.random.fold_in(own, 4), (number_of // 2,), 0, 1 << 20) % (room + 1)
    tallies = tallies.at[giver].add(-moved).at[receiver].add(moved)
    labels = jnp.searchsorted(jnp.cumsum(tallies), jnp.arange(rows * top), side="right").astype(jnp.int32)
    table = labels.reshape(top, rows).T
    table = table[jax.random.permutation(jax.random.fold_in(own, 1), rows)]
    rotation = jax.random.randint(jax.random.fold_in(own, 2), (rows, 1), 0, top)
    return jnp.take_along_axis(table, (jnp.arange(top)[None, :] + rotation) % top, axis=1)


def portions_of(number_of, total, bound, slope, full):
    weights = [(1 << 20) // math.isqrt(grade ** slope) + 1 for grade in range(1, number_of + 1)]
    largest = bound if full else min(bound, max(-(-total // number_of), total * weights[0] // sum(weights)))
    least = 1 if total - largest >= number_of - 1 else 0
    given, spare = [largest] + [least] * (number_of - 1), total - largest - least * (number_of - 1)
    while spare > 0:
        movable = [i for i in range(1, number_of) if given[i] < largest] or [i for i in range(1, number_of) if given[i] < bound]
        pool, budget = sum([weights[i] for i in movable]), spare
        for i in movable:
            addition = min(bound - given[i], max(1, budget * weights[i] // pool), spare)
            given[i] = given[i] + addition
            spare = spare - addition
    return np.array(given)


def noise(own_key, dims, scale, most, held_as=jnp.bfloat16):
    array = scale * jax.random.normal(own_key, dims, jnp.float32)
    return jnp.clip(array, min=-most, max=most).astype(held_as)


def setup_inputs(seed: int = 0) -> dict:
    arg_keys = jax.random.split(jax.random.key(seed), 30)
    frames = jnp.clip(1.0 * jax.random.uniform(arg_keys[0], (TRANS, STACK, FRAME, FRAME), jnp.float32) ** block_scale(arg_keys[0], (TRANS, STACK, FRAME, FRAME), ((0, 16),), -0.2, 0.2), 0.0, 1.0).astype(jnp.bfloat16)
    next_frames = jnp.clip(1.0 * jax.random.uniform(arg_keys[1], (TRANS, STACK, FRAME, FRAME), jnp.float32) ** block_scale(arg_keys[1], (TRANS, STACK, FRAME, FRAME), ((0, 16),), -0.2, 0.2), 0.0, 1.0).astype(jnp.bfloat16)
    actions = set_ends(jax.random.randint(arg_keys[2], (TRANS,), 0, ACTIONS), jax.random.fold_in(arg_keys[2], 1), 0, ACTIONS - 1).astype(jnp.int32)
    next_actions = set_ends(jax.random.randint(arg_keys[3], (TRANS,), 0, ACTIONS), jax.random.fold_in(arg_keys[3], 1), 0, ACTIONS - 1).astype(jnp.int32)
    lengths = set_ends(jax.random.randint(arg_keys[4], (TRANS,), 1, NSTEP + 1), jax.random.fold_in(arg_keys[4], 1), 1, NSTEP).astype(jnp.int32)
    terminal = set_ends((jax.random.randint(arg_keys[5], (TRANS,), 0, 8) < 1).astype(jnp.int32), jax.random.fold_in(arg_keys[5], 1), 0, 1)
    rewards = jnp.clip(jax.random.uniform(arg_keys[6], (TRANS, NSTEP), jnp.float32, -1.0, 1.0) * block_scale(arg_keys[6], (TRANS, NSTEP), ((0, 16),), -0.4, 0.0), -1.0, 1.0)
    discounts = jnp.clip(0.85 + 0.14899999 * jax.random.uniform(arg_keys[7], (TRANS, NSTEP), jnp.float32) ** block_scale(arg_keys[7], (TRANS, NSTEP), ((0, 16),), -0.2, 0.2), 0.85, 0.999)
    owners_keys = jax.random.split(jax.random.fold_in(arg_keys[8], 1), TRANS // TRANS_DEV)
    owners_turns = jax.random.permutation(jax.random.fold_in(arg_keys[8], 3), TRANS // TRANS_DEV)
    owners = jax.vmap(lambda own, number: shared_out(jax.random.fold_in(arg_keys[8], 2), own, number, TRANS_DEV, N_BATCH, 1, CAP, 2))(owners_keys, owners_turns).reshape((TRANS, 1))
    conv_one_weight = noise(arg_keys[9], (C1, STACK, 8, 8), (STACK * 64) ** -0.5, 0.375)
    conv_one_offset = noise(arg_keys[10], (C1,), 0.2, 1.0)
    conv_two_weight = noise(arg_keys[11], (C2, C1, 4, 4), (C1 * 16) ** -0.5, 0.25)
    conv_two_offset = noise(arg_keys[12], (C2,), 0.2, 1.0)
    conv_three_weight = noise(arg_keys[13], (C3, C2, 3, 3), (C2 * 9) ** -0.5, 0.25)
    conv_three_offset = noise(arg_keys[14], (C3,), 0.2, 1.0)
    dense_one_weight = noise(arg_keys[15], (FLAT, HID), FLAT ** -0.5, 0.109375)
    dense_one_offset = noise(arg_keys[16], (HID,), 0.2, 1.0)
    dense_two_weight = noise(arg_keys[17], (HID, ACTIONS * ATOMS), (HID // 8) ** -0.5, 0.75)
    dense_two_offset = noise(arg_keys[18], (ACTIONS * ATOMS,), 0.3, 1.5)
    target_conv_one_weight = noise(arg_keys[19], (C1, STACK, 8, 8), (STACK * 64) ** -0.5, 0.375)
    target_conv_one_offset = noise(arg_keys[20], (C1,), 0.2, 1.0)
    target_conv_two_weight = noise(arg_keys[21], (C2, C1, 4, 4), (C1 * 16) ** -0.5, 0.25)
    target_conv_two_offset = noise(arg_keys[22], (C2,), 0.2, 1.0)
    target_conv_three_weight = noise(arg_keys[23], (C3, C2, 3, 3), (C2 * 9) ** -0.5, 0.25)
    target_conv_three_offset = noise(arg_keys[24], (C3,), 0.2, 1.0)
    target_dense_one_weight = noise(arg_keys[25], (FLAT, HID), FLAT ** -0.5, 0.109375)
    target_dense_one_offset = noise(arg_keys[26], (HID,), 0.2, 1.0)
    target_dense_two_weight = noise(arg_keys[27], (HID, ACTIONS * ATOMS), (HID // 8) ** -0.5, 0.75)
    target_dense_two_offset = noise(arg_keys[28], (ACTIONS * ATOMS,), 0.3, 1.5)
    return {"frames": frames, "next_frames": next_frames, "actions": actions, "next_actions": next_actions, "lengths": lengths, "terminal": terminal, "rewards": rewards, "discounts": discounts, "owners": owners, "conv_one_weight": conv_one_weight, "conv_one_offset": conv_one_offset, "conv_two_weight": conv_two_weight, "conv_two_offset": conv_two_offset, "conv_three_weight": conv_three_weight, "conv_three_offset": conv_three_offset, "dense_one_weight": dense_one_weight, "dense_one_offset": dense_one_offset, "dense_two_weight": dense_two_weight, "dense_two_offset": dense_two_offset, "target_conv_one_weight": target_conv_one_weight, "target_conv_one_offset": target_conv_one_offset, "target_conv_two_weight": target_conv_two_weight, "target_conv_two_offset": target_conv_two_offset, "target_conv_three_weight": target_conv_three_weight, "target_conv_three_offset": target_conv_three_offset, "target_dense_one_weight": target_dense_one_weight, "target_dense_one_offset": target_dense_one_offset, "target_dense_two_weight": target_dense_two_weight, "target_dense_two_offset": target_dense_two_offset}


support_low = -10.0
support_high = 10.0

@jax.custom_vjp
def low(v):
    return lax.optimization_barrier(v.astype(jnp.bfloat16)).astype(jnp.float32)

@jax.custom_vjp
def low_back(v):
    return v

def low_keep(v):
    return (low(v), None)

def low_pass(kept, grad):
    return (grad,)

def back_keep(v):
    return (v, None)

def back_low(kept, grad):
    return (low(grad),)
low.defvjp(low_keep, low_pass)
low_back.defvjp(back_keep, back_low)

def convolve(inputs, kernel, offset, stride):
    result = lax.conv_general_dilated(inputs, kernel, (stride, stride), 'VALID', dimension_numbers=('NCHW', 'OIHW', 'NCHW'), precision=lax.Precision.HIGHEST)
    return result + offset[None, :, None, None]

def conv_tower(inputs, weight_one, offset_one, weight_two, offset_two, weight_three, offset_three):
    pre_one = low_back(convolve(inputs, weight_one, offset_one, 4))
    act_one = low(jax.nn.silu(pre_one))
    pre_two = low_back(convolve(act_one, weight_two, offset_two, 2))
    act_two = low(jax.nn.silu(pre_two))
    pre_three = low_back(convolve(act_two, weight_three, offset_three, 1))
    act_three = low(jax.nn.silu(pre_three))
    return low_back(act_three.reshape(act_three.shape[0], -1))

def dense_head(feature, weight_one, offset_one, weight_two, offset_two):
    hidden = low_back(jnp.dot(feature, weight_one, precision=lax.Precision.HIGHEST) + offset_one)
    active = low(jax.nn.silu(hidden))
    return low_back(jnp.dot(active, weight_two, precision=lax.Precision.HIGHEST) + offset_two)

def pick_action(logits, chosen_ids):
    shaped = logits.reshape(logits.shape[0], ACTIONS, ATOMS)
    action_hot = (chosen_ids[:, None] == jnp.arange(ACTIONS, dtype=jnp.int32)[None, :]).astype(jnp.float32)
    return lax.optimization_barrier(jnp.sum(shaped * action_hot[:, :, None], axis=1))

def projection(probabilities, rewards, discounts, lengths, terminal):
    step_ids = jnp.arange(NSTEP, dtype=jnp.int32)[None, :]
    inside_steps = (step_ids < lengths[:, None]).astype(jnp.float32)
    products = jnp.cumprod(discounts, axis=1)
    earlier = jnp.concatenate([jnp.ones_like(products[:, :1]), products[:, :-1]], axis=1)
    returns = lax.optimization_barrier(jnp.sum(inside_steps * earlier * rewards, axis=1))
    final_step = (step_ids == lengths[:, None] - 1).astype(jnp.float32)
    bootstrap = lax.optimization_barrier(jnp.sum(final_step * products, axis=1)) * (1.0 - terminal.astype(jnp.float32))
    spacing = (support_high - support_low) / (ATOMS - 1)
    atom_values = support_low + spacing * jnp.arange(ATOMS, dtype=jnp.float32)
    shifted_atoms = jnp.clip(returns[:, None] + bootstrap[:, None] * atom_values[None, :], support_low, support_high)
    position = (shifted_atoms - support_low) / spacing
    weights = jnp.maximum(0.0, 1.0 - jnp.abs(position[:, :, None] - jnp.arange(ATOMS, dtype=jnp.float32)[None, None, :]))
    return jnp.einsum('rj,rji->ri', probabilities, weights, precision=lax.Precision.HIGHEST)

def reference(frames, next_frames, actions, next_actions, lengths, terminal, rewards, discounts, owners, conv_one_weight, conv_one_offset, conv_two_weight, conv_two_offset, conv_three_weight, conv_three_offset, dense_one_weight, dense_one_offset, dense_two_weight, dense_two_offset, target_conv_one_weight, target_conv_one_offset, target_conv_two_weight, target_conv_two_offset, target_conv_three_weight, target_conv_three_offset, target_dense_one_weight, target_dense_one_offset, target_dense_two_weight, target_dense_two_offset):
    online = tuple((tensor.astype(jnp.float32) for tensor in (conv_one_weight, conv_one_offset, conv_two_weight, conv_two_offset, conv_three_weight, conv_three_offset, dense_one_weight, dense_one_offset, dense_two_weight, dense_two_offset)))
    target = tuple((tensor.astype(jnp.float32) for tensor in (target_conv_one_weight, target_conv_one_offset, target_conv_two_weight, target_conv_two_offset, target_conv_three_weight, target_conv_three_offset, target_dense_one_weight, target_dense_one_offset, target_dense_two_weight, target_dense_two_offset)))

    def blocked(tensor):
        return tensor.reshape((N_BATCH, TRANS_DEV) + tensor.shape[1:])
    blocks = tuple((blocked(tensor) for tensor in (frames, next_frames, actions, next_actions, lengths, terminal, rewards, discounts, owners[:, 0])))

    def one_block(totals, block):
        now_frames, later_frames, action_ids, next_ids, length_ids, terminal_ids, reward_rows, discount_rows, owner_ids = block

        def objective(params, images):
            feature_next = conv_tower(later_frames.astype(jnp.float32), *target[:6])
            target_logits = dense_head(feature_next, *target[6:])
            probabilities = jax.nn.softmax(pick_action(target_logits, next_ids), axis=-1)
            mass = projection(probabilities, reward_rows, discount_rows, length_ids, terminal_ids)
            logits = dense_head(conv_tower(images, *params[:6]), *params[6:])
            row_loss = -lax.optimization_barrier(jnp.sum(mass * jax.nn.log_softmax(pick_action(logits, action_ids), axis=-1), axis=1))
            return (jnp.sum(row_loss), row_loss)
        summed, pullback, row_loss = jax.vjp(objective, online, now_frames.astype(jnp.float32), has_aux=True)
        param_grads, image_grads = pullback(jnp.ones_like(summed))
        totals = jax.tree.map(jnp.add, totals, param_grads)
        owner_hot = (owner_ids[:, None] == jnp.arange(N_BATCH, dtype=jnp.int32)[None, :]).astype(jnp.int32)
        ranks = (lax.optimization_barrier(jnp.sum(jnp.cumsum(owner_hot, axis=0) * owner_hot, axis=1)) - 1).astype(jnp.int32)
        return (totals, (image_grads.astype(jnp.bfloat16), row_loss, ranks))
    totals, outputs = lax.scan(one_block, jax.tree.map(jnp.zeros_like, online), blocks)
    image_grads, row_losses, ranks = outputs
    sources = jnp.broadcast_to(jnp.arange(N_BATCH, dtype=jnp.int32)[:, None], (N_BATCH, TRANS_DEV))
    table = jnp.zeros((N_BATCH, N_BATCH, CAP), jnp.float32).at[blocks[8], sources, ranks].set(row_losses)
    mean_loss = jnp.mean(row_losses)
    return (mean_loss, image_grads.reshape(frames.shape), totals[0], totals[1], totals[2], totals[3], totals[4], totals[5], totals[6], totals[7], totals[8], totals[9], table)
```

```python
import functools

import jax
import jax.numpy as jnp
import numpy as np
from jax import lax
from jax.experimental import pallas as pl
from jax.experimental.pallas import tpu as pltpu
from jax.sharding import PartitionSpec as P

ACTIONS = 18
ATOMS = 51
NSTEP = 3
LANES = 128
SLICE = 32
ROW_CHUNKS = ((0, 36), (36, 84))
MESH = pl.DeviceIdType.MESH
support_low = -10.0
support_high = 10.0
F32 = jnp.float32
BF16 = jnp.bfloat16
NT = (((1,), (1,)), ((), ()))


def nn_dot(a, b):
    return jnp.dot(a, b, preferred_element_type=F32)


def nt_dot(a, b):
    return lax.dot_general(a, b, NT, preferred_element_type=F32)


def stack(parts):
    return jnp.concatenate(parts, axis=0)


def beside(parts):
    return jnp.concatenate(parts, axis=1)


def eye(size):
    rows = lax.broadcasted_iota(jnp.int32, (size, size), 0)
    cols = lax.broadcasted_iota(jnp.int32, (size, size), 1)
    return jnp.where(rows == cols, 1.0, 0.0).astype(BF16)


def order_rows(channels, extent):
    count = channels * extent * extent
    chosen = np.zeros((count, count), np.float32)
    for c in range(channels):
        for u in range(extent):
            for v in range(extent):
                chosen[(u * extent + v) * channels + c, (c * extent + u) * extent + v] = 1.0
    return jnp.asarray(chosen, BF16)


def back_one_choice():
    chosen = np.zeros((2, 8, 4, 28, 2, 128), np.float32)
    for dp in range(2):
        for dq in range(8):
            for i in range(4):
                for x in range(28):
                    u, v = i + 4 * (1 - dp), x + 4 - 4 * dq
                    if 0 <= v < 8:
                        for ch in range(2):
                            chosen[dp, dq, i, x, ch, ch * 64 + u * 8 + v] = 1.0
    return jnp.asarray(chosen.reshape(16 * 224, 128), BF16)


def lane_bias(row, size):
    return nt_dot(eye(size), jnp.broadcast_to(row, (LANES, size)))


def activate(h):
    t = jnp.tanh(h)
    m = h * t
    return h + m, (1.0 + t) * ((1.0 + h) - m)


def in_turn(jobs):
    waiting = None
    for first, then in jobs:
        value = first()
        if waiting is not None:
            waiting[0](waiting[1])
        waiting = (then, value)
    waiting[0](waiting[1])


def whole(shape):
    return pl.BlockSpec(shape, lambda i, *_: (0,) * len(shape))


def by_lane(shape):
    return pl.BlockSpec(shape[:-1] + (LANES,), lambda i, *_: (0,) * (len(shape) - 1) + (i,))


def lane_column(row):
    size = row.shape[1]
    parts = []
    for at in range(0, size, LANES):
        step = min(LANES, size - at)
        parts.append(lane_bias(row[:, at : at + step], step))
    return stack(parts)


def softmax_terms(v):
    top = jnp.max(v, axis=0, keepdims=True)
    e = jnp.exp(v - top)
    total = jnp.sum(e, axis=0, keepdims=True)
    return e / total, v - top - jnp.log(total)


def head_kernel(
    x_any,
    y_any,
    dense_any,
    target_dense_any,
    w1_ref,
    w2_ref,
    w3_ref,
    o1_ref,
    o2_ref,
    o3_ref,
    v1_ref,
    v2_ref,
    v3_ref,
    q1_ref,
    q2_ref,
    q3_ref,
    p1_ref,
    p2_ref,
    out_ref,
    target_out_ref,
    b1_ref,
    d1_ref,
    action_ref,
    later_action_ref,
    length_ref,
    terminal_ref,
    b2_ref,
    d2_ref,
    rewards_ref,
    discounts_ref,
    a1_any,
    s1_any,
    a2_any,
    s2_any,
    s3_any,
    f_any,
    active_ref,
    lg_ref,
    hg_ref,
    loss_ref,
    sum1_ref,
    sum2_ref,
    wt1,
    wt2,
    wt3,
    wt4,
    c1,
    c2,
    c3,
    c4,
    fs,
    fb,
    xbuf,
    a1,
    s1,
    a2,
    s2,
    s3,
    wd,
    wdt,
    pre,
    hidden,
    late,
    back,
    logits,
    logits_later,
    lgs,
    probs,
    position,
    x_sems,
    out_sems,
    wd_sem,
    sent,
    came,
):
    section, batch = lax.axis_index("section"), lax.axis_index("batch")
    step, steps = pl.program_id(0), pl.num_programs(0)
    lanes = hidden.shape[1]
    tiles = lanes // LANES
    targets = tiles - 1
    online = step >= targets
    slot = lax.rem(step, 2)
    height, width, stacked, _ = x_any.shape

    def lanes_of(index):
        return pl.ds(pl.multiple_of(index * LANES, LANES), LANES)

    def x_copy(source, tile, at, k):
        place = lax.rem(at, 2)
        first, last = ROW_CHUNKS[k]
        pixels = source.reshape(height, width * stacked, lanes)
        return pltpu.make_async_copy(
            pixels.at[first:last, :, lanes_of(tile)], xbuf.at[place, first:last], x_sems.at[place, k]
        )

    def start_x(at):
        @pl.when(at < targets)
        def _():
            for k in range(len(ROW_CHUNKS)):
                x_copy(y_any, jnp.minimum(at, targets - 1) + section, at, k).start()

        @pl.when((at >= targets) & (at < steps))
        def _():
            for k in range(len(ROW_CHUNKS)):
                x_copy(x_any, jnp.clip(at - targets, 0, tiles - 1), at, k).start()

    tile = jnp.maximum(step - targets, 0)
    outs = ((a1, a1_any), (s1, s1_any), (a2, a2_any), (s2, s2_any), (s3, s3_any), (fb, f_any))

    def out_copy(k, at):
        source, into = outs[k]
        place = into.at[:, lanes_of(at)] if k == 5 else into.at[at]
        return pltpu.make_async_copy(source, place, out_sems.at[k])

    def wait_outs(which):
        @pl.when(step > targets)
        def _():
            for k in which:
                out_copy(k, jnp.maximum(tile - 1, 0)).wait()

    def start_outs(which):
        @pl.when(online)
        def _():
            for k in which:
                out_copy(k, tile).start()

    def swap():
        return pltpu.make_async_remote_copy(
            src_ref=late.at[:, lanes_of((tiles - 1) * section)],
            dst_ref=late.at[:, lanes_of((tiles - 1) * section)],
            send_sem=sent,
            recv_sem=came,
            device_id=(1 - section, batch),
            device_id_type=MESH,
        )

    def dense_copy(source):
        return pltpu.make_async_copy(source, wd, wd_sem)

    @pl.when(step == 0)
    def _():
        barrier = pltpu.get_barrier_semaphore()
        pl.semaphore_signal(barrier, inc=1, device_id=(1 - section, batch), device_id_type=MESH)
        start_x(step)
        dense_copy(target_dense_any).start()

    start_x(step + 1)

    def prepare(one_ref, two_ref, three_ref, off_one, off_two, off_three):
        wt1[...] = jnp.zeros_like(wt1)
        wt2[...] = jnp.zeros_like(wt2)
        wt3[...] = jnp.zeros_like(wt3)
        base = nt_dot(eye(32), nn_dot(p1_ref[...], one_ref[...]).astype(BF16))
        base = (0.5 * base).astype(BF16)
        for t in range(5):
            for u in range(8):
                wt1[32 * t : 32 * t + 32, 96 * u + 16 * t : 96 * u + 16 * t + 32] = base[:, 32 * u : 32 * u + 32]
        base = nt_dot(eye(64), nn_dot(p2_ref[...], two_ref[...]).astype(BF16))
        base = (0.5 * base).astype(BF16)
        for t in range(3):
            for u in range(4):
                wt2[64 * t : 64 * t + 64, 256 * u + 64 * t : 256 * u + 64 * t + 128] = base[:, 128 * u : 128 * u + 128]
        for u in range(3):
            for v in range(3):
                piece = (0.5 * three_ref[3 * u + v].astype(F32)).astype(BF16)
                wt4[:, 192 * u + 64 * v : 192 * u + 64 * v + 64] = piece
                for t in range(2):
                    at = 256 * u + 64 * t + 64 * v
                    wt3[64 * t : 64 * t + 64, at : at + 64] = piece
        c1[...] = stack([0.5 * lane_bias(off_one[...], 32)] * 5)
        c2[...] = stack([0.5 * lane_bias(off_two[...], 64)] * 3)
        column = 0.5 * lane_bias(off_three[...], 64)
        c3[...] = stack([column] * 2)
        c4[...] = column

    @pl.when(step == 0)
    def _():
        prepare(v1_ref, v2_ref, v3_ref, q1_ref, q2_ref, q3_ref)

    @pl.when(step == targets)
    def _():
        prepare(w1_ref, w2_ref, w3_ref, o1_ref, o2_ref, o3_ref)

    def put(bias, act, slope, places):
        def then(value):
            for k, (row, at, size) in enumerate(places):
                a, s = activate(value[:, LANES * k : LANES * k + LANES] + bias[...])
                act[row, at : at + size, :] = a.astype(BF16)
                slope[row, at : at + size, :] = s.astype(BF16)

        return then

    def strips_one(i, s):
        def dot():
            cols = [
                stack([xbuf[slot, 8 * i + 4 * k + u, 80 * s : 80 * s + 96, :] for u in range(8)])
                for k in range(2)
            ]
            return nn_dot(wt1[...], beside(cols))

        return dot, put(c1, a1, s1, [(2 * i + k, 160 * s, 160) for k in range(2)])

    wait_outs((0, 1))
    for k, pairs in enumerate((range(0, 4), range(4, 10))):
        x_copy(x_any, tile, step, k).wait()
        in_turn([strips_one(i, s) for i in pairs for s in range(4)])
    start_outs((0, 1))
    wait_outs((2, 3, 4, 5))

    def strips_two(places):
        def dot():
            cols = [
                stack([a1[2 * p + u, 192 * s : 192 * s + 256, :] for u in range(4)])
                for p, s in places
            ]
            return nn_dot(wt2[...], beside(cols))

        return dot, put(c2, a2, s2, [(p, 192 * s, 192) for p, s in places])

    def strips_three(places, weight, bias, count):
        def dot():
            cols = [
                stack([a2[p + u, 64 * q : 64 * q + 64 * count + 128, :] for u in range(3)])
                for p, q in places
            ]
            return nn_dot(weight[...], beside(cols))

        def then(value):
            for k, (p, q) in enumerate(places):
                a, s = activate(value[:, LANES * k : LANES * k + LANES] + bias[...])
                for t in range(count):
                    fs[pl.ds(7 * p + q + t, 64, stride=49), :] = a[64 * t : 64 * t + 64, :]
                s3[p, 64 * q : 64 * q + 64 * count, :] = s.astype(BF16)

        return dot, then

    two = [(2 * i + k, s) for i in range(4) for s in range(3) for k in range(2)]
    two += [(8, s) for s in range(3)]
    three = [(p, q) for p in range(7) for q in (0, 2, 4)]
    ends = [(p, 6) for p in range(7)]
    in_turn(
        [strips_two(two[k : k + 2]) for k in range(0, len(two), 2)]
        + [strips_three(three[k : k + 2], wt3, c3, 2) for k in range(0, len(three), 2)]
        + [strips_three(ends[k : k + 2], wt4, c4, 1) for k in range(0, len(ends), 2)]
    )
    fb[...] = fs[...].astype(BF16)
    start_outs((2, 3, 4, 5))

    def turn(source):
        dense_copy(source).wait()
        unit = eye(512)
        for at in range(0, wd.shape[0], 256):
            size = min(256, wd.shape[0] - at)
            wdt[:, at : at + size] = nt_dot(unit, wd[at : at + size, :]).astype(BF16)

    @pl.when(step == 0)
    def _():
        turn(target_dense_any)
        dense_copy(dense_any).start()

    @pl.when(step == targets)
    def _():
        turn(dense_any)

    def column(rows_ref):
        return stack([lane_bias(rows_ref[k : k + 1, :], LANES) for k in range(rows_ref.shape[0])])

    pre[...] = nn_dot(wdt[...], fb[...])

    @pl.when(step < targets)
    def _():
        later, _ = activate(0.5 * (pre[...] + column(d1_ref)))
        late[:, lanes_of(jnp.minimum(step, targets - 1) + section)] = later.astype(BF16)

    @pl.when(step == targets - 1)
    def _():
        pl.semaphore_wait(pltpu.get_barrier_semaphore(), 1)
        swap().start()

    @pl.when(online)
    def _():
        hidden[:, lanes_of(tile)] = pre[...] + column(b1_ref)

    @pl.when(step == steps - 1)
    def _():
        count = out_ref.shape[0]
        back[...] = jnp.zeros_like(back)
        lgs[...] = jnp.zeros_like(lgs)
        for at in range(0, count, 256):
            size = min(256, count - at)
            back[:, at : at + size] = nt_dot(eye(512), out_ref[at : at + size, :]).astype(BF16)

        def wide(ref):
            return beside([lane_column(ref[...].reshape(1, count))] * tiles)

        active, slope = activate(0.5 * hidden[...])
        active = active.astype(BF16)
        active_ref[...] = active
        logits[...] = nn_dot(out_ref[...], active) + wide(b2_ref)
        swap().wait()
        logits_later[...] = nn_dot(target_out_ref[...], late[...]) + wide(d2_ref)

        def row(ref):
            return beside([ref[k : k + 1, :] for k in range(tiles)])

        action, later_action = row(action_ref), row(later_action_ref)
        length, terminal = row(length_ref), row(terminal_ref)

        def pick(ref, ids):
            total = jnp.zeros((ATOMS, lanes), F32)
            for a in range(ACTIONS):
                total = total + jnp.where(ids == a, ref[ATOMS * a : ATOMS * a + ATOMS, :], 0.0)
            return total

        soft, log_soft = softmax_terms(pick(logits, action))
        returns = jnp.zeros((1, lanes), F32)
        bootstrap = jnp.zeros((1, lanes), F32)
        product = jnp.ones((1, lanes), F32)
        for k in range(NSTEP):
            returns = returns + jnp.where(length > k, product * rewards_ref[k : k + 1, :], 0.0)
            product = product * discounts_ref[k : k + 1, :]
            bootstrap = bootstrap + jnp.where(length == k + 1, product, 0.0)
        bootstrap = bootstrap * (1.0 - terminal.astype(F32))
        spacing = (support_high - support_low) / (ATOMS - 1)
        ids = lax.broadcasted_iota(jnp.int32, (ATOMS, lanes), 0).astype(F32)
        shifted = jnp.clip(returns + bootstrap * (support_low + spacing * ids), support_low, support_high)
        position[...] = (shifted - support_low) / spacing
        probs[...], _ = softmax_terms(pick(logits_later, later_action))
        mass = jnp.zeros((ATOMS, lanes), F32)
        for j in range(ATOMS):
            weight = jnp.maximum(0.0, 1.0 - jnp.abs(position[j : j + 1, :] - ids))
            mass = mass + probs[j : j + 1, :] * weight
        loss_ref[...] = -jnp.sum(mass * log_soft, axis=0, keepdims=True)
        chosen_grad = jnp.sum(mass, axis=0, keepdims=True) * soft - mass
        for a in range(ACTIONS):
            lgs[ATOMS * a : ATOMS * a + ATOMS, :] = jnp.where(action == a, chosen_grad, 0.0)
        lg = lgs[...].astype(BF16)
        lg_ref[...] = lg[0:count]
        hg = (nn_dot(back[...], lg) * (0.5 * slope)).astype(BF16)
        hg_ref[...] = hg
        ones = jnp.ones((8, lanes), BF16)
        sum1_ref[...] = nt_dot(ones, hg)
        sum2_ref[...] = nt_dot(ones, lg[0:count])
        for k in range(len(outs)):
            out_copy(k, tile).wait()


def head(x, y, dense_one, target_dense_one, small):
    lanes = x.shape[3]
    count = small[14].shape[0]
    tiles = lanes // LANES
    outs = [(20, 640), (20, 640), (9, 576), (9, 576), (7, 448)]
    outs = [(tiles,) + shape + (LANES,) for shape in outs] + [(3136, lanes)]
    rest = [((512, lanes), BF16), ((count, lanes), BF16), ((512, lanes), BF16), ((1, lanes), F32)]
    rest += [((8, 512), F32), ((8, count), F32)]
    anywhere = pl.BlockSpec(memory_space=pl.ANY)
    buffers = [
        ((160, 768), BF16),
        ((192, 1024), BF16),
        ((128, 768), BF16),
        ((64, 576), BF16),
        ((160, LANES), F32),
        ((192, LANES), F32),
        ((128, LANES), F32),
        ((64, LANES), F32),
        ((3136, LANES), F32),
        ((3136, LANES), BF16),
        ((2, 84, 336, LANES), BF16),
        ((20, 640, LANES), BF16),
        ((20, 640, LANES), BF16),
        ((9, 576, LANES), BF16),
        ((9, 576, LANES), BF16),
        ((7, 448, LANES), BF16),
        ((3136, 512), BF16),
        ((512, 3136), BF16),
        ((512, LANES), F32),
        ((512, lanes), F32),
        ((512, lanes), BF16),
        ((512, 1024), BF16),
        ((count, lanes), F32),
        ((count, lanes), F32),
        ((1024, lanes), F32),
        ((ATOMS, lanes), F32),
        ((ATOMS, lanes), F32),
    ]
    return pl.pallas_call(
        head_kernel,
        grid=(2 * (lanes // LANES) - 1,),
        in_specs=[anywhere] * 4 + [whole(a.shape) for a in small],
        out_specs=[anywhere] * len(outs) + [whole(s) for s, _ in rest],
        out_shape=[jax.ShapeDtypeStruct(s, BF16) for s in outs]
        + [jax.ShapeDtypeStruct(s, t) for s, t in rest],
        scratch_shapes=[pltpu.VMEM(s, t) for s, t in buffers]
        + [
            pltpu.SemaphoreType.DMA((2, len(ROW_CHUNKS))),
            pltpu.SemaphoreType.DMA((len(outs),)),
            pltpu.SemaphoreType.DMA,
            pltpu.SemaphoreType.DMA,
            pltpu.SemaphoreType.DMA,
        ],
        compiler_params=pltpu.CompilerParams(
            collective_id=0, has_side_effects=True, vmem_limit_bytes=60 * 1024 * 1024
        ),
        cost_estimate=pl.CostEstimate(
            flops=5 * 2 * 9785600 * LANES, bytes_accessed=2**26, transcendentals=0
        ),
    )(x, y, dense_one, target_dense_one, *small)


def backward_kernel(
    capacity,
    a2_ref,
    s2_ref,
    s3_ref,
    a1_any,
    s1_any,
    x_any,
    f_any,
    dense_weight_any,
    hg_ref,
    lg_ref,
    active_ref,
    w1_ref,
    w2_ref,
    w3_ref,
    p2_ref,
    q1_ref,
    owner_ref,
    loss_ref,
    sum1_ref,
    sum2_ref,
    frames_any,
    dense_any,
    sum_ref,
    own_ref,
    t1_ref,
    t2_ref,
    t3_ref,
    tb_ref,
    fcs,
    stage,
    turned,
    first,
    packed,
    wb2,
    wb3,
    g2,
    g3,
    g1,
    frames,
    wb1,
    frame_sems,
    dense_sem,
    a1_ref,
    s1_ref,
    xbuf,
    fbuf,
    dense_weight_ref,
    weight_sem,
    slab,
    landed,
    shared,
    a_sems,
    x_sem,
    f_sem,
    sent,
    came,
    pack,
    arrived,
    total,
    crossed,
    share,
    gathered,
    left,
    reached,
):
    section, batch = lax.axis_index("section"), lax.axis_index("batch")
    owners = lax.axis_size("batch")
    bits = owners.bit_length() - 1
    tile = pl.program_id(0)
    last_tile = pl.num_programs(0) - 1

    dense_rows = slab.shape[0]
    bit = [lax.rem(batch // (1 << k), 2) for k in range(bits)]
    colours = 2 if bits < 7 else 1
    region = dense_rows // (2 * colours)
    orders = [list(range(1, bits)) for _ in range(colours)]
    orders[-1] = orders[-1][(bits - 1) // 2 :] + orders[-1][: (bits - 1) // 2]
    base = (dense_rows // 2) * bit[0]
    bases = []
    for c in range(colours):
        starts = [base + c * region]
        for m, k in enumerate(orders[c]):
            starts.append(starts[-1] + (region >> (m + 1)) * bit[k])
        bases.append(starts)

    def rows_at(start, size):
        return pl.ds(pl.multiple_of(start, 16), size)

    def moves(phase):
        if phase in (0, 2 * bits - 1):
            half = dense_rows // 2
            if phase:
                return [(0, base, half, None, None)]
            return [(0, half * (1 - bit[0]), half, 0, base)]
        found = []
        for c in range(colours):
            m = phase - 1 if phase < bits else 2 * bits - 2 - phase
            size = region >> (m + 1)
            k, start = orders[c][m], bases[c][m]
            if phase < bits:
                place = dense_rows // 2 + (c + 1) * region - 2 * size
                found.append((k, start + size * (1 - bit[k]), size, place, bases[c][m + 1]))
            else:
                found.append((k, bases[c][m + 1], size, None, None))
        return found

    def transfers(phase):
        copies = []
        for c, (k, start, size, place, _) in enumerate(moves(phase)):
            if phase < bits:
                source, into = slab.at[rows_at(start, size), :], landed.at[pl.ds(place, size), :]
            else:
                source = into = shared.at[rows_at(start, size), :]
            copies.append(
                pltpu.make_async_remote_copy(
                    src_ref=source,
                    dst_ref=into,
                    send_sem=sent.at[2 * phase + c],
                    recv_sem=came.at[2 * phase + c],
                    device_id=(section, batch + (1 << k) * (1 - 2 * bit[k])),
                    device_id_type=MESH,
                )
            )
        return copies

    def complete(phase):
        for copy, (_, _, size, place, to) in zip(transfers(phase), moves(phase)):
            copy.wait()
            if phase < bits:
                step = min(size, 64)

                def add(n, carry, step=step, place=place, to=to):
                    at = rows_at(to + step * n, step)
                    more = landed[pl.ds(pl.multiple_of(place + step * n, 16), step), :]
                    slab[at, :] = (slab[at, :].astype(F32) + more.astype(F32)).astype(BF16)
                    return carry

                lax.fori_loop(0, size // step, add, 0)
        if phase == bits - 1:
            for c in range(colours):
                own = rows_at(bases[c][-1], region >> (bits - 1))
                shared[own, :] = slab[own, :]

    starts = [0, 1, 2, 3, 5, 6, 8]
    if bits != 4:
        starts = [9 * phase // (2 * bits - 1) for phase in range(2 * bits - 1)]
    last_phase = 2 * bits - 1

    def slot(index):
        for phase, at in enumerate(starts):
            if phase > 0 and at % 3 == index:

                @pl.when(tile == at // 3)
                def _(phase=phase):
                    complete(phase - 1)
                    for copy in transfers(phase):
                        copy.start()

    high_count = owners // 4
    block = high_count * SLICE
    low, high = lax.rem(batch, 4), batch // 4
    group = section * 4 + low
    place = low * high_count + high

    def near(k):
        index = lax.rem(group + k, 8)
        return index, (index // 4, high * 4 + lax.rem(index, 4))

    def far(k):
        index = lax.rem(high + k, high_count)
        return index, (section, index * 4 + low)

    def send(source, into, device, number):
        return pltpu.make_async_remote_copy(
            src_ref=source,
            dst_ref=into,
            send_sem=left.at[number],
            recv_sem=reached.at[number],
            device_id=device,
            device_id_type=MESH,
        )

    def rows_of(index, size):
        return pl.ds(pl.multiple_of(index * size, size), size)

    def to_near(k):
        index, device = near(k)
        return send(pack.at[rows_of(index, block), :], arrived.at[group], device, k)

    short = high_count <= 4

    def to_far(k):
        index, device = far(k)
        source = crossed.at[high] if short else total.at[rows_of(index, SLICE), :]
        return send(source, crossed.at[high], device, 8 + k)

    def back_far(k):
        return send(share, gathered.at[place], far(k)[1], 8 + high_count + k)

    def back_near(k):
        ours = gathered.at[pl.ds(low * high_count, high_count)]
        device = (section, high * 4 + lax.rem(low + k, 4))
        return send(ours, ours, device, 8 + 2 * high_count + k)

    def a_copy(at, k):
        source, into = ((a1_any, a1_ref), (s1_any, s1_ref))[k]
        return pltpu.make_async_copy(source.at[at], into, a_sems.at[k])

    def dense_copy():
        return pltpu.make_async_copy(shared, dense_any, dense_sem)

    height, width, stacked, lane_count = x_any.shape
    pixels = x_any.reshape(height, width * stacked, lane_count)

    def x_copy():
        return pltpu.make_async_copy(
            pixels.at[pl.ds(40 * section, 44), :, pl.ds(pl.multiple_of(tile * LANES, LANES), LANES)],
            xbuf,
            x_sem,
        )

    def f_copy():
        half = fbuf.shape[0]
        return pltpu.make_async_copy(f_any.at[rows_at(half * section, half), :], fbuf, f_sem)

    def weight_copy():
        return pltpu.make_async_copy(dense_weight_any, dense_weight_ref, weight_sem)

    @pl.when(tile == 0)
    def _():
        f_copy().start()
        weight_copy().start()
        for k in range(2):
            a_copy(tile, k).start()
        barrier = pltpu.get_barrier_semaphore()
        for k in range(1, 8):
            pl.semaphore_signal(barrier, inc=1, device_id=near(k)[1], device_id_type=MESH)
        for k in range(1, high_count):
            pl.semaphore_signal(barrier, inc=1, device_id=far(k)[1], device_id_type=MESH)
        f_copy().wait()

        def dense_one(start, stop):
            for at in range(start, stop, 256):
                rows = slice(at, min(at + 256, stop))
                slab[rows, :] = nt_dot(fbuf[rows, :], hg_ref[...]).astype(BF16)

        def upper_half():
            slab[1568:dense_rows, :] = jnp.zeros((dense_rows - 1568, 512), BF16)
            mine = active_ref[pl.ds(pl.multiple_of(256 * section, 256), 256), :]
            slab[1568:2032, 0:256] = nt_dot(lg_ref[0:464, :], mine).astype(BF16)
            slab[1568:2022, 256:512] = nt_dot(lg_ref[464:918, :], mine).astype(BF16)
            dense_one(1024, 1568)

        @pl.when(bit[0] == 0)
        def _():
            upper_half()

        @pl.when(bit[0] == 1)
        def _():
            dense_one(0, 1024)

        pl.semaphore_wait(barrier, 6 + high_count)
        for copy in transfers(0):
            copy.start()

        @pl.when(bit[0] == 0)
        def _():
            dense_one(0, 1024)

        @pl.when(bit[0] == 1)
        def _():
            upper_half()

        for ref in (t1_ref, t2_ref, t3_ref, tb_ref, wb1, wb2, wb3):
            ref[...] = jnp.zeros_like(ref)
        for ref, edge, width in ((g1, 1, 32), (g2, 1, 64), (g3, 2, 64)):
            side = jnp.zeros((edge * width, LANES), BF16)
            for r in range(ref.shape[0]):
                if edge <= r < ref.shape[0] - edge:
                    ref[r, 0 : edge * width, :] = side
                    ref[r, ref.shape[1] - edge * width :, :] = side
                else:
                    ref[r] = jnp.zeros((ref.shape[1], LANES), BF16)
        rows = (0.5 * nn_dot(p2_ref[...], w2_ref[...])).astype(BF16)
        for dp in range(2):
            for dq in range(2):
                for b in range(2):
                    for x in range(2):
                        u, v = b + 2 * (1 - dp), x + 2 * (1 - dq)
                        to, at, of = 32 * (2 * b + x), 64 * (2 * dp + dq), 32 * (4 * u + v)
                        wb2[to : to + 32, at : at + 64] = rows[of : of + 32, :]
        for u in range(3):
            for v in range(3):
                piece = (0.5 * nt_dot(eye(64), w3_ref[3 * u + v])).astype(BF16)
                for t in range(3):
                    at = 320 * (2 - u) + 64 * (t + 2 - v)
                    wb3[64 * t : 64 * t + 64, at : at + 64] = piece
        half = w1_ref[pl.ds(pl.multiple_of(section * 128, 128), 128), :]
        pieces = nn_dot(q1_ref[...], half).astype(BF16)
        for k in range(16):
            wb1[:, 32 * k : 32 * k + 32] = pieces[224 * k : 224 * k + 224, :]
        weight_copy().wait()

    slot(0)
    x_copy().start()

    def sums(value, size):
        total = value[0:size]
        for at in range(size, value.shape[0], size):
            total = total + value[at : at + size]
        return total

    hg = hg_ref[:, pl.ds(pl.multiple_of(tile * LANES, LANES), LANES)]

    def feature_grad(n, carry):
        at = pl.ds(pl.multiple_of(448 * n, 448), 448)
        fcs[at, :] = 0.5 * nn_dot(dense_weight_ref[at, :], hg).astype(BF16).astype(F32)
        return carry

    lax.fori_loop(0, 7, feature_grad, 0, unroll=True)

    def cot_three(p, carry):
        cot = stack([fcs[pl.ds(7 * p + q, 64, stride=49), :] for q in range(7)])
        g = cot * s3_ref[p].astype(F32)
        g3[p + 2, 128:576, :] = g.astype(BF16)
        tb_ref[96:160, :] += sums(g, 64)
        return carry

    lax.fori_loop(0, 7, cot_three, 0, unroll=True)

    blocks, cots = [], []
    nothing = jnp.zeros((64, LANES), BF16)
    for n in range(4):
        p = 4 * section + n
        rows = [jnp.minimum(p + u, 8) for u in range(3)]
        blocks.append(stack([a2_ref[r, 0:384, :] for r in rows]))
        blocks.append(stack([part for r in rows for part in (a2_ref[r, 256:576, :], nothing)]))
        cots += [g3[p + 2, 128:384, :], g3[p + 2, 384:640, :]]
    t3_ref[...] += nt_dot(beside(blocks), beside(cots))


    def patch_three(y, s):
        return stack([g3[y + d, 192 * s : 192 * s + 320, :] for d in range(3)])

    def strips_two(places):
        def dot():
            return nn_dot(wb3[...], beside([patch_three(y, s) for y, s in places]))

        def then(value):
            for k, (y, s) in enumerate(places):
                slope = s2_ref[y, 192 * s : 192 * s + 192, :].astype(F32)
                g = value[:, LANES * k : LANES * k + LANES] * slope
                g2[y + 1, 64 + 192 * s : 256 + 192 * s, :] = g.astype(BF16)
                tb_ref[32:96, :] += sums(g, 64)

        return dot, then

    pairs = [(2 * i, s) for i in range(4) for s in range(3)]
    in_turn(
        [strips_two([(y, s), (y + 1, s)]) for y, s in pairs]
        + [strips_two([(8, 0), (8, 1)]), strips_two([(8, 2)])]
    )

    slot(1)
    a_copy(tile, 0).wait()
    a_copy(tile, 1).wait()

    blocks, cots = [], []
    for n in range(5):
        p = 5 * section + n
        rows = [jnp.minimum(2 * p + u, 19) for u in range(4)]
        for q in range(3):
            blocks.append(stack([a1_ref[r, 192 * q : 192 * q + 256, :] for r in rows]))
            cots.append(g2[p + 1, 64 + 192 * q : 256 + 192 * q, :])
    t2_ref[...] += nt_dot(beside(blocks), beside(cots))


    def back_two(i):
        def strip(s):
            def dot():
                cols = [
                    stack([g2[2 * i + k + d, 64 * s : 64 * s + 128, :] for d in range(2)])
                    for k in range(2)
                ]
                return nn_dot(wb2[...], beside(cols))

            def then(v):
                total = jnp.zeros((32, LANES), F32)
                for k in range(2):
                    for b in range(2):
                        row = 4 * i + 2 * k + b
                        slope = s1_ref[row, 64 * s : 64 * s + 64, :].astype(F32)
                        g = v[64 * b : 64 * b + 64, LANES * k : LANES * k + LANES] * slope
                        g1[row + 1, 32 + 64 * s : 96 + 64 * s, :] = g.astype(BF16)
                        total = total + sums(g, 32)
                tb_ref[0:32, :] += total

            return dot, then

        return [strip(s) for s in range(10)]

    in_turn([job for i in range(5) for job in back_two(i)])
    slot(2)

    @pl.when(tile < last_tile)
    def _():
        for k in range(2):
            a_copy(tile + 1, k).start()

    x_copy().wait()

    for first_row in (0, 5):
        blocks, cots = [], []
        for n in range(first_row, first_row + 5):
            for q in range(4):
                blocks.append(stack([xbuf[4 * n + u, 80 * q : 80 * q + 96, :] for u in range(8)]))
                cots.append(g1[10 * section + n + 1, 32 + 160 * q : 192 + 160 * q, :])
        t1_ref[...] += nt_dot(beside(blocks), beside(cots))


    height, width, channels, lane_count = frames_any.shape
    out_pixels = frames_any.reshape(height, width * channels, lane_count)

    def frames_copy(at, part):
        lanes = pl.ds(pl.multiple_of(at * LANES, LANES), LANES)
        rows = pl.ds(28 * part, 28)
        return pltpu.make_async_copy(frames.at[rows], out_pixels.at[rows, :, lanes], frame_sems.at[part])

    def frames_part(part):
        def strips(places):
            def dot():
                cols = [
                    stack([g1[7 * part + a + d, 224 * s : 224 * s + 256, :] for d in range(2)])
                    for a, s in places
                ]
                return nn_dot(wb1[...], beside(cols))

            def then(v):
                for k, (a, s) in enumerate(places):
                    for i in range(4):
                        frames[28 * part + 4 * a + i, 56 * s : 56 * s + 56, :] = v[
                            56 * i : 56 * i + 56, LANES * k : LANES * k + LANES
                        ].astype(BF16)

            return dot, then

        places = [(a, s) for a in range(7) for s in range(3)]
        in_turn([strips(places[k : k + 2]) for k in range(0, len(places), 2)])

    @pl.when(tile < last_tile)
    def _():
        def one_part(part, carry):
            @pl.when(tile > 0)
            def _():
                frames_copy(tile - 1, part).wait()

            frames_part(part)
            frames_copy(tile, part).start()
            return carry

        lax.fori_loop(0, 3, one_part, 0)

    def last_part(part):
        frames_copy(tile - 1, part).wait()
        frames_part(part)
        frames_copy(tile, part).start()

    @pl.when(tile == last_tile)
    def _():
        rows = owner_ref.shape[1]
        half_rows = SLICE * owners
        owner_hot = owner_ref[...] == lax.broadcasted_iota(jnp.int32, (owners, rows), 0)
        owner_hot = jnp.where(owner_hot, 1.0, 0.0)
        before = lax.broadcasted_iota(jnp.int32, (rows, rows), 0)
        before = before < lax.broadcasted_iota(jnp.int32, (rows, rows), 1)
        before = nn_dot(owner_hot.astype(BF16), jnp.where(before, 1.0, 0.0).astype(BF16))
        slots = jnp.sum(before * owner_hot, axis=0, keepdims=True)
        slot_ids = lax.broadcasted_iota(jnp.int32, (32, rows), 0)
        slot_ids = slot_ids - capacity * (batch // SLICE)
        slot_hot = jnp.where(slots.astype(jnp.int32) == slot_ids, 1.0, 0.0).astype(BF16)
        outgoing = nt_dot((owner_hot * loss_ref[...]).astype(BF16), slot_hot)
        count = sum2_ref.shape[1] // 2
        for k in range(9):
            u, v = k // 3, k % 3
            pieces = [
                t3_ref[384 * u + 64 * (q + v) : 384 * u + 64 * (q + v) + 64, 64 * q : 64 * q + 64]
                for q in range(4)
            ]
            turned[64 * k : 64 * k + 64, 0:64] = functools.reduce(jnp.add, pieces)
        for k in range(16):
            u, v = k // 4, k % 4
            pieces = [
                t2_ref[256 * u + 32 * (2 * q + v) : 256 * u + 32 * (2 * q + v) + 32, 64 * q : 64 * q + 64]
                for q in range(3)
            ]
            turned[32 * k : 32 * k + 32, 64:128] = functools.reduce(jnp.add, pieces)
        for u in range(8):
            pieces = [
                t1_ref[96 * u + 16 * q : 96 * u + 16 * q + 32, 32 * q : 32 * q + 32] for q in range(5)
            ]
            first[32 * u : 32 * u + 32, 0:32] = functools.reduce(jnp.add, pieces)
        both = jnp.transpose(turned[...])
        ones = jnp.ones((8, LANES), F32)
        bias = lax.dot_general(
            ones, tb_ref[...], NT, precision=lax.Precision.HIGHEST, preferred_element_type=F32
        )
        for h in range(2):
            packed[...] = jnp.zeros_like(packed)
            for k in range(9):
                packed[32 * k : 32 * k + 32, 0:64] = both[32 * h : 32 * h + 32, 64 * k : 64 * k + 64]
            for k in range(16):
                piece = both[64 + 32 * h : 96 + 32 * h, 32 * k : 32 * k + 32]
                stage[pl.ds(k, 32, stride=16), :] = jnp.pad(piece, ((0, 0), (0, 96)))
            packed[0:512, 64:96] = stage[:, 0:32]
            for c in range(4):
                rows_c = first[pl.ds(c, 64, stride=4), :]
                packed[288 : 352, 16 * c : 16 * c + 16] = rows_c[:, 16 * h : 16 * h + 16]
            packed[352 : 353, 0:16] = bias[0:1, 16 * h : 16 * h + 16]
            packed[353 : 354, 0:32] = bias[0:1, 32 + 32 * h : 64 + 32 * h]
            packed[354 : 355, 0:32] = bias[0:1, 96 + 32 * h : 128 + 32 * h]
            packed[355 : 356, 0:1] = jnp.sum(loss_ref[...], axis=1, keepdims=True)
            for k in range(4):
                packed[384 + k : 385 + k, 0:64] = sum1_ref[0:1, 256 * h + 64 * k : 256 * h + 64 * k + 64]
            for k in range(8):
                at = 64 * k
                size = min(64, count - at)
                packed[388 + k : 389 + k, 0:size] = sum2_ref[0:1, count * h + at : count * h + at + size]
            for o in range(owners):
                at = SLICE * ((o % 4) * (owners // 4) + o // 4)
                packed[pl.ds(at + lax.rem(batch, SLICE), 1), 96:128] = outgoing[o : o + 1, :]
            pack[half_rows * h : half_rows * h + half_rows, :] = packed[...].astype(BF16)
        for k in range(1, 8):
            to_near(k).start()
        last_part(0)
        total[...] = pack[rows_of(group, block), :].astype(F32)
        for k in range(1, 8):
            to_near(k).wait()
            total[...] += arrived[lax.rem(group + 8 - k, 8)].astype(F32)
        if short:
            crossed[high] = total[...].astype(BF16)
            for k in range(1, high_count):
                to_far(k).start()
            last_part(1)
            complete(last_phase - 1)
            for copy in transfers(last_phase):
                copy.start()
            for k in range(1, high_count):
                to_far(k).wait()
            ours = crossed[0].astype(F32)
            for k in range(1, high_count):
                ours = ours + crossed[k].astype(F32)
            total[...] = ours
            for k in range(high_count):
                gathered[low * high_count + k] = ours[SLICE * k : SLICE * k + SLICE, :]
            own_ref[...] = total[rows_of(high, SLICE), :]
        else:
            for k in range(1, high_count):
                to_far(k).start()
            last_part(1)
            complete(last_phase - 1)
            for copy in transfers(last_phase):
                copy.start()
            share[...] = total[rows_of(high, SLICE), :]
            for k in range(1, high_count):
                to_far(k).wait()
                share[...] += crossed[lax.rem(high + high_count - k, high_count)]
            for k in range(1, high_count):
                back_far(k).start()
            gathered[place] = share[...]
            own_ref[...] = share[...]
            for k in range(1, high_count):
                back_far(k).wait()
        for k in range(1, 4):
            back_near(k).start()
        last_part(2)
        complete(last_phase)
        dense_copy().start()
        for k in range(1, 4):
            back_near(k).wait()
        sum_ref[...] = gathered[0:16]
        dense_copy().wait()
        for part in range(3):
            frames_copy(tile, part).wait()


def backward(tiles, anys, hg, lg, active, w1, w2, w3, p2, q1, owners, owner_count, capacity, losses, sum1, sum2):
    lanes = hg.shape[-1]
    small = (hg, lg, active, w1, w2, w3, p2, q1, owners, losses, sum1, sum2)
    totals = [(768, 160), (1024, 192), (1152, 256), (160, LANES), (3136, LANES), (512, LANES)]
    totals += [(576, LANES), (256, LANES)]
    pack_shape = (2 * SLICE * owner_count, LANES)
    dense_shape = (2048, 512)
    frames_shape = (84, 84, 2, lanes)
    high_count = owner_count // 4
    copies = 8 + 2 * high_count + 4
    transfers = 4 * (owner_count.bit_length() - 1)
    return pl.pallas_call(
        functools.partial(backward_kernel, capacity),
        grid=(lanes // LANES,),
        in_specs=[pl.BlockSpec((None,) + a.shape[1:], lambda i: (i, 0, 0, 0)) for a in tiles]
        + [pl.BlockSpec(memory_space=pl.ANY)] * len(anys)
        + [whole(a.shape) for a in small],
        out_specs=[pl.BlockSpec(memory_space=pl.ANY)] * 2 + [whole((16, SLICE, LANES)), whole((SLICE, LANES))],
        out_shape=[jax.ShapeDtypeStruct(s, BF16) for s in (frames_shape, dense_shape)]
        + [jax.ShapeDtypeStruct(s, F32) for s in ((16, SLICE, LANES), (SLICE, LANES))],
        scratch_shapes=[pltpu.VMEM(s, F32) for s in totals + [(pack_shape[0] // 2, LANES)]]
        + [
            pltpu.VMEM((128, 256), BF16),
            pltpu.VMEM((192, 960), BF16),
            pltpu.VMEM((11, 11 * 64, LANES), BF16),
            pltpu.VMEM((11, 11 * 64, LANES), BF16),
            pltpu.VMEM((22, 704, LANES), BF16),
            pltpu.VMEM((84, 168, LANES), BF16),
            pltpu.VMEM((224, 512), BF16),
            pltpu.SemaphoreType.DMA((3,)),
            pltpu.SemaphoreType.DMA,
            pltpu.VMEM((20, 640, LANES), BF16),
            pltpu.VMEM((20, 640, LANES), BF16),
            pltpu.VMEM((44, 336, LANES), BF16),
            pltpu.VMEM((1568, lanes), BF16),
            pltpu.VMEM((3136, 512), BF16),
            pltpu.SemaphoreType.DMA,
            pltpu.VMEM(dense_shape, BF16),
            pltpu.VMEM(dense_shape, BF16),
            pltpu.VMEM(dense_shape, BF16),
            pltpu.SemaphoreType.DMA((2,)),
            pltpu.SemaphoreType.DMA,
            pltpu.SemaphoreType.DMA,
            pltpu.SemaphoreType.DMA((transfers,)),
            pltpu.SemaphoreType.DMA((transfers,)),
            pltpu.VMEM(pack_shape, BF16),
            pltpu.VMEM((8, high_count * SLICE, LANES), BF16),
            pltpu.VMEM((high_count * SLICE, LANES), F32),
            pltpu.VMEM((high_count, high_count * SLICE, LANES), BF16)
            if high_count <= 4
            else pltpu.VMEM((high_count, SLICE, LANES), F32),
            pltpu.VMEM((SLICE, LANES), F32),
            pltpu.VMEM((owner_count, SLICE, LANES), F32),
            pltpu.SemaphoreType.DMA((copies,)),
            pltpu.SemaphoreType.DMA((copies,)),
        ],
        compiler_params=pltpu.CompilerParams(
            collective_id=1, has_side_effects=True, vmem_limit_bytes=60 * 1024 * 1024
        ),
        cost_estimate=pl.CostEstimate(
            flops=3 * 7729152 * lanes, bytes_accessed=6 * 28224 * lanes, transcendentals=0
        ),
    )(*tiles, *anys, *small)


def last_kernel(
    owners,
    loss_scale,
    section_ref,
    frames_any,
    dense_ref,
    sum_ref,
    own_ref,
    out_any,
    one_ref,
    two_ref,
    k1_ref,
    k2_ref,
    k3_ref,
    o1_ref,
    o2_ref,
    o3_ref,
    d1_ref,
    d2_ref,
    loss_ref,
    table_ref,
    buffer,
    in_sems,
    out_sems,
):
    step = pl.program_id(0)
    parts = in_sems.shape[0]
    part_rows = frames_any.shape[0] // parts

    def copy_in(k):
        rows = pl.ds(part_rows * k, part_rows)
        return pltpu.make_async_copy(frames_any.at[rows], buffer.at[rows], in_sems.at[k])

    def copy_out(k):
        rows = pl.ds(part_rows * k, part_rows)
        return pltpu.make_async_copy(buffer.at[rows], out_any.at[rows], out_sems.at[k])

    @pl.when(step == 0)
    def _():
        for k in range(parts):
            copy_in(k).start()
        two_ref[0:464, :] = dense_ref[1568:2032, 0:256].astype(F32)
        two_ref[464:918, :] = dense_ref[1568:2022, 256:512].astype(F32)
        if owners == 16:
            mine = own_ref[pl.ds(pl.multiple_of(8 * section_ref[0], 8), 8), :]
            table_ref[0] = 0.5 * mine[:, 96 : 96 + table_ref.shape[2]]
        for c in range(4):
            k1_ref[64 * c : 64 * c + 64, :] = sum_ref[288:352, 16 * c : 16 * c + 16]
        k2_ref[...] = sum_ref[:, 64:96]
        k3_ref[...] = sum_ref[0:288, 0:64]
        o1_ref[...] = 0.5 * sum_ref[352:353, 0:16]
        o2_ref[...] = 0.5 * sum_ref[353:354, 0:32]
        o3_ref[...] = 0.5 * sum_ref[354:355, 0:32]
        loss_ref[...] = loss_scale * sum_ref[355:356, 0:1]
        for k in range(4):
            d1_ref[:, 64 * k : 64 * k + 64] = 0.5 * sum_ref[384 + k : 385 + k, 0:64]
        for k in range(8):
            size = min(64, 459 - 64 * k)
            d2_ref[:, 64 * k : 64 * k + size] = 0.5 * sum_ref[388 + k : 389 + k, 0:size]

        for k in range(parts):
            copy_in(k).wait()
            copy_out(k).start()

    at = pl.ds(pl.multiple_of(step * 784, 16), 784)
    one_ref[...] = dense_ref[at, :].astype(F32)

    @pl.when(step == pl.num_programs(0) - 1)
    def _():
        for k in range(parts):
            copy_out(k).wait()


def last(owners, capacity, section, frames, dense, sums, own):
    others = [(918, 256), (256, 16), (512, 32), (288, 64), (1, 16), (1, 32), (1, 32), (1, 256), (1, 459), (1, 1), (1, 8, capacity)]
    return pl.pallas_call(
        functools.partial(last_kernel, owners, 0.5 / (frames.shape[3] * owners)),
        grid=(2,),
        in_specs=[
            pl.BlockSpec(memory_space=pltpu.SMEM),
            pl.BlockSpec(memory_space=pl.ANY),
            whole(dense.shape),
            whole(sums.shape),
            whole(own.shape),
        ],
        out_specs=[pl.BlockSpec(memory_space=pl.ANY), pl.BlockSpec((784, 512), lambda i: (i, 0))]
        + [whole(a) for a in others],
        out_shape=[
            jax.ShapeDtypeStruct(frames.shape, BF16),
            jax.ShapeDtypeStruct((1568, 512), F32),
        ]
        + [jax.ShapeDtypeStruct(a, F32) for a in others],
        scratch_shapes=[
            pltpu.VMEM(frames.shape, BF16),
            pltpu.SemaphoreType.DMA((7,)),
            pltpu.SemaphoreType.DMA((7,)),
        ],
        compiler_params=pltpu.CompilerParams(vmem_limit_bytes=60 * 1024 * 1024),
        cost_estimate=pl.CostEstimate(flops=0, bytes_accessed=2**25, transcendentals=0),
    )(section, frames, dense, sums, own)


def shards(
    frames,
    next_frames,
    actions,
    next_actions,
    lengths,
    terminal,
    rewards,
    discounts,
    owners,
    conv_one_weight,
    conv_one_offset,
    conv_two_weight,
    conv_two_offset,
    conv_three_weight,
    conv_three_offset,
    dense_one_weight,
    dense_one_offset,
    dense_two_weight,
    dense_two_offset,
    target_conv_one_weight,
    target_conv_one_offset,
    target_conv_two_weight,
    target_conv_two_offset,
    target_conv_three_weight,
    target_conv_three_offset,
    target_dense_one_weight,
    target_dense_one_offset,
    target_dense_two_weight,
    target_dense_two_offset,
):
    section = lax.axis_index("section")
    owner_count = lax.axis_size("batch")
    rows = frames.shape[0]
    p1, p2, q1 = order_rows(4, 8), order_rows(32, 4), back_one_choice()

    def tower_weights(one, two, three, off_one, off_two, off_three):
        return (
            one.transpose(1, 2, 3, 0).reshape(256, 32),
            two.transpose(1, 2, 3, 0).reshape(512, 64),
            three.transpose(2, 3, 0, 1).reshape(9, 64, 64),
            off_one[None, :],
            off_two[None, :],
            off_three[None, :],
        )

    online = tower_weights(
        conv_one_weight, conv_two_weight, conv_three_weight, conv_one_offset, conv_two_offset, conv_three_offset
    )
    target = tower_weights(
        target_conv_one_weight,
        target_conv_two_weight,
        target_conv_three_weight,
        target_conv_one_offset,
        target_conv_two_offset,
        target_conv_three_offset,
    )
    x = frames.transpose(2, 3, 1, 0)
    x_next = next_frames.transpose(2, 3, 1, 0)
    section_row = section.reshape(1).astype(jnp.int32)
    vectors = [
        a.reshape(a.shape[0] // LANES, LANES)
        for a in (dense_one_offset, target_dense_one_offset, actions, next_actions, lengths, terminal)
    ]
    a1, s1, a2, s2, s3, feature, active, logit_grad, hidden_grad, row_loss, sum1, sum2 = head(
        x,
        x_next,
        dense_one_weight,
        target_dense_one_weight,
        (
            *online,
            *target,
            p1,
            p2,
            dense_two_weight.T,
            target_dense_two_weight.T,
            *vectors,
            dense_two_offset,
            target_dense_two_offset,
            rewards.T,
            discounts.T,
        ),
    )

    capacity = (rows + owner_count - 1) // owner_count + 1
    frames_grad, dense, sums, own = backward(
        (a2, s2, s3),
        (a1, s1, x, feature, dense_one_weight),
        hidden_grad,
        logit_grad,
        active,
        *online[:3],
        p2,
        q1,
        owners.T,
        owner_count,
        capacity,
        row_loss,
        sum1,
        sum2,
    )
    frames_grad, grad_dense_one, grad_dense_two, one, two, three, *rest = last(
        owner_count, capacity, section_row, frames_grad, dense, sums.reshape(16 * SLICE, LANES), own
    )
    off_one, off_two, off_three, dense_off_one, dense_off_two, loss, table = rest
    if owner_count != 16:
        groups = -(-owner_count // SLICE)
        table = 0.5 * own[:, 96 : 96 + groups * capacity].reshape(SLICE, groups, capacity)
        table = table.transpose(1, 0, 2).reshape(groups * SLICE, capacity)
        table = lax.dynamic_slice_in_dim(table, section * (owner_count // 2), owner_count // 2, 0)[None]
    return (
        loss[0, 0],
        frames_grad.transpose(3, 2, 0, 1),
        one.reshape(4, 8, 8, 16).transpose(3, 0, 1, 2),
        off_one[0],
        two.reshape(32, 4, 4, 32).transpose(0, 3, 1, 2),
        off_two[0],
        three.reshape(3, 3, 32, 64).transpose(2, 3, 0, 1),
        off_three[0],
        grad_dense_one,
        dense_off_one[0],
        grad_dense_two.T,
        dense_off_two[0],
        table,
    )


def solution(mesh):
    return jax.shard_map(
        shards,
        mesh=mesh,
        in_specs=(P("batch", None, None, None),) * 2
        + (P("batch"),) * 4
        + (P("batch", None),) * 3
        + (P(),) * 20,
        out_specs=(
            P(),
            P("batch", "section", None, None),
            P("section", None, None, None),
            P("section"),
            P("section", None, None, None),
            P("section"),
            P("section", None, None, None),
            P("section"),
            P("section", None),
            P("section"),
            P("section", None),
            P("section"),
            P("batch", "section", None),
        ),
        check_vma=False,
    )
```

```python
import functools

import jax
import jax.numpy as jnp
import numpy as np
from jax import lax
from jax.experimental import pallas as pl
from jax.experimental.pallas import tpu as pltpu
from jax.sharding import PartitionSpec as P

ACTIONS = 18
ATOMS = 51
NSTEP = 3
LANES = 128
SLICE = 32
ROW_CHUNKS = ((0, 36), (36, 84))
MESH = pl.DeviceIdType.MESH
support_low = -10.0
support_high = 10.0
F32 = jnp.float32
BF16 = jnp.bfloat16
NT = (((1,), (1,)), ((), ()))


def nn_dot(a, b):
    return jnp.dot(a, b, preferred_element_type=F32)


def nt_dot(a, b):
    return lax.dot_general(a, b, NT, preferred_element_type=F32)


def stack(parts):
    return jnp.concatenate(parts, axis=0)


def beside(parts):
    return jnp.concatenate(parts, axis=1)


def eye(size):
    rows = lax.broadcasted_iota(jnp.int32, (size, size), 0)
    cols = lax.broadcasted_iota(jnp.int32, (size, size), 1)
    return jnp.where(rows == cols, 1.0, 0.0).astype(BF16)


def order_rows(channels, extent):
    count = channels * extent * extent
    chosen = np.zeros((count, count), np.float32)
    for c in range(channels):
        for u in range(extent):
            for v in range(extent):
                chosen[(u * extent + v) * channels + c, (c * extent + u) * extent + v] = 1.0
    return jnp.asarray(chosen, BF16)


def back_one_choice():
    chosen = np.zeros((2, 8, 4, 28, 2, 128), np.float32)
    for dp in range(2):
        for dq in range(8):
            for i in range(4):
                for x in range(28):
                    u, v = i + 4 * (1 - dp), x + 4 - 4 * dq
                    if 0 <= v < 8:
                        for ch in range(2):
                            chosen[dp, dq, i, x, ch, ch * 64 + u * 8 + v] = 1.0
    return jnp.asarray(chosen.reshape(16 * 224, 128), BF16)


def lane_bias(row, size):
    return nt_dot(eye(size), jnp.broadcast_to(row, (LANES, size)))


def activate(h):
    t = jnp.tanh(h)
    m = h * t
    return h + m, (1.0 + t) * ((1.0 + h) - m)


def in_turn(jobs):
    waiting = None
    for first, then in jobs:
        value = first()
        if waiting is not None:
            waiting[0](waiting[1])
        waiting = (then, value)
    waiting[0](waiting[1])


def whole(shape):
    return pl.BlockSpec(shape, lambda i, *_: (0,) * len(shape))


def by_lane(shape):
    return pl.BlockSpec(shape[:-1] + (LANES,), lambda i, *_: (0,) * (len(shape) - 1) + (i,))


def lane_column(row):
    size = row.shape[1]
    parts = []
    for at in range(0, size, LANES):
        step = min(LANES, size - at)
        parts.append(lane_bias(row[:, at : at + step], step))
    return stack(parts)


def softmax_terms(v):
    top = jnp.max(v, axis=0, keepdims=True)
    e = jnp.exp(v - top)
    total = jnp.sum(e, axis=0, keepdims=True)
    return e / total, v - top - jnp.log(total)


def head_kernel(
    x_any,
    y_any,
    dense_any,
    target_dense_any,
    w1_ref,
    w2_ref,
    w3_ref,
    o1_ref,
    o2_ref,
    o3_ref,
    v1_ref,
    v2_ref,
    v3_ref,
    q1_ref,
    q2_ref,
    q3_ref,
    p1_ref,
    p2_ref,
    out_ref,
    target_out_ref,
    b1_ref,
    d1_ref,
    action_ref,
    later_action_ref,
    length_ref,
    terminal_ref,
    b2_ref,
    d2_ref,
    rewards_ref,
    discounts_ref,
    a1_any,
    s1_any,
    a2_any,
    s2_any,
    s3_any,
    f_any,
    active_ref,
    lg_ref,
    hg_ref,
    loss_ref,
    sum1_ref,
    sum2_ref,
    wt1,
    wt2,
    wt3,
    wt4,
    c1,
    c2,
    c3,
    c4,
    fs,
    fb,
    xbuf,
    a1,
    s1,
    a2,
    s2,
    s3,
    wd,
    wdt,
    pre,
    hidden,
    late,
    back,
    logits,
    logits_later,
    lgs,
    probs,
    position,
    n1,
    n2,
    n3,
    m1,
    m2,
    m3,
    x_sems,
    out_sems,
    wd_sem,
    sent,
    came,
):
    section, batch = lax.axis_index("section"), lax.axis_index("batch")
    step, steps = pl.program_id(0), pl.num_programs(0)
    lanes = hidden.shape[1]
    tiles = lanes // LANES
    targets = tiles - 1
    online = step >= targets
    slot = lax.rem(step, 2)
    height, width, stacked, _ = x_any.shape

    def lanes_of(index):
        return pl.ds(pl.multiple_of(index * LANES, LANES), LANES)

    def x_copy(source, tile, at, k):
        place = lax.rem(at, 2)
        first, last = ROW_CHUNKS[k]
        pixels = source.reshape(height, width * stacked, lanes)
        return pltpu.make_async_copy(
            pixels.at[first:last, :, lanes_of(tile)], xbuf.at[place, first:last], x_sems.at[place, k]
        )

    def start_x(at):
        @pl.when(at < targets)
        def _():
            for k in range(len(ROW_CHUNKS)):
                x_copy(y_any, jnp.minimum(at, targets - 1) + section, at, k).start()

        @pl.when((at >= targets) & (at < steps))
        def _():
            for k in range(len(ROW_CHUNKS)):
                x_copy(x_any, jnp.clip(at - targets, 0, tiles - 1), at, k).start()

    tile = jnp.maximum(step - targets, 0)
    outs = ((a1, a1_any), (s1, s1_any), (a2, a2_any), (s2, s2_any), (s3, s3_any), (fb, f_any))

    def out_copy(k, at):
        source, into = outs[k]
        place = into.at[:, lanes_of(at)] if k == 5 else into.at[at]
        return pltpu.make_async_copy(source, place, out_sems.at[k])

    def wait_outs(which):
        @pl.when(step > targets)
        def _():
            for k in which:
                out_copy(k, jnp.maximum(tile - 1, 0)).wait()

    def start_outs(which):
        @pl.when(online)
        def _():
            for k in which:
                out_copy(k, tile).start()

    def swap():
        return pltpu.make_async_remote_copy(
            src_ref=late.at[:, lanes_of((tiles - 1) * section)],
            dst_ref=late.at[:, lanes_of((tiles - 1) * section)],
            send_sem=sent,
            recv_sem=came,
            device_id=(1 - section, batch),
            device_id_type=MESH,
        )

    def dense_copy(source):
        return pltpu.make_async_copy(source, wd, wd_sem)

    @pl.when(step == 0)
    def _():
        barrier = pltpu.get_barrier_semaphore()
        pl.semaphore_signal(barrier, inc=1, device_id=(1 - section, batch), device_id_type=MESH)
        start_x(step)
        dense_copy(target_dense_any).start()

    start_x(step + 1)

    def prepare(one_ref, two_ref, three_ref, off_one, off_two, off_three):
        wt1[...] = jnp.zeros_like(wt1)
        wt2[...] = jnp.zeros_like(wt2)
        wt3[...] = jnp.zeros_like(wt3)
        base = nt_dot(eye(32), nn_dot(p1_ref[...], one_ref[...]).astype(BF16))
        base = (0.5 * base).astype(BF16)
        for t in range(5):
            for u in range(8):
                wt1[32 * t : 32 * t + 32, 96 * u + 16 * t : 96 * u + 16 * t + 32] = base[:, 32 * u : 32 * u + 32]
        base = nt_dot(eye(64), nn_dot(p2_ref[...], two_ref[...]).astype(BF16))
        base = (0.5 * base).astype(BF16)
        for t in range(3):
            for u in range(4):
                wt2[64 * t : 64 * t + 64, 256 * u + 64 * t : 256 * u + 64 * t + 128] = base[:, 128 * u : 128 * u + 128]
        for u in range(3):
            for v in range(3):
                piece = (0.5 * three_ref[3 * u + v].astype(F32)).astype(BF16)
                wt4[:, 192 * u + 64 * v : 192 * u + 64 * v + 64] = piece
                for t in range(2):
                    at = 256 * u + 64 * t + 64 * v
                    wt3[64 * t : 64 * t + 64, at : at + 64] = piece
        c1[...] = stack([0.5 * lane_bias(off_one[...], 32)] * 5)
        c2[...] = stack([0.5 * lane_bias(off_two[...], 64)] * 3)
        column = 0.5 * lane_bias(off_three[...], 64)
        c3[...] = stack([column] * 2)
        c4[...] = column

    now = (n1, n2, n3, m1, m2, m3)

    @pl.when(step == 0)
    def _():
        for to, of in zip(now, (v1_ref, v2_ref, v3_ref, q1_ref, q2_ref, q3_ref)):
            to[...] = of[...]

    @pl.when(step == targets)
    def _():
        for to, of in zip(now, (w1_ref, w2_ref, w3_ref, o1_ref, o2_ref, o3_ref)):
            to[...] = of[...]

    @pl.when((step == 0) | (step == targets))
    def _():
        prepare(*now)

    def put(bias, act, slope, places):
        def then(value):
            for k, (row, at, size) in enumerate(places):
                a, s = activate(value[:, LANES * k : LANES * k + LANES] + bias[...])
                act[row, at : at + size, :] = a.astype(BF16)
                slope[row, at : at + size, :] = s.astype(BF16)

        return then

    def strips_one(i, s):
        def dot():
            cols = [
                stack([xbuf[slot, 8 * i + 4 * k + u, 80 * s : 80 * s + 96, :] for u in range(8)])
                for k in range(2)
            ]
            return nn_dot(wt1[...], beside(cols))

        return dot, put(c1, a1, s1, [(2 * i + k, 160 * s, 160) for k in range(2)])

    wait_outs((0, 1))
    for k, pairs in enumerate((range(0, 4), range(4, 10))):
        x_copy(x_any, tile, step, k).wait()
        in_turn([strips_one(i, s) for i in pairs for s in range(4)])
    start_outs((0, 1))
    wait_outs((2, 3, 4, 5))

    def strips_two(places):
        def dot():
            cols = [
                stack([a1[2 * p + u, 192 * s : 192 * s + 256, :] for u in range(4)])
                for p, s in places
            ]
            return nn_dot(wt2[...], beside(cols))

        return dot, put(c2, a2, s2, [(p, 192 * s, 192) for p, s in places])

    def strips_three(places, weight, bias, count):
        def dot():
            cols = [
                stack([a2[p + u, 64 * q : 64 * q + 64 * count + 128, :] for u in range(3)])
                for p, q in places
            ]
            return nn_dot(weight[...], beside(cols))

        def then(value):
            for k, (p, q) in enumerate(places):
                a, s = activate(value[:, LANES * k : LANES * k + LANES] + bias[...])
                for t in range(count):
                    fs[pl.ds(7 * p + q + t, 64, stride=49), :] = a[64 * t : 64 * t + 64, :]
                s3[p, 64 * q : 64 * q + 64 * count, :] = s.astype(BF16)

        return dot, then

    two = [(2 * i + k, s) for i in range(4) for s in range(3) for k in range(2)]
    two += [(8, s) for s in range(3)]
    three = [(p, q) for p in range(7) for q in (0, 2, 4)]
    ends = [(p, 6) for p in range(7)]
    in_turn(
        [strips_two(two[k : k + 2]) for k in range(0, len(two), 2)]
        + [strips_three(three[k : k + 2], wt3, c3, 2) for k in range(0, len(three), 2)]
        + [strips_three(ends[k : k + 2], wt4, c4, 1) for k in range(0, len(ends), 2)]
    )
    fb[...] = fs[...].astype(BF16)
    start_outs((2, 3, 4, 5))

    def turn(source):
        dense_copy(source).wait()
        unit = eye(512)
        for at in range(0, wd.shape[0], 256):
            size = min(256, wd.shape[0] - at)
            wdt[:, at : at + size] = nt_dot(unit, wd[at : at + size, :]).astype(BF16)

    @pl.when((step == 0) | (step == targets))
    def _():
        turn(dense_any)

    @pl.when(step == 0)
    def _():
        dense_copy(dense_any).start()

    def column(rows_ref):
        return stack([lane_bias(rows_ref[k : k + 1, :], LANES) for k in range(rows_ref.shape[0])])

    pre[...] = nn_dot(wdt[...], fb[...])

    @pl.when(step < targets)
    def _():
        later, _ = activate(0.5 * (pre[...] + column(d1_ref)))
        late[:, lanes_of(jnp.minimum(step, targets - 1) + section)] = later.astype(BF16)

    @pl.when(step == targets - 1)
    def _():
        pl.semaphore_wait(pltpu.get_barrier_semaphore(), 1)
        swap().start()

    @pl.when(online)
    def _():
        hidden[:, lanes_of(tile)] = pre[...] + column(b1_ref)

    @pl.when(step == steps - 1)
    def _():
        count = out_ref.shape[0]
        back[...] = jnp.zeros_like(back)
        lgs[...] = jnp.zeros_like(lgs)
        for at in range(0, count, 256):
            size = min(256, count - at)
            back[:, at : at + size] = nt_dot(eye(512), out_ref[at : at + size, :]).astype(BF16)

        def wide(ref):
            return beside([lane_column(ref[...].reshape(1, count))] * tiles)

        active, slope = activate(0.5 * hidden[...])
        active = active.astype(BF16)
        active_ref[...] = active
        logits[...] = nn_dot(out_ref[...], active) + wide(b2_ref)
        swap().wait()
        logits_later[...] = nn_dot(target_out_ref[...], late[...]) + wide(d2_ref)

        def row(ref):
            return beside([ref[k : k + 1, :] for k in range(tiles)])

        action, later_action = row(action_ref), row(later_action_ref)
        length, terminal = row(length_ref), row(terminal_ref)

        def pick(ref, ids):
            total = jnp.zeros((ATOMS, lanes), F32)
            for a in range(ACTIONS):
                total = total + jnp.where(ids == a, ref[ATOMS * a : ATOMS * a + ATOMS, :], 0.0)
            return total

        soft, log_soft = softmax_terms(pick(logits, action))
        returns = jnp.zeros((1, lanes), F32)
        bootstrap = jnp.zeros((1, lanes), F32)
        product = jnp.ones((1, lanes), F32)
        for k in range(NSTEP):
            returns = returns + jnp.where(length > k, product * rewards_ref[k : k + 1, :], 0.0)
            product = product * discounts_ref[k : k + 1, :]
            bootstrap = bootstrap + jnp.where(length == k + 1, product, 0.0)
        bootstrap = bootstrap * (1.0 - terminal.astype(F32))
        spacing = (support_high - support_low) / (ATOMS - 1)
        ids = lax.broadcasted_iota(jnp.int32, (ATOMS, lanes), 0).astype(F32)
        shifted = jnp.clip(returns + bootstrap * (support_low + spacing * ids), support_low, support_high)
        position[...] = (shifted - support_low) / spacing
        probs[...], _ = softmax_terms(pick(logits_later, later_action))
        mass = jnp.zeros((ATOMS, lanes), F32)
        for j in range(ATOMS):
            weight = jnp.maximum(0.0, 1.0 - jnp.abs(position[j : j + 1, :] - ids))
            mass = mass + probs[j : j + 1, :] * weight
        loss_ref[...] = -jnp.sum(mass * log_soft, axis=0, keepdims=True)
        chosen_grad = jnp.sum(mass, axis=0, keepdims=True) * soft - mass
        for a in range(ACTIONS):
            lgs[ATOMS * a : ATOMS * a + ATOMS, :] = jnp.where(action == a, chosen_grad, 0.0)
        lg = lgs[...].astype(BF16)
        lg_ref[...] = lg[0:count]
        hg = (nn_dot(back[...], lg) * (0.5 * slope)).astype(BF16)
        hg_ref[...] = hg
        ones = jnp.ones((8, lanes), BF16)
        sum1_ref[...] = nt_dot(ones, hg)
        sum2_ref[...] = nt_dot(ones, lg[0:count])
        for k in range(len(outs)):
            out_copy(k, tile).wait()


def head(x, y, dense_one, target_dense_one, small):
    lanes = x.shape[3]
    count = small[14].shape[0]
    tiles = lanes // LANES
    outs = [(20, 640), (20, 640), (9, 576), (9, 576), (7, 448)]
    outs = [(tiles,) + shape + (LANES,) for shape in outs] + [(3136, lanes)]
    rest = [((512, lanes), BF16), ((count, lanes), BF16), ((512, lanes), BF16), ((1, lanes), F32)]
    rest += [((8, 512), F32), ((8, count), F32)]
    anywhere = pl.BlockSpec(memory_space=pl.ANY)
    buffers = [
        ((160, 768), BF16),
        ((192, 1024), BF16),
        ((128, 768), BF16),
        ((64, 576), BF16),
        ((160, LANES), F32),
        ((192, LANES), F32),
        ((128, LANES), F32),
        ((64, LANES), F32),
        ((3136, LANES), F32),
        ((3136, LANES), BF16),
        ((2, 84, 336, LANES), BF16),
        ((20, 640, LANES), BF16),
        ((20, 640, LANES), BF16),
        ((9, 576, LANES), BF16),
        ((9, 576, LANES), BF16),
        ((7, 448, LANES), BF16),
        ((3136, 512), BF16),
        ((512, 3136), BF16),
        ((512, LANES), F32),
        ((512, lanes), F32),
        ((512, lanes), BF16),
        ((512, 1024), BF16),
        ((count, lanes), F32),
        ((count, lanes), F32),
        ((1024, lanes), F32),
        ((ATOMS, lanes), F32),
        ((ATOMS, lanes), F32),
    ] + [(a.shape, BF16) for a in small[:6]]
    return pl.pallas_call(
        head_kernel,
        grid=(2 * (lanes // LANES) - 1,),
        in_specs=[anywhere] * 4 + [whole(a.shape) for a in small],
        out_specs=[anywhere] * len(outs) + [whole(s) for s, _ in rest],
        out_shape=[jax.ShapeDtypeStruct(s, BF16) for s in outs]
        + [jax.ShapeDtypeStruct(s, t) for s, t in rest],
        scratch_shapes=[pltpu.VMEM(s, t) for s, t in buffers]
        + [
            pltpu.SemaphoreType.DMA((2, len(ROW_CHUNKS))),
            pltpu.SemaphoreType.DMA((len(outs),)),
            pltpu.SemaphoreType.DMA,
            pltpu.SemaphoreType.DMA,
            pltpu.SemaphoreType.DMA,
        ],
        compiler_params=pltpu.CompilerParams(
            collective_id=0, has_side_effects=True, vmem_limit_bytes=60 * 1024 * 1024
        ),
        cost_estimate=pl.CostEstimate(
            flops=5 * 2 * 9785600 * LANES, bytes_accessed=2**26, transcendentals=0
        ),
    )(x, y, dense_one, target_dense_one, *small)


def backward_kernel(
    capacity,
    a2_ref,
    s2_ref,
    s3_ref,
    a1_any,
    s1_any,
    x_any,
    f_any,
    dense_weight_any,
    hg_ref,
    lg_ref,
    active_ref,
    w1_ref,
    w2_ref,
    w3_ref,
    p2_ref,
    q1_ref,
    owner_ref,
    loss_ref,
    sum1_ref,
    sum2_ref,
    frames_any,
    dense_any,
    sum_ref,
    own_ref,
    t1_ref,
    t2_ref,
    t3_ref,
    tb_ref,
    fcs,
    stage,
    turned,
    first,
    packed,
    wb2,
    wb3,
    g2,
    g3,
    g1,
    frames,
    wb1,
    frame_sems,
    dense_sem,
    a1_ref,
    s1_ref,
    xbuf,
    fbuf,
    dense_weight_ref,
    weight_sem,
    slab,
    landed,
    shared,
    a_sems,
    x_sem,
    f_sem,
    sent,
    came,
    pack,
    arrived,
    total,
    crossed,
    share,
    gathered,
    left,
    reached,
):
    section, batch = lax.axis_index("section"), lax.axis_index("batch")
    owners = lax.axis_size("batch")
    bits = owners.bit_length() - 1
    tile = pl.program_id(0)
    last_tile = pl.num_programs(0) - 1

    dense_rows = slab.shape[0]
    bit = [lax.rem(batch // (1 << k), 2) for k in range(bits)]
    colours = 2 if bits < 7 else 1
    region = dense_rows // (2 * colours)
    orders = [list(range(1, bits)) for _ in range(colours)]
    orders[-1] = orders[-1][(bits - 1) // 2 :] + orders[-1][: (bits - 1) // 2]
    base = (dense_rows // 2) * bit[0]
    bases = []
    for c in range(colours):
        starts = [base + c * region]
        for m, k in enumerate(orders[c]):
            starts.append(starts[-1] + (region >> (m + 1)) * bit[k])
        bases.append(starts)

    def rows_at(start, size):
        return pl.ds(pl.multiple_of(start, 16), size)

    def moves(phase):
        if phase in (0, 2 * bits - 1):
            half = dense_rows // 2
            if phase:
                return [(0, base, half, None, None)]
            return [(0, half * (1 - bit[0]), half, 0, base)]
        found = []
        for c in range(colours):
            m = phase - 1 if phase < bits else 2 * bits - 2 - phase
            size = region >> (m + 1)
            k, start = orders[c][m], bases[c][m]
            if phase < bits:
                place = dense_rows // 2 + (c + 1) * region - 2 * size
                found.append((k, start + size * (1 - bit[k]), size, place, bases[c][m + 1]))
            else:
                found.append((k, bases[c][m + 1], size, None, None))
        return found

    def transfers(phase):
        copies = []
        for c, (k, start, size, place, _) in enumerate(moves(phase)):
            if phase < bits:
                source, into = slab.at[rows_at(start, size), :], landed.at[pl.ds(place, size), :]
            else:
                source = into = shared.at[rows_at(start, size), :]
            copies.append(
                pltpu.make_async_remote_copy(
                    src_ref=source,
                    dst_ref=into,
                    send_sem=sent.at[2 * phase + c],
                    recv_sem=came.at[2 * phase + c],
                    device_id=(section, batch + (1 << k) * (1 - 2 * bit[k])),
                    device_id_type=MESH,
                )
            )
        return copies

    def complete(phase):
        for copy, (_, _, size, place, to) in zip(transfers(phase), moves(phase)):
            copy.wait()
            if phase < bits:
                step = min(size, 64)

                def add(n, carry, step=step, place=place, to=to):
                    at = rows_at(to + step * n, step)
                    more = landed[pl.ds(pl.multiple_of(place + step * n, 16), step), :]
                    slab[at, :] = (slab[at, :].astype(F32) + more.astype(F32)).astype(BF16)
                    return carry

                lax.fori_loop(0, size // step, add, 0)
        if phase == bits - 1:
            for c in range(colours):
                own = rows_at(bases[c][-1], region >> (bits - 1))
                shared[own, :] = slab[own, :]

    starts = [0, 1, 2, 3, 5, 6, 8]
    if bits != 4:
        starts = [9 * phase // (2 * bits - 1) for phase in range(2 * bits - 1)]
    last_phase = 2 * bits - 1

    def slot(index):
        for phase, at in enumerate(starts):
            if phase > 0 and at % 3 == index:

                @pl.when(tile == at // 3)
                def _(phase=phase):
                    complete(phase - 1)
                    for copy in transfers(phase):
                        copy.start()

    high_count = owners // 4
    block = high_count * SLICE
    low, high = lax.rem(batch, 4), batch // 4
    group = section * 4 + low
    place = low * high_count + high

    def near(k):
        index = lax.rem(group + k, 8)
        return index, (index // 4, high * 4 + lax.rem(index, 4))

    def far(k):
        index = lax.rem(high + k, high_count)
        return index, (section, index * 4 + low)

    def send(source, into, device, number):
        return pltpu.make_async_remote_copy(
            src_ref=source,
            dst_ref=into,
            send_sem=left.at[number],
            recv_sem=reached.at[number],
            device_id=device,
            device_id_type=MESH,
        )

    def rows_of(index, size):
        return pl.ds(pl.multiple_of(index * size, size), size)

    def to_near(k):
        index, device = near(k)
        return send(pack.at[rows_of(index, block), :], arrived.at[group], device, k)

    short = high_count <= 4

    def to_far(k):
        index, device = far(k)
        source = crossed.at[high] if short else total.at[rows_of(index, SLICE), :]
        return send(source, crossed.at[high], device, 8 + k)

    def back_far(k):
        return send(share, gathered.at[place], far(k)[1], 8 + high_count + k)

    def back_near(k):
        ours = gathered.at[pl.ds(low * high_count, high_count)]
        device = (section, high * 4 + lax.rem(low + k, 4))
        return send(ours, ours, device, 8 + 2 * high_count + k)

    def a_copy(at, k):
        source, into = ((a1_any, a1_ref), (s1_any, s1_ref))[k]
        return pltpu.make_async_copy(source.at[at], into, a_sems.at[k])

    def dense_copy():
        return pltpu.make_async_copy(shared, dense_any, dense_sem)

    height, width, stacked, lane_count = x_any.shape
    pixels = x_any.reshape(height, width * stacked, lane_count)

    def x_copy():
        return pltpu.make_async_copy(
            pixels.at[pl.ds(40 * section, 44), :, pl.ds(pl.multiple_of(tile * LANES, LANES), LANES)],
            xbuf,
            x_sem,
        )

    def f_copy():
        half = fbuf.shape[0]
        return pltpu.make_async_copy(f_any.at[rows_at(half * section, half), :], fbuf, f_sem)

    def weight_copy():
        return pltpu.make_async_copy(dense_weight_any, dense_weight_ref, weight_sem)

    @pl.when(tile == 0)
    def _():
        f_copy().start()
        weight_copy().start()
        for k in range(2):
            a_copy(tile, k).start()
        barrier = pltpu.get_barrier_semaphore()
        for k in range(1, 8):
            pl.semaphore_signal(barrier, inc=1, device_id=near(k)[1], device_id_type=MESH)
        for k in range(1, high_count):
            pl.semaphore_signal(barrier, inc=1, device_id=far(k)[1], device_id_type=MESH)
        f_copy().wait()

        def dense_one(start, stop):
            for at in range(start, stop, 256):
                rows = slice(at, min(at + 256, stop))
                slab[rows, :] = nt_dot(fbuf[rows, :], hg_ref[...]).astype(BF16)

        def upper_half():
            slab[1568:dense_rows, :] = jnp.zeros((dense_rows - 1568, 512), BF16)
            mine = active_ref[pl.ds(pl.multiple_of(256 * section, 256), 256), :]
            slab[1568:2032, 0:256] = nt_dot(lg_ref[0:464, :], mine).astype(BF16)
            slab[1568:2022, 256:512] = nt_dot(lg_ref[464:918, :], mine).astype(BF16)
            dense_one(1024, 1568)

        @pl.when(bit[0] == 0)
        def _():
            upper_half()

        @pl.when(bit[0] == 1)
        def _():
            dense_one(0, 1024)

        pl.semaphore_wait(barrier, 6 + high_count)
        for copy in transfers(0):
            copy.start()

        @pl.when(bit[0] == 0)
        def _():
            dense_one(0, 1024)

        @pl.when(bit[0] == 1)
        def _():
            upper_half()

        for ref in (t1_ref, t2_ref, t3_ref, tb_ref, wb1, wb2, wb3):
            ref[...] = jnp.zeros_like(ref)
        for ref, edge, width in ((g1, 1, 32), (g2, 1, 64), (g3, 2, 64)):
            side = jnp.zeros((edge * width, LANES), BF16)
            for r in range(ref.shape[0]):
                if edge <= r < ref.shape[0] - edge:
                    ref[r, 0 : edge * width, :] = side
                    ref[r, ref.shape[1] - edge * width :, :] = side
                else:
                    ref[r] = jnp.zeros((ref.shape[1], LANES), BF16)
        rows = (0.5 * nn_dot(p2_ref[...], w2_ref[...])).astype(BF16)
        for dp in range(2):
            for dq in range(2):
                for b in range(2):
                    for x in range(2):
                        u, v = b + 2 * (1 - dp), x + 2 * (1 - dq)
                        to, at, of = 32 * (2 * b + x), 64 * (2 * dp + dq), 32 * (4 * u + v)
                        wb2[to : to + 32, at : at + 64] = rows[of : of + 32, :]
        for u in range(3):
            for v in range(3):
                piece = (0.5 * nt_dot(eye(64), w3_ref[3 * u + v])).astype(BF16)
                for t in range(3):
                    at = 320 * (2 - u) + 64 * (t + 2 - v)
                    wb3[64 * t : 64 * t + 64, at : at + 64] = piece
        half = w1_ref[pl.ds(pl.multiple_of(section * 128, 128), 128), :]
        pieces = nn_dot(q1_ref[...], half).astype(BF16)
        for k in range(16):
            wb1[:, 32 * k : 32 * k + 32] = pieces[224 * k : 224 * k + 224, :]
        weight_copy().wait()

    slot(0)
    x_copy().start()

    def sums(value, size):
        total = value[0:size]
        for at in range(size, value.shape[0], size):
            total = total + value[at : at + size]
        return total

    hg = hg_ref[:, pl.ds(pl.multiple_of(tile * LANES, LANES), LANES)]

    def feature_grad(n, carry):
        at = pl.ds(pl.multiple_of(448 * n, 448), 448)
        fcs[at, :] = 0.5 * nn_dot(dense_weight_ref[at, :], hg).astype(BF16).astype(F32)
        return carry

    lax.fori_loop(0, 7, feature_grad, 0, unroll=True)

    def cot_three(p, carry):
        cot = stack([fcs[pl.ds(7 * p + q, 64, stride=49), :] for q in range(7)])
        g = cot * s3_ref[p].astype(F32)
        g3[p + 2, 128:576, :] = g.astype(BF16)
        tb_ref[96:160, :] += sums(g, 64)
        return carry

    lax.fori_loop(0, 7, cot_three, 0, unroll=True)

    blocks, cots = [], []
    nothing = jnp.zeros((64, LANES), BF16)
    for n in range(4):
        p = 4 * section + n
        rows = [jnp.minimum(p + u, 8) for u in range(3)]
        blocks.append(stack([a2_ref[r, 0:384, :] for r in rows]))
        blocks.append(stack([part for r in rows for part in (a2_ref[r, 256:576, :], nothing)]))
        cots += [g3[p + 2, 128:384, :], g3[p + 2, 384:640, :]]
    t3_ref[...] += nt_dot(beside(blocks), beside(cots))


    def patch_three(y, s):
        return stack([g3[y + d, 192 * s : 192 * s + 320, :] for d in range(3)])

    def strips_two(places):
        def dot():
            return nn_dot(wb3[...], beside([patch_three(y, s) for y, s in places]))

        def then(value):
            for k, (y, s) in enumerate(places):
                slope = s2_ref[y, 192 * s : 192 * s + 192, :].astype(F32)
                g = value[:, LANES * k : LANES * k + LANES] * slope
                g2[y + 1, 64 + 192 * s : 256 + 192 * s, :] = g.astype(BF16)
                tb_ref[32:96, :] += sums(g, 64)

        return dot, then

    pairs = [(2 * i, s) for i in range(4) for s in range(3)]
    in_turn(
        [strips_two([(y, s), (y + 1, s)]) for y, s in pairs]
        + [strips_two([(8, 0), (8, 1)]), strips_two([(8, 2)])]
    )

    slot(1)
    a_copy(tile, 0).wait()
    a_copy(tile, 1).wait()

    blocks, cots = [], []
    for n in range(5):
        p = 5 * section + n
        rows = [jnp.minimum(2 * p + u, 19) for u in range(4)]
        for q in range(3):
            blocks.append(stack([a1_ref[r, 192 * q : 192 * q + 256, :] for r in rows]))
            cots.append(g2[p + 1, 64 + 192 * q : 256 + 192 * q, :])
    t2_ref[...] += nt_dot(beside(blocks), beside(cots))


    def back_two(i):
        def strip(s):
            def dot():
                cols = [
                    stack([g2[2 * i + k + d, 64 * s : 64 * s + 128, :] for d in range(2)])
                    for k in range(2)
                ]
                return nn_dot(wb2[...], beside(cols))

            def then(v):
                total = jnp.zeros((32, LANES), F32)
                for k in range(2):
                    for b in range(2):
                        row = 4 * i + 2 * k + b
                        slope = s1_ref[row, 64 * s : 64 * s + 64, :].astype(F32)
                        g = v[64 * b : 64 * b + 64, LANES * k : LANES * k + LANES] * slope
                        g1[row + 1, 32 + 64 * s : 96 + 64 * s, :] = g.astype(BF16)
                        total = total + sums(g, 32)
                tb_ref[0:32, :] += total

            return dot, then

        return [strip(s) for s in range(10)]

    in_turn([job for i in range(5) for job in back_two(i)])
    slot(2)

    @pl.when(tile < last_tile)
    def _():
        for k in range(2):
            a_copy(tile + 1, k).start()

    x_copy().wait()

    for first_row in (0, 5):
        blocks, cots = [], []
        for n in range(first_row, first_row + 5):
            for q in range(4):
                blocks.append(stack([xbuf[4 * n + u, 80 * q : 80 * q + 96, :] for u in range(8)]))
                cots.append(g1[10 * section + n + 1, 32 + 160 * q : 192 + 160 * q, :])
        t1_ref[...] += nt_dot(beside(blocks), beside(cots))


    height, width, channels, lane_count = frames_any.shape
    out_pixels = frames_any.reshape(height, width * channels, lane_count)

    def frames_copy(at, part):
        lanes = pl.ds(pl.multiple_of(at * LANES, LANES), LANES)
        rows = pl.ds(28 * part, 28)
        return pltpu.make_async_copy(frames.at[rows], out_pixels.at[rows, :, lanes], frame_sems.at[part])

    def frames_part(part):
        def strips(places):
            def dot():
                cols = [
                    stack([g1[7 * part + a + d, 224 * s : 224 * s + 256, :] for d in range(2)])
                    for a, s in places
                ]
                return nn_dot(wb1[...], beside(cols))

            def then(v):
                for k, (a, s) in enumerate(places):
                    for i in range(4):
                        frames[28 * part + 4 * a + i, 56 * s : 56 * s + 56, :] = v[
                            56 * i : 56 * i + 56, LANES * k : LANES * k + LANES
                        ].astype(BF16)

            return dot, then

        places = [(a, s) for a in range(7) for s in range(3)]
        in_turn([strips(places[k : k + 2]) for k in range(0, len(places), 2)])

    @pl.when(tile == last_tile)
    def _():
        rows = owner_ref.shape[1]
        half_rows = SLICE * owners
        owner_hot = owner_ref[...] == lax.broadcasted_iota(jnp.int32, (owners, rows), 0)
        owner_hot = jnp.where(owner_hot, 1.0, 0.0)
        before = lax.broadcasted_iota(jnp.int32, (rows, rows), 0)
        before = before < lax.broadcasted_iota(jnp.int32, (rows, rows), 1)
        before = nn_dot(owner_hot.astype(BF16), jnp.where(before, 1.0, 0.0).astype(BF16))
        slots = jnp.sum(before * owner_hot, axis=0, keepdims=True)
        slot_ids = lax.broadcasted_iota(jnp.int32, (32, rows), 0)
        slot_ids = slot_ids - capacity * (batch // SLICE)
        slot_hot = jnp.where(slots.astype(jnp.int32) == slot_ids, 1.0, 0.0).astype(BF16)
        outgoing = nt_dot((owner_hot * loss_ref[...]).astype(BF16), slot_hot)
        count = sum2_ref.shape[1] // 2
        for k in range(9):
            u, v = k // 3, k % 3
            pieces = [
                t3_ref[384 * u + 64 * (q + v) : 384 * u + 64 * (q + v) + 64, 64 * q : 64 * q + 64]
                for q in range(4)
            ]
            turned[64 * k : 64 * k + 64, 0:64] = functools.reduce(jnp.add, pieces)
        for k in range(16):
            u, v = k // 4, k % 4
            pieces = [
                t2_ref[256 * u + 32 * (2 * q + v) : 256 * u + 32 * (2 * q + v) + 32, 64 * q : 64 * q + 64]
                for q in range(3)
            ]
            turned[32 * k : 32 * k + 32, 64:128] = functools.reduce(jnp.add, pieces)
        for u in range(8):
            pieces = [
                t1_ref[96 * u + 16 * q : 96 * u + 16 * q + 32, 32 * q : 32 * q + 32] for q in range(5)
            ]
            first[32 * u : 32 * u + 32, 0:32] = functools.reduce(jnp.add, pieces)
        both = jnp.transpose(turned[...])
        ones = jnp.ones((8, LANES), F32)
        bias = lax.dot_general(
            ones, tb_ref[...], NT, precision=lax.Precision.HIGHEST, preferred_element_type=F32
        )
        for h in range(2):
            packed[...] = jnp.zeros_like(packed)
            for k in range(9):
                packed[32 * k : 32 * k + 32, 0:64] = both[32 * h : 32 * h + 32, 64 * k : 64 * k + 64]
            for k in range(16):
                piece = both[64 + 32 * h : 96 + 32 * h, 32 * k : 32 * k + 32]
                stage[pl.ds(k, 32, stride=16), :] = jnp.pad(piece, ((0, 0), (0, 96)))
            packed[0:512, 64:96] = stage[:, 0:32]
            for c in range(4):
                rows_c = first[pl.ds(c, 64, stride=4), :]
                packed[288 : 352, 16 * c : 16 * c + 16] = rows_c[:, 16 * h : 16 * h + 16]
            packed[352 : 353, 0:16] = bias[0:1, 16 * h : 16 * h + 16]
            packed[353 : 354, 0:32] = bias[0:1, 32 + 32 * h : 64 + 32 * h]
            packed[354 : 355, 0:32] = bias[0:1, 96 + 32 * h : 128 + 32 * h]
            packed[355 : 356, 0:1] = jnp.sum(loss_ref[...], axis=1, keepdims=True)
            for k in range(4):
                packed[384 + k : 385 + k, 0:64] = sum1_ref[0:1, 256 * h + 64 * k : 256 * h + 64 * k + 64]
            for k in range(8):
                at = 64 * k
                size = min(64, count - at)
                packed[388 + k : 389 + k, 0:size] = sum2_ref[0:1, count * h + at : count * h + at + size]
            for o in range(owners):
                at = SLICE * ((o % 4) * (owners // 4) + o // 4)
                packed[pl.ds(at + lax.rem(batch, SLICE), 1), 96:128] = outgoing[o : o + 1, :]
            pack[half_rows * h : half_rows * h + half_rows, :] = packed[...].astype(BF16)
        for k in range(1, 8):
            to_near(k).start()

    def after_near():
        total[...] = pack[rows_of(group, block), :].astype(F32)
        for k in range(1, 8):
            to_near(k).wait()
            total[...] += arrived[lax.rem(group + 8 - k, 8)].astype(F32)
        if short:
            crossed[high] = total[...].astype(BF16)
        for k in range(1, high_count):
            to_far(k).start()

    def after_far():
        complete(last_phase - 1)
        for copy in transfers(last_phase):
            copy.start()
        if short:
            for k in range(1, high_count):
                to_far(k).wait()
            ours = crossed[0].astype(F32)
            for k in range(1, high_count):
                ours = ours + crossed[k].astype(F32)
            total[...] = ours
            for k in range(high_count):
                gathered[low * high_count + k] = ours[SLICE * k : SLICE * k + SLICE, :]
            own_ref[...] = total[rows_of(high, SLICE), :]
        else:
            share[...] = total[rows_of(high, SLICE), :]
            for k in range(1, high_count):
                to_far(k).wait()
                share[...] += crossed[lax.rem(high + high_count - k, high_count)]
            for k in range(1, high_count):
                back_far(k).start()
            gathered[place] = share[...]
            own_ref[...] = share[...]
            for k in range(1, high_count):
                back_far(k).wait()
        for k in range(1, 4):
            back_near(k).start()

    def one_part(part, carry):
        @pl.when(tile > 0)
        def _():
            frames_copy(tile - 1, part).wait()

        frames_part(part)
        frames_copy(tile, part).start()

        @pl.when((tile == last_tile) & (part == 0))
        def _():
            after_near()

        @pl.when((tile == last_tile) & (part == 1))
        def _():
            after_far()

        return carry

    lax.fori_loop(0, 3, one_part, 0)

    @pl.when(tile == last_tile)
    def _():
        complete(last_phase)
        dense_copy().start()
        for k in range(1, 4):
            back_near(k).wait()
        sum_ref[...] = gathered[0:16]
        dense_copy().wait()
        for part in range(3):
            frames_copy(tile, part).wait()


def backward(tiles, anys, hg, lg, active, w1, w2, w3, p2, q1, owners, owner_count, capacity, losses, sum1, sum2):
    lanes = hg.shape[-1]
    small = (hg, lg, active, w1, w2, w3, p2, q1, owners, losses, sum1, sum2)
    totals = [(768, 160), (1024, 192), (1152, 256), (160, LANES), (3136, LANES), (512, LANES)]
    totals += [(576, LANES), (256, LANES)]
    pack_shape = (2 * SLICE * owner_count, LANES)
    dense_shape = (2048, 512)
    frames_shape = (84, 84, 2, lanes)
    high_count = owner_count // 4
    copies = 8 + 2 * high_count + 4
    transfers = 4 * (owner_count.bit_length() - 1)
    return pl.pallas_call(
        functools.partial(backward_kernel, capacity),
        grid=(lanes // LANES,),
        in_specs=[pl.BlockSpec((None,) + a.shape[1:], lambda i: (i, 0, 0, 0)) for a in tiles]
        + [pl.BlockSpec(memory_space=pl.ANY)] * len(anys)
        + [whole(a.shape) for a in small],
        out_specs=[pl.BlockSpec(memory_space=pl.ANY)] * 2 + [whole((16, SLICE, LANES)), whole((SLICE, LANES))],
        out_shape=[jax.ShapeDtypeStruct(s, BF16) for s in (frames_shape, dense_shape)]
        + [jax.ShapeDtypeStruct(s, F32) for s in ((16, SLICE, LANES), (SLICE, LANES))],
        scratch_shapes=[pltpu.VMEM(s, F32) for s in totals + [(pack_shape[0] // 2, LANES)]]
        + [
            pltpu.VMEM((128, 256), BF16),
            pltpu.VMEM((192, 960), BF16),
            pltpu.VMEM((11, 11 * 64, LANES), BF16),
            pltpu.VMEM((11, 11 * 64, LANES), BF16),
            pltpu.VMEM((22, 704, LANES), BF16),
            pltpu.VMEM((84, 168, LANES), BF16),
            pltpu.VMEM((224, 512), BF16),
            pltpu.SemaphoreType.DMA((3,)),
            pltpu.SemaphoreType.DMA,
            pltpu.VMEM((20, 640, LANES), BF16),
            pltpu.VMEM((20, 640, LANES), BF16),
            pltpu.VMEM((44, 336, LANES), BF16),
            pltpu.VMEM((1568, lanes), BF16),
            pltpu.VMEM((3136, 512), BF16),
            pltpu.SemaphoreType.DMA,
            pltpu.VMEM(dense_shape, BF16),
            pltpu.VMEM(dense_shape, BF16),
            pltpu.VMEM(dense_shape, BF16),
            pltpu.SemaphoreType.DMA((2,)),
            pltpu.SemaphoreType.DMA,
            pltpu.SemaphoreType.DMA,
            pltpu.SemaphoreType.DMA((transfers,)),
            pltpu.SemaphoreType.DMA((transfers,)),
            pltpu.VMEM(pack_shape, BF16),
            pltpu.VMEM((8, high_count * SLICE, LANES), BF16),
            pltpu.VMEM((high_count * SLICE, LANES), F32),
            pltpu.VMEM((high_count, high_count * SLICE, LANES), BF16)
            if high_count <= 4
            else pltpu.VMEM((high_count, SLICE, LANES), F32),
            pltpu.VMEM((SLICE, LANES), F32),
            pltpu.VMEM((owner_count, SLICE, LANES), F32),
            pltpu.SemaphoreType.DMA((copies,)),
            pltpu.SemaphoreType.DMA((copies,)),
        ],
        compiler_params=pltpu.CompilerParams(
            collective_id=1, has_side_effects=True, vmem_limit_bytes=60 * 1024 * 1024
        ),
        cost_estimate=pl.CostEstimate(
            flops=3 * 7729152 * lanes, bytes_accessed=6 * 28224 * lanes, transcendentals=0
        ),
    )(*tiles, *anys, *small)


def last_kernel(
    owners,
    loss_scale,
    section_ref,
    frames_any,
    dense_any,
    sum_ref,
    own_ref,
    out_any,
    one_ref,
    two_ref,
    k1_ref,
    k2_ref,
    k3_ref,
    o1_ref,
    o2_ref,
    o3_ref,
    d1_ref,
    d2_ref,
    loss_ref,
    table_ref,
    buffer,
    dense_ref,
    dense_sem,
    in_sems,
    out_sems,
):
    step = pl.program_id(0)
    dense_copy = pltpu.make_async_copy(dense_any, dense_ref, dense_sem)
    parts = in_sems.shape[0]
    part_rows = frames_any.shape[0] // parts

    def copy_in(k):
        rows = pl.ds(part_rows * k, part_rows)
        return pltpu.make_async_copy(frames_any.at[rows], buffer.at[rows], in_sems.at[k])

    def copy_out(k):
        rows = pl.ds(part_rows * k, part_rows)
        return pltpu.make_async_copy(buffer.at[rows], out_any.at[rows], out_sems.at[k])

    @pl.when(step == 0)
    def _():
        for k in range(parts):
            copy_in(k).start()
        dense_copy.start()
        if owners == 16:
            mine = own_ref[pl.ds(pl.multiple_of(8 * section_ref[0], 8), 8), :]
            table_ref[0] = 0.5 * mine[:, 96 : 96 + table_ref.shape[2]]
        for c in range(4):
            k1_ref[64 * c : 64 * c + 64, :] = sum_ref[288:352, 16 * c : 16 * c + 16]
        k2_ref[...] = sum_ref[:, 64:96]
        k3_ref[...] = sum_ref[0:288, 0:64]
        o1_ref[...] = 0.5 * sum_ref[352:353, 0:16]
        o2_ref[...] = 0.5 * sum_ref[353:354, 0:32]
        o3_ref[...] = 0.5 * sum_ref[354:355, 0:32]
        loss_ref[...] = loss_scale * sum_ref[355:356, 0:1]
        for k in range(4):
            d1_ref[:, 64 * k : 64 * k + 64] = 0.5 * sum_ref[384 + k : 385 + k, 0:64]
        for k in range(8):
            size = min(64, 459 - 64 * k)
            d2_ref[:, 64 * k : 64 * k + size] = 0.5 * sum_ref[388 + k : 389 + k, 0:size]

        for k in range(parts):
            copy_in(k).wait()
            copy_out(k).start()
        dense_copy.wait()
        two_ref[0:464, :] = dense_ref[1568:2032, 0:256].astype(F32)
        two_ref[464:918, :] = dense_ref[1568:2022, 256:512].astype(F32)

    at = pl.ds(pl.multiple_of(step * 784, 16), 784)
    one_ref[...] = dense_ref[at, :].astype(F32)

    @pl.when(step == pl.num_programs(0) - 1)
    def _():
        for k in range(parts):
            copy_out(k).wait()


def last(owners, capacity, section, frames, dense, sums, own):
    others = [(918, 256), (256, 16), (512, 32), (288, 64), (1, 16), (1, 32), (1, 32), (1, 256), (1, 459), (1, 1), (1, 8, capacity)]
    return pl.pallas_call(
        functools.partial(last_kernel, owners, 0.5 / (frames.shape[3] * owners)),
        grid=(2,),
        in_specs=[
            pl.BlockSpec(memory_space=pltpu.SMEM),
            pl.BlockSpec(memory_space=pl.ANY),
            pl.BlockSpec(memory_space=pl.ANY),
            whole(sums.shape),
            whole(own.shape),
        ],
        out_specs=[pl.BlockSpec(memory_space=pl.ANY), pl.BlockSpec((784, 512), lambda i: (i, 0))]
        + [whole(a) for a in others],
        out_shape=[
            jax.ShapeDtypeStruct(frames.shape, BF16),
            jax.ShapeDtypeStruct((1568, 512), F32),
        ]
        + [jax.ShapeDtypeStruct(a, F32) for a in others],
        scratch_shapes=[
            pltpu.VMEM(frames.shape, BF16),
            pltpu.VMEM(dense.shape, BF16),
            pltpu.SemaphoreType.DMA,
            pltpu.SemaphoreType.DMA((7,)),
            pltpu.SemaphoreType.DMA((7,)),
        ],
        compiler_params=pltpu.CompilerParams(vmem_limit_bytes=60 * 1024 * 1024),
        cost_estimate=pl.CostEstimate(flops=0, bytes_accessed=2**25, transcendentals=0),
    )(section, frames, dense, sums, own)


def shards(
    frames,
    next_frames,
    actions,
    next_actions,
    lengths,
    terminal,
    rewards,
    discounts,
    owners,
    conv_one_weight,
    conv_one_offset,
    conv_two_weight,
    conv_two_offset,
    conv_three_weight,
    conv_three_offset,
    dense_one_weight,
    dense_one_offset,
    dense_two_weight,
    dense_two_offset,
    target_conv_one_weight,
    target_conv_one_offset,
    target_conv_two_weight,
    target_conv_two_offset,
    target_conv_three_weight,
    target_conv_three_offset,
    target_dense_one_weight,
    target_dense_one_offset,
    target_dense_two_weight,
    target_dense_two_offset,
):
    section = lax.axis_index("section")
    owner_count = lax.axis_size("batch")
    rows = frames.shape[0]
    p1, p2, q1 = order_rows(4, 8), order_rows(32, 4), back_one_choice()

    def tower_weights(one, two, three, off_one, off_two, off_three):
        return (
            one.transpose(1, 2, 3, 0).reshape(256, 32),
            two.transpose(1, 2, 3, 0).reshape(512, 64),
            three.transpose(2, 3, 0, 1).reshape(9, 64, 64),
            off_one[None, :],
            off_two[None, :],
            off_three[None, :],
        )

    online = tower_weights(
        conv_one_weight, conv_two_weight, conv_three_weight, conv_one_offset, conv_two_offset, conv_three_offset
    )
    target = tower_weights(
        target_conv_one_weight,
        target_conv_two_weight,
        target_conv_three_weight,
        target_conv_one_offset,
        target_conv_two_offset,
        target_conv_three_offset,
    )
    x = frames.transpose(2, 3, 1, 0)
    x_next = next_frames.transpose(2, 3, 1, 0)
    section_row = section.reshape(1).astype(jnp.int32)
    vectors = [
        a.reshape(a.shape[0] // LANES, LANES)
        for a in (dense_one_offset, target_dense_one_offset, actions, next_actions, lengths, terminal)
    ]
    a1, s1, a2, s2, s3, feature, active, logit_grad, hidden_grad, row_loss, sum1, sum2 = head(
        x,
        x_next,
        dense_one_weight,
        target_dense_one_weight,
        (
            *online,
            *target,
            p1,
            p2,
            dense_two_weight.T,
            target_dense_two_weight.T,
            *vectors,
            dense_two_offset,
            target_dense_two_offset,
            rewards.T,
            discounts.T,
        ),
    )

    capacity = (rows + owner_count - 1) // owner_count + 1
    frames_grad, dense, sums, own = backward(
        (a2, s2, s3),
        (a1, s1, x, feature, dense_one_weight),
        hidden_grad,
        logit_grad,
        active,
        *online[:3],
        p2,
        q1,
        owners.T,
        owner_count,
        capacity,
        row_loss,
        sum1,
        sum2,
    )
    frames_grad, grad_dense_one, grad_dense_two, one, two, three, *rest = last(
        owner_count, capacity, section_row, frames_grad, dense, sums.reshape(16 * SLICE, LANES), own
    )
    off_one, off_two, off_three, dense_off_one, dense_off_two, loss, table = rest
    if owner_count != 16:
        groups = -(-owner_count // SLICE)
        table = 0.5 * own[:, 96 : 96 + groups * capacity].reshape(SLICE, groups, capacity)
        table = table.transpose(1, 0, 2).reshape(groups * SLICE, capacity)
        table = lax.dynamic_slice_in_dim(table, section * (owner_count // 2), owner_count // 2, 0)[None]
    return (
        loss[0, 0],
        frames_grad.transpose(3, 2, 0, 1),
        one.reshape(4, 8, 8, 16).transpose(3, 0, 1, 2),
        off_one[0],
        two.reshape(32, 4, 4, 32).transpose(0, 3, 1, 2),
        off_two[0],
        three.reshape(3, 3, 32, 64).transpose(2, 3, 0, 1),
        off_three[0],
        grad_dense_one,
        dense_off_one[0],
        grad_dense_two.T,
        dense_off_two[0],
        table,
    )


def solution(mesh):
    return jax.shard_map(
        shards,
        mesh=mesh,
        in_specs=(P("batch", None, None, None),) * 2
        + (P("batch"),) * 4
        + (P("batch", None),) * 3
        + (P(),) * 20,
        out_specs=(
            P(),
            P("batch", "section", None, None),
            P("section", None, None, None),
            P("section"),
            P("section", None, None, None),
            P("section"),
            P("section", None, None, None),
            P("section"),
            P("section", None),
            P("section"),
            P("section", None),
            P("section"),
            P("batch", "section", None),
        ),
        check_vma=False,
    )
```

```python
import functools

import jax
import jax.numpy as jnp
import numpy as np
from jax import lax
from jax.experimental import pallas as pl
from jax.experimental.pallas import tpu as pltpu
from jax.sharding import PartitionSpec as P

ACTIONS = 18
ATOMS = 51
NSTEP = 3
LANES = 128
SLICE = 32
ROW_CHUNKS = ((0, 36), (36, 84))
MESH = pl.DeviceIdType.MESH
support_low = -10.0
support_high = 10.0
F32 = jnp.float32
BF16 = jnp.bfloat16
NT = (((1,), (1,)), ((), ()))


def nn_dot(a, b):
    return jnp.dot(a, b, preferred_element_type=F32)


def nt_dot(a, b):
    return lax.dot_general(a, b, NT, preferred_element_type=F32)


def stack(parts):
    return jnp.concatenate(parts, axis=0)


def beside(parts):
    return jnp.concatenate(parts, axis=1)


def eye(size):
    rows = lax.broadcasted_iota(jnp.int32, (size, size), 0)
    cols = lax.broadcasted_iota(jnp.int32, (size, size), 1)
    return jnp.where(rows == cols, 1.0, 0.0).astype(BF16)


def order_rows(channels, extent):
    count = channels * extent * extent
    chosen = np.zeros((count, count), np.float32)
    for c in range(channels):
        for u in range(extent):
            for v in range(extent):
                chosen[(u * extent + v) * channels + c, (c * extent + u) * extent + v] = 1.0
    return jnp.asarray(chosen, BF16)


def back_one_choice():
    chosen = np.zeros((2, 8, 4, 28, 2, 128), np.float32)
    for dp in range(2):
        for dq in range(8):
            for i in range(4):
                for x in range(28):
                    u, v = i + 4 * (1 - dp), x + 4 - 4 * dq
                    if 0 <= v < 8:
                        for ch in range(2):
                            chosen[dp, dq, i, x, ch, ch * 64 + u * 8 + v] = 1.0
    return jnp.asarray(chosen.reshape(16 * 224, 128), BF16)


def lane_bias(row, size):
    return nt_dot(eye(size), jnp.broadcast_to(row, (LANES, size)))


def activate(h):
    t = jnp.tanh(h)
    m = h * t
    return h + m, (1.0 + t) * ((1.0 + h) - m)


def in_turn(jobs):
    waiting = None
    for first, then in jobs:
        value = first()
        if waiting is not None:
            waiting[0](waiting[1])
        waiting = (then, value)
    waiting[0](waiting[1])


def whole(shape):
    return pl.BlockSpec(shape, lambda i, *_: (0,) * len(shape))


def by_lane(shape):
    return pl.BlockSpec(shape[:-1] + (LANES,), lambda i, *_: (0,) * (len(shape) - 1) + (i,))


def lane_column(row):
    size = row.shape[1]
    parts = []
    for at in range(0, size, LANES):
        step = min(LANES, size - at)
        parts.append(lane_bias(row[:, at : at + step], step))
    return stack(parts)


def softmax_terms(v):
    top = jnp.max(v, axis=0, keepdims=True)
    e = jnp.exp(v - top)
    total = jnp.sum(e, axis=0, keepdims=True)
    return e / total, v - top - jnp.log(total)


def head_kernel(
    x_any,
    y_any,
    dense_any,
    target_dense_any,
    w1_ref,
    w2_ref,
    w3_ref,
    o1_ref,
    o2_ref,
    o3_ref,
    v1_ref,
    v2_ref,
    v3_ref,
    q1_ref,
    q2_ref,
    q3_ref,
    p1_ref,
    p2_ref,
    out_ref,
    target_out_ref,
    b1_ref,
    d1_ref,
    action_ref,
    later_action_ref,
    length_ref,
    terminal_ref,
    b2_ref,
    d2_ref,
    rewards_ref,
    discounts_ref,
    a1_any,
    s1_any,
    a2_any,
    s2_any,
    s3_any,
    f_any,
    active_ref,
    lg_ref,
    hg_ref,
    loss_ref,
    sum1_ref,
    sum2_ref,
    wt1,
    wt2,
    wt3,
    wt4,
    c1,
    c2,
    c3,
    c4,
    fs,
    fb,
    xbuf,
    a1,
    s1,
    a2,
    s2,
    s3,
    wd,
    wdt,
    pre,
    hidden,
    late,
    back,
    logits,
    logits_later,
    lgs,
    probs,
    position,
    x_sems,
    out_sems,
    wd_sem,
    sent,
    came,
):
    section, batch = lax.axis_index("section"), lax.axis_index("batch")
    step, steps = pl.program_id(0), pl.num_programs(0)
    lanes = hidden.shape[1]
    tiles = lanes // LANES
    targets = tiles - 1
    online = step >= targets
    slot = lax.rem(step, 2)
    height, width, stacked, _ = x_any.shape

    def lanes_of(index):
        return pl.ds(pl.multiple_of(index * LANES, LANES), LANES)

    def x_copy(source, tile, at, k):
        place = lax.rem(at, 2)
        first, last = ROW_CHUNKS[k]
        pixels = source.reshape(height, width * stacked, lanes)
        return pltpu.make_async_copy(
            pixels.at[first:last, :, lanes_of(tile)], xbuf.at[place, first:last], x_sems.at[place, k]
        )

    def start_x(at):
        @pl.when(at < targets)
        def _():
            for k in range(len(ROW_CHUNKS)):
                x_copy(y_any, jnp.minimum(at, targets - 1) + section, at, k).start()

        @pl.when((at >= targets) & (at < steps))
        def _():
            for k in range(len(ROW_CHUNKS)):
                x_copy(x_any, jnp.clip(at - targets, 0, tiles - 1), at, k).start()

    tile = jnp.maximum(step - targets, 0)
    outs = ((a1, a1_any), (s1, s1_any), (a2, a2_any), (s2, s2_any), (s3, s3_any), (fb, f_any))

    def out_copy(k, at):
        source, into = outs[k]
        place = into.at[:, lanes_of(at)] if k == 5 else into.at[at]
        return pltpu.make_async_copy(source, place, out_sems.at[k])

    def wait_outs(which):
        @pl.when(step > targets)
        def _():
            for k in which:
                out_copy(k, jnp.maximum(tile - 1, 0)).wait()

    def start_outs(which):
        @pl.when(online)
        def _():
            for k in which:
                out_copy(k, tile).start()

    def swap():
        return pltpu.make_async_remote_copy(
            src_ref=late.at[:, lanes_of((tiles - 1) * section)],
            dst_ref=late.at[:, lanes_of((tiles - 1) * section)],
            send_sem=sent,
            recv_sem=came,
            device_id=(1 - section, batch),
            device_id_type=MESH,
        )

    def dense_copy(source):
        return pltpu.make_async_copy(source, wd, wd_sem)

    @pl.when(step == 0)
    def _():
        barrier = pltpu.get_barrier_semaphore()
        pl.semaphore_signal(barrier, inc=1, device_id=(1 - section, batch), device_id_type=MESH)
        start_x(step)

    def prepare(one_ref, two_ref, three_ref, off_one, off_two, off_three):
        wt1[...] = jnp.zeros_like(wt1)
        wt2[...] = jnp.zeros_like(wt2)
        wt3[...] = jnp.zeros_like(wt3)
        base = nt_dot(eye(32), nn_dot(p1_ref[...], one_ref[...]).astype(BF16))
        base = (0.5 * base).astype(BF16)
        for t in range(5):
            for u in range(8):
                wt1[32 * t : 32 * t + 32, 96 * u + 16 * t : 96 * u + 16 * t + 32] = base[:, 32 * u : 32 * u + 32]
        base = nt_dot(eye(64), nn_dot(p2_ref[...], two_ref[...]).astype(BF16))
        base = (0.5 * base).astype(BF16)
        for t in range(3):
            for u in range(4):
                wt2[64 * t : 64 * t + 64, 256 * u + 64 * t : 256 * u + 64 * t + 128] = base[:, 128 * u : 128 * u + 128]
        for u in range(3):
            for v in range(3):
                piece = (0.5 * three_ref[3 * u + v].astype(F32)).astype(BF16)
                wt4[:, 192 * u + 64 * v : 192 * u + 64 * v + 64] = piece
                for t in range(2):
                    at = 256 * u + 64 * t + 64 * v
                    wt3[64 * t : 64 * t + 64, at : at + 64] = piece
        c1[...] = stack([0.5 * lane_bias(off_one[...], 32)] * 5)
        c2[...] = stack([0.5 * lane_bias(off_two[...], 64)] * 3)
        column = 0.5 * lane_bias(off_three[...], 64)
        c3[...] = stack([column] * 2)
        c4[...] = column

    @pl.when(step == 0)
    def _():
        prepare(v1_ref, v2_ref, v3_ref, q1_ref, q2_ref, q3_ref)

    @pl.when(step == targets)
    def _():
        prepare(w1_ref, w2_ref, w3_ref, o1_ref, o2_ref, o3_ref)

    def put(bias, act, slope, places):
        def then(value):
            for k, (row, at, size) in enumerate(places):
                a, s = activate(value[:, LANES * k : LANES * k + LANES] + bias[...])
                act[row, at : at + size, :] = a.astype(BF16)
                slope[row, at : at + size, :] = s.astype(BF16)

        return then

    def strips_one(i, s):
        def dot():
            cols = [
                stack([xbuf[slot, 8 * i + 4 * k + u, 80 * s : 80 * s + 96, :] for u in range(8)])
                for k in range(2)
            ]
            return nn_dot(wt1[...], beside(cols))

        return dot, put(c1, a1, s1, [(2 * i + k, 160 * s, 160) for k in range(2)])

    wait_outs((0, 1))
    for k, pairs in enumerate((range(0, 4), range(4, 10))):
        x_copy(x_any, tile, step, k).wait()
        in_turn([strips_one(i, s) for i in pairs for s in range(4)])
    start_outs((0, 1))
    start_x(step + 1)

    @pl.when(step == 0)
    def _():
        dense_copy(target_dense_any).start()

    wait_outs((2, 3, 4, 5))

    def strips_two(places):
        def dot():
            cols = [
                stack([a1[2 * p + u, 192 * s : 192 * s + 256, :] for u in range(4)])
                for p, s in places
            ]
            return nn_dot(wt2[...], beside(cols))

        return dot, put(c2, a2, s2, [(p, 192 * s, 192) for p, s in places])

    def strips_three(places, weight, bias, count):
        def dot():
            cols = [
                stack([a2[p + u, 64 * q : 64 * q + 64 * count + 128, :] for u in range(3)])
                for p, q in places
            ]
            return nn_dot(weight[...], beside(cols))

        def then(value):
            for k, (p, q) in enumerate(places):
                a, s = activate(value[:, LANES * k : LANES * k + LANES] + bias[...])
                for t in range(count):
                    fs[pl.ds(7 * p + q + t, 64, stride=49), :] = a[64 * t : 64 * t + 64, :]
                s3[p, 64 * q : 64 * q + 64 * count, :] = s.astype(BF16)

        return dot, then

    two = [(2 * i + k, s) for i in range(4) for s in range(3) for k in range(2)]
    two += [(8, s) for s in range(3)]
    three = [(p, q) for p in range(7) for q in (0, 2, 4)]
    ends = [(p, 6) for p in range(7)]
    in_turn(
        [strips_two(two[k : k + 2]) for k in range(0, len(two), 2)]
        + [strips_three(three[k : k + 2], wt3, c3, 2) for k in range(0, len(three), 2)]
        + [strips_three(ends[k : k + 2], wt4, c4, 1) for k in range(0, len(ends), 2)]
    )
    fb[...] = fs[...].astype(BF16)
    start_outs((2, 3, 4, 5))

    def turn(source):
        dense_copy(source).wait()
        unit = eye(512)
        for at in range(0, wd.shape[0], 256):
            size = min(256, wd.shape[0] - at)
            wdt[:, at : at + size] = nt_dot(unit, wd[at : at + size, :]).astype(BF16)

    @pl.when(step == 0)
    def _():
        turn(target_dense_any)
        dense_copy(dense_any).start()

    @pl.when(step == targets)
    def _():
        turn(dense_any)

    def column(rows_ref):
        return stack([lane_bias(rows_ref[k : k + 1, :], LANES) for k in range(rows_ref.shape[0])])

    pre[...] = nn_dot(wdt[...], fb[...])

    @pl.when(step < targets)
    def _():
        later, _ = activate(0.5 * (pre[...] + column(d1_ref)))
        late[:, lanes_of(jnp.minimum(step, targets - 1) + section)] = later.astype(BF16)

    @pl.when(step == targets - 1)
    def _():
        pl.semaphore_wait(pltpu.get_barrier_semaphore(), 1)
        swap().start()

    @pl.when(online)
    def _():
        hidden[:, lanes_of(tile)] = pre[...] + column(b1_ref)

    @pl.when(step == steps - 1)
    def _():
        count = out_ref.shape[0]
        back[...] = jnp.zeros_like(back)
        lgs[...] = jnp.zeros_like(lgs)
        for at in range(0, count, 256):
            size = min(256, count - at)
            back[:, at : at + size] = nt_dot(eye(512), out_ref[at : at + size, :]).astype(BF16)

        def wide(ref):
            return beside([lane_column(ref[...].reshape(1, count))] * tiles)

        active, slope = activate(0.5 * hidden[...])
        active = active.astype(BF16)
        active_ref[...] = active
        logits[...] = nn_dot(out_ref[...], active) + wide(b2_ref)
        swap().wait()
        logits_later[...] = nn_dot(target_out_ref[...], late[...]) + wide(d2_ref)

        def row(ref):
            return beside([ref[k : k + 1, :] for k in range(tiles)])

        action, later_action = row(action_ref), row(later_action_ref)
        length, terminal = row(length_ref), row(terminal_ref)

        def pick(ref, ids):
            total = jnp.zeros((ATOMS, lanes), F32)
            for a in range(ACTIONS):
                total = total + jnp.where(ids == a, ref[ATOMS * a : ATOMS * a + ATOMS, :], 0.0)
            return total

        soft, log_soft = softmax_terms(pick(logits, action))
        returns = jnp.zeros((1, lanes), F32)
        bootstrap = jnp.zeros((1, lanes), F32)
        product = jnp.ones((1, lanes), F32)
        for k in range(NSTEP):
            returns = returns + jnp.where(length > k, product * rewards_ref[k : k + 1, :], 0.0)
            product = product * discounts_ref[k : k + 1, :]
            bootstrap = bootstrap + jnp.where(length == k + 1, product, 0.0)
        bootstrap = bootstrap * (1.0 - terminal.astype(F32))
        spacing = (support_high - support_low) / (ATOMS - 1)
        ids = lax.broadcasted_iota(jnp.int32, (ATOMS, lanes), 0).astype(F32)
        shifted = jnp.clip(returns + bootstrap * (support_low + spacing * ids), support_low, support_high)
        position[...] = (shifted - support_low) / spacing
        probs[...], _ = softmax_terms(pick(logits_later, later_action))
        mass = jnp.zeros((ATOMS, lanes), F32)
        for j in range(ATOMS):
            weight = jnp.maximum(0.0, 1.0 - jnp.abs(position[j : j + 1, :] - ids))
            mass = mass + probs[j : j + 1, :] * weight
        loss_ref[...] = -jnp.sum(mass * log_soft, axis=0, keepdims=True)
        chosen_grad = jnp.sum(mass, axis=0, keepdims=True) * soft - mass
        for a in range(ACTIONS):
            lgs[ATOMS * a : ATOMS * a + ATOMS, :] = jnp.where(action == a, chosen_grad, 0.0)
        lg = lgs[...].astype(BF16)
        lg_ref[...] = lg[0:count]
        hg = (nn_dot(back[...], lg) * (0.5 * slope)).astype(BF16)
        hg_ref[...] = hg
        ones = jnp.ones((8, lanes), BF16)
        sum1_ref[...] = nt_dot(ones, hg)
        sum2_ref[...] = nt_dot(ones, lg[0:count])
        for k in range(len(outs)):
            out_copy(k, tile).wait()


def head(x, y, dense_one, target_dense_one, small):
    lanes = x.shape[3]
    count = small[14].shape[0]
    tiles = lanes // LANES
    outs = [(20, 640), (20, 640), (9, 576), (9, 576), (7, 448)]
    outs = [(tiles,) + shape + (LANES,) for shape in outs] + [(3136, lanes)]
    rest = [((512, lanes), BF16), ((count, lanes), BF16), ((512, lanes), BF16), ((1, lanes), F32)]
    rest += [((8, 512), F32), ((8, count), F32)]
    anywhere = pl.BlockSpec(memory_space=pl.ANY)
    buffers = [
        ((160, 768), BF16),
        ((192, 1024), BF16),
        ((128, 768), BF16),
        ((64, 576), BF16),
        ((160, LANES), F32),
        ((192, LANES), F32),
        ((128, LANES), F32),
        ((64, LANES), F32),
        ((3136, LANES), F32),
        ((3136, LANES), BF16),
        ((2, 84, 336, LANES), BF16),
        ((20, 640, LANES), BF16),
        ((20, 640, LANES), BF16),
        ((9, 576, LANES), BF16),
        ((9, 576, LANES), BF16),
        ((7, 448, LANES), BF16),
        ((3136, 512), BF16),
        ((512, 3136), BF16),
        ((512, LANES), F32),
        ((512, lanes), F32),
        ((512, lanes), BF16),
        ((512, 1024), BF16),
        ((count, lanes), F32),
        ((count, lanes), F32),
        ((1024, lanes), F32),
        ((ATOMS, lanes), F32),
        ((ATOMS, lanes), F32),
    ]
    return pl.pallas_call(
        head_kernel,
        grid=(2 * (lanes // LANES) - 1,),
        in_specs=[anywhere] * 4 + [whole(a.shape) for a in small],
        out_specs=[anywhere] * len(outs) + [whole(s) for s, _ in rest],
        out_shape=[jax.ShapeDtypeStruct(s, BF16) for s in outs]
        + [jax.ShapeDtypeStruct(s, t) for s, t in rest],
        scratch_shapes=[pltpu.VMEM(s, t) for s, t in buffers]
        + [
            pltpu.SemaphoreType.DMA((2, len(ROW_CHUNKS))),
            pltpu.SemaphoreType.DMA((len(outs),)),
            pltpu.SemaphoreType.DMA,
            pltpu.SemaphoreType.DMA,
            pltpu.SemaphoreType.DMA,
        ],
        compiler_params=pltpu.CompilerParams(
            collective_id=0, has_side_effects=True, vmem_limit_bytes=60 * 1024 * 1024
        ),
        cost_estimate=pl.CostEstimate(
            flops=5 * 2 * 9785600 * LANES, bytes_accessed=2**26, transcendentals=0
        ),
    )(x, y, dense_one, target_dense_one, *small)


def backward_kernel(
    capacity,
    a2_ref,
    s2_ref,
    s3_ref,
    a1_any,
    s1_any,
    x_any,
    f_any,
    dense_weight_any,
    p2_any,
    q1_any,
    hg_ref,
    lg_ref,
    active_ref,
    w1_ref,
    w2_ref,
    w3_ref,
    owner_ref,
    loss_ref,
    sum1_ref,
    sum2_ref,
    frames_any,
    dense_any,
    sum_ref,
    own_ref,
    t1_ref,
    t2_ref,
    t3_ref,
    tb_ref,
    fcs,
    stage,
    turned,
    first,
    packed,
    wb2,
    wb3,
    g2,
    g3,
    g1,
    frames,
    wb1,
    frame_sems,
    dense_sem,
    a1_ref,
    s1_ref,
    p2_ref,
    q1_ref,
    choice_sems,
    xbuf,
    fbuf,
    dense_weight_ref,
    weight_sem,
    slab,
    landed,
    shared,
    a_sems,
    x_sem,
    f_sem,
    sent,
    came,
    pack,
    arrived,
    total,
    crossed,
    share,
    gathered,
    left,
    reached,
):
    section, batch = lax.axis_index("section"), lax.axis_index("batch")
    owners = lax.axis_size("batch")
    bits = owners.bit_length() - 1
    tile = pl.program_id(0)
    last_tile = pl.num_programs(0) - 1

    dense_rows = slab.shape[0]
    bit = [lax.rem(batch // (1 << k), 2) for k in range(bits)]
    colours = 2 if bits < 7 else 1
    region = dense_rows // (2 * colours)
    orders = [list(range(1, bits)) for _ in range(colours)]
    orders[-1] = orders[-1][(bits - 1) // 2 :] + orders[-1][: (bits - 1) // 2]
    base = (dense_rows // 2) * bit[0]
    bases = []
    for c in range(colours):
        starts = [base + c * region]
        for m, k in enumerate(orders[c]):
            starts.append(starts[-1] + (region >> (m + 1)) * bit[k])
        bases.append(starts)

    def rows_at(start, size):
        return pl.ds(pl.multiple_of(start, 16), size)

    def moves(phase):
        if phase in (0, 2 * bits - 1):
            half = dense_rows // 2
            if phase:
                return [(0, base, half, None, None)]
            return [(0, half * (1 - bit[0]), half, 0, base)]
        found = []
        for c in range(colours):
            m = phase - 1 if phase < bits else 2 * bits - 2 - phase
            size = region >> (m + 1)
            k, start = orders[c][m], bases[c][m]
            if phase < bits:
                place = dense_rows // 2 + (c + 1) * region - 2 * size
                found.append((k, start + size * (1 - bit[k]), size, place, bases[c][m + 1]))
            else:
                found.append((k, bases[c][m + 1], size, None, None))
        return found

    def transfers(phase):
        copies = []
        for c, (k, start, size, place, _) in enumerate(moves(phase)):
            if phase < bits:
                source, into = slab.at[rows_at(start, size), :], landed.at[pl.ds(place, size), :]
            else:
                source = into = shared.at[rows_at(start, size), :]
            copies.append(
                pltpu.make_async_remote_copy(
                    src_ref=source,
                    dst_ref=into,
                    send_sem=sent.at[2 * phase + c],
                    recv_sem=came.at[2 * phase + c],
                    device_id=(section, batch + (1 << k) * (1 - 2 * bit[k])),
                    device_id_type=MESH,
                )
            )
        return copies

    def complete(phase):
        for copy, (_, _, size, place, to) in zip(transfers(phase), moves(phase)):
            copy.wait()
            if phase < bits:
                step = min(size, 64)

                def add(n, carry, step=step, place=place, to=to):
                    at = rows_at(to + step * n, step)
                    more = landed[pl.ds(pl.multiple_of(place + step * n, 16), step), :]
                    slab[at, :] = (slab[at, :].astype(F32) + more.astype(F32)).astype(BF16)
                    return carry

                lax.fori_loop(0, size // step, add, 0)
        if phase == bits - 1:
            for c in range(colours):
                own = rows_at(bases[c][-1], region >> (bits - 1))
                shared[own, :] = slab[own, :]

    starts = [0, 1, 2, 3, 5, 6, 8]
    if bits != 4:
        starts = [9 * phase // (2 * bits - 1) for phase in range(2 * bits - 1)]
    last_phase = 2 * bits - 1

    def slot(index):
        for phase, at in enumerate(starts):
            if phase > 0 and at % 3 == index:

                @pl.when(tile == at // 3)
                def _(phase=phase):
                    complete(phase - 1)
                    for copy in transfers(phase):
                        copy.start()

    high_count = owners // 4
    block = high_count * SLICE
    low, high = lax.rem(batch, 4), batch // 4
    group = section * 4 + low
    place = low * high_count + high

    def near(k):
        index = lax.rem(group + k, 8)
        return index, (index // 4, high * 4 + lax.rem(index, 4))

    def far(k):
        index = lax.rem(high + k, high_count)
        return index, (section, index * 4 + low)

    def send(source, into, device, number):
        return pltpu.make_async_remote_copy(
            src_ref=source,
            dst_ref=into,
            send_sem=left.at[number],
            recv_sem=reached.at[number],
            device_id=device,
            device_id_type=MESH,
        )

    def rows_of(index, size):
        return pl.ds(pl.multiple_of(index * size, size), size)

    def to_near(k):
        index, device = near(k)
        return send(pack.at[rows_of(index, block), :], arrived.at[group], device, k)

    short = high_count <= 4

    def to_far(k):
        index, device = far(k)
        source = crossed.at[high] if short else total.at[rows_of(index, SLICE), :]
        return send(source, crossed.at[high], device, 8 + k)

    def back_far(k):
        return send(share, gathered.at[place], far(k)[1], 8 + high_count + k)

    def back_near(k):
        ours = gathered.at[pl.ds(low * high_count, high_count)]
        device = (section, high * 4 + lax.rem(low + k, 4))
        return send(ours, ours, device, 8 + 2 * high_count + k)

    def a_copy(at, k):
        source, into = ((a1_any, a1_ref), (s1_any, s1_ref))[k]
        return pltpu.make_async_copy(source.at[at], into, a_sems.at[k])

    def dense_copy():
        return pltpu.make_async_copy(shared, dense_any, dense_sem)

    height, width, stacked, lane_count = x_any.shape
    pixels = x_any.reshape(height, width * stacked, lane_count)

    def x_copy():
        return pltpu.make_async_copy(
            pixels.at[pl.ds(40 * section, 44), :, pl.ds(pl.multiple_of(tile * LANES, LANES), LANES)],
            xbuf,
            x_sem,
        )

    def f_copy():
        half = fbuf.shape[0]
        return pltpu.make_async_copy(f_any.at[rows_at(half * section, half), :], fbuf, f_sem)

    def choice_copy(k):
        source, into = ((p2_any, p2_ref), (q1_any, q1_ref))[k]
        return pltpu.make_async_copy(source, into, choice_sems.at[k])

    def weight_copy():
        return pltpu.make_async_copy(dense_weight_any, dense_weight_ref, weight_sem)

    @pl.when(tile == 0)
    def _():
        f_copy().start()
        barrier = pltpu.get_barrier_semaphore()
        for k in range(1, 8):
            pl.semaphore_signal(barrier, inc=1, device_id=near(k)[1], device_id_type=MESH)
        for k in range(1, high_count):
            pl.semaphore_signal(barrier, inc=1, device_id=far(k)[1], device_id_type=MESH)
        f_copy().wait()
        for k in range(2):
            choice_copy(k).start()
        weight_copy().start()
        for k in range(2):
            a_copy(tile, k).start()

        def dense_one(start, stop):
            for at in range(start, stop, 256):
                rows = slice(at, min(at + 256, stop))
                slab[rows, :] = nt_dot(fbuf[rows, :], hg_ref[...]).astype(BF16)

        def upper_half():
            slab[1568:dense_rows, :] = jnp.zeros((dense_rows - 1568, 512), BF16)
            mine = active_ref[pl.ds(pl.multiple_of(256 * section, 256), 256), :]
            slab[1568:2032, 0:256] = nt_dot(lg_ref[0:464, :], mine).astype(BF16)
            slab[1568:2022, 256:512] = nt_dot(lg_ref[464:918, :], mine).astype(BF16)
            dense_one(1024, 1568)

        @pl.when(bit[0] == 0)
        def _():
            upper_half()

        @pl.when(bit[0] == 1)
        def _():
            dense_one(0, 1024)

        pl.semaphore_wait(barrier, 6 + high_count)
        for copy in transfers(0):
            copy.start()

        @pl.when(bit[0] == 0)
        def _():
            dense_one(0, 1024)

        @pl.when(bit[0] == 1)
        def _():
            upper_half()

        for ref in (t1_ref, t2_ref, t3_ref, tb_ref, wb1, wb2, wb3):
            ref[...] = jnp.zeros_like(ref)
        for ref, edge, width in ((g1, 1, 32), (g2, 1, 64), (g3, 2, 64)):
            side = jnp.zeros((edge * width, LANES), BF16)
            for r in range(ref.shape[0]):
                if edge <= r < ref.shape[0] - edge:
                    ref[r, 0 : edge * width, :] = side
                    ref[r, ref.shape[1] - edge * width :, :] = side
                else:
                    ref[r] = jnp.zeros((ref.shape[1], LANES), BF16)
        for k in range(2):
            choice_copy(k).wait()
        rows = (0.5 * nn_dot(p2_ref[...], w2_ref[...])).astype(BF16)
        for dp in range(2):
            for dq in range(2):
                for b in range(2):
                    for x in range(2):
                        u, v = b + 2 * (1 - dp), x + 2 * (1 - dq)
                        to, at, of = 32 * (2 * b + x), 64 * (2 * dp + dq), 32 * (4 * u + v)
                        wb2[to : to + 32, at : at + 64] = rows[of : of + 32, :]
        for u in range(3):
            for v in range(3):
                piece = (0.5 * nt_dot(eye(64), w3_ref[3 * u + v])).astype(BF16)
                for t in range(3):
                    at = 320 * (2 - u) + 64 * (t + 2 - v)
                    wb3[64 * t : 64 * t + 64, at : at + 64] = piece
        half = w1_ref[pl.ds(pl.multiple_of(section * 128, 128), 128), :]
        pieces = nn_dot(q1_ref[...], half).astype(BF16)
        for k in range(16):
            wb1[:, 32 * k : 32 * k + 32] = pieces[224 * k : 224 * k + 224, :]
        weight_copy().wait()

    slot(0)
    x_copy().start()

    def sums(value, size):
        total = value[0:size]
        for at in range(size, value.shape[0], size):
            total = total + value[at : at + size]
        return total

    hg = hg_ref[:, pl.ds(pl.multiple_of(tile * LANES, LANES), LANES)]

    def feature_grad(n, carry):
        at = pl.ds(pl.multiple_of(448 * n, 448), 448)
        fcs[at, :] = 0.5 * nn_dot(dense_weight_ref[at, :], hg).astype(BF16).astype(F32)
        return carry

    lax.fori_loop(0, 7, feature_grad, 0, unroll=True)

    def cot_three(p, carry):
        cot = stack([fcs[pl.ds(7 * p + q, 64, stride=49), :] for q in range(7)])
        g = cot * s3_ref[p].astype(F32)
        g3[p + 2, 128:576, :] = g.astype(BF16)
        tb_ref[96:160, :] += sums(g, 64)
        return carry

    lax.fori_loop(0, 7, cot_three, 0, unroll=True)

    blocks, cots = [], []
    nothing = jnp.zeros((64, LANES), BF16)
    for n in range(4):
        p = 4 * section + n
        rows = [jnp.minimum(p + u, 8) for u in range(3)]
        blocks.append(stack([a2_ref[r, 0:384, :] for r in rows]))
        blocks.append(stack([part for r in rows for part in (a2_ref[r, 256:576, :], nothing)]))
        cots += [g3[p + 2, 128:384, :], g3[p + 2, 384:640, :]]
    t3_ref[...] += nt_dot(beside(blocks), beside(cots))


    def patch_three(y, s):
        return stack([g3[y + d, 192 * s : 192 * s + 320, :] for d in range(3)])

    def strips_two(places):
        def dot():
            return nn_dot(wb3[...], beside([patch_three(y, s) for y, s in places]))

        def then(value):
            for k, (y, s) in enumerate(places):
                slope = s2_ref[y, 192 * s : 192 * s + 192, :].astype(F32)
                g = value[:, LANES * k : LANES * k + LANES] * slope
                g2[y + 1, 64 + 192 * s : 256 + 192 * s, :] = g.astype(BF16)
                tb_ref[32:96, :] += sums(g, 64)

        return dot, then

    pairs = [(2 * i, s) for i in range(4) for s in range(3)]
    in_turn(
        [strips_two([(y, s), (y + 1, s)]) for y, s in pairs]
        + [strips_two([(8, 0), (8, 1)]), strips_two([(8, 2)])]
    )

    slot(1)
    a_copy(tile, 0).wait()
    a_copy(tile, 1).wait()

    blocks, cots = [], []
    for n in range(5):
        p = 5 * section + n
        rows = [jnp.minimum(2 * p + u, 19) for u in range(4)]
        for q in range(3):
            blocks.append(stack([a1_ref[r, 192 * q : 192 * q + 256, :] for r in rows]))
            cots.append(g2[p + 1, 64 + 192 * q : 256 + 192 * q, :])
    t2_ref[...] += nt_dot(beside(blocks), beside(cots))


    def back_two(i):
        def strip(s):
            def dot():
                cols = [
                    stack([g2[2 * i + k + d, 64 * s : 64 * s + 128, :] for d in range(2)])
                    for k in range(2)
                ]
                return nn_dot(wb2[...], beside(cols))

            def then(v):
                total = jnp.zeros((32, LANES), F32)
                for k in range(2):
                    for b in range(2):
                        row = 4 * i + 2 * k + b
                        slope = s1_ref[row, 64 * s : 64 * s + 64, :].astype(F32)
                        g = v[64 * b : 64 * b + 64, LANES * k : LANES * k + LANES] * slope
                        g1[row + 1, 32 + 64 * s : 96 + 64 * s, :] = g.astype(BF16)
                        total = total + sums(g, 32)
                tb_ref[0:32, :] += total

            return dot, then

        return [strip(s) for s in range(10)]

    in_turn([job for i in range(5) for job in back_two(i)])
    slot(2)

    @pl.when(tile < last_tile)
    def _():
        for k in range(2):
            a_copy(tile + 1, k).start()

    x_copy().wait()

    for first_row in (0, 5):
        blocks, cots = [], []
        for n in range(first_row, first_row + 5):
            for q in range(4):
                blocks.append(stack([xbuf[4 * n + u, 80 * q : 80 * q + 96, :] for u in range(8)]))
                cots.append(g1[10 * section + n + 1, 32 + 160 * q : 192 + 160 * q, :])
        t1_ref[...] += nt_dot(beside(blocks), beside(cots))


    height, width, channels, lane_count = frames_any.shape
    out_pixels = frames_any.reshape(height, width * channels, lane_count)

    def frames_copy(at, part):
        lanes = pl.ds(pl.multiple_of(at * LANES, LANES), LANES)
        rows = pl.ds(28 * part, 28)
        return pltpu.make_async_copy(frames.at[rows], out_pixels.at[rows, :, lanes], frame_sems.at[part])

    def frames_part(part):
        def strips(places):
            def dot():
                cols = [
                    stack([g1[7 * part + a + d, 224 * s : 224 * s + 256, :] for d in range(2)])
                    for a, s in places
                ]
                return nn_dot(wb1[...], beside(cols))

            def then(v):
                for k, (a, s) in enumerate(places):
                    for i in range(4):
                        frames[28 * part + 4 * a + i, 56 * s : 56 * s + 56, :] = v[
                            56 * i : 56 * i + 56, LANES * k : LANES * k + LANES
                        ].astype(BF16)

            return dot, then

        places = [(a, s) for a in range(7) for s in range(3)]
        in_turn([strips(places[k : k + 2]) for k in range(0, len(places), 2)])

    @pl.when(tile < last_tile)
    def _():
        def one_part(part, carry):
            @pl.when(tile > 0)
            def _():
                frames_copy(tile - 1, part).wait()

            frames_part(part)
            frames_copy(tile, part).start()
            return carry

        lax.fori_loop(0, 3, one_part, 0)

    def last_part(part):
        frames_copy(tile - 1, part).wait()
        frames_part(part)
        frames_copy(tile, part).start()

    @pl.when(tile == last_tile)
    def _():
        rows = owner_ref.shape[1]
        half_rows = SLICE * owners
        owner_hot = owner_ref[...] == lax.broadcasted_iota(jnp.int32, (owners, rows), 0)
        owner_hot = jnp.where(owner_hot, 1.0, 0.0)
        before = lax.broadcasted_iota(jnp.int32, (rows, rows), 0)
        before = before < lax.broadcasted_iota(jnp.int32, (rows, rows), 1)
        before = nn_dot(owner_hot.astype(BF16), jnp.where(before, 1.0, 0.0).astype(BF16))
        slots = jnp.sum(before * owner_hot, axis=0, keepdims=True)
        slot_ids = lax.broadcasted_iota(jnp.int32, (32, rows), 0)
        slot_ids = slot_ids - capacity * (batch // SLICE)
        slot_hot = jnp.where(slots.astype(jnp.int32) == slot_ids, 1.0, 0.0).astype(BF16)
        outgoing = nt_dot((owner_hot * loss_ref[...]).astype(BF16), slot_hot)
        count = sum2_ref.shape[1] // 2
        for k in range(9):
            u, v = k // 3, k % 3
            pieces = [
                t3_ref[384 * u + 64 * (q + v) : 384 * u + 64 * (q + v) + 64, 64 * q : 64 * q + 64]
                for q in range(4)
            ]
            turned[64 * k : 64 * k + 64, 0:64] = functools.reduce(jnp.add, pieces)
        for k in range(16):
            u, v = k // 4, k % 4
            pieces = [
                t2_ref[256 * u + 32 * (2 * q + v) : 256 * u + 32 * (2 * q + v) + 32, 64 * q : 64 * q + 64]
                for q in range(3)
            ]
            turned[32 * k : 32 * k + 32, 64:128] = functools.reduce(jnp.add, pieces)
        for u in range(8):
            pieces = [
                t1_ref[96 * u + 16 * q : 96 * u + 16 * q + 32, 32 * q : 32 * q + 32] for q in range(5)
            ]
            first[32 * u : 32 * u + 32, 0:32] = functools.reduce(jnp.add, pieces)
        both = jnp.transpose(turned[...])
        ones = jnp.ones((8, LANES), F32)
        bias = lax.dot_general(
            ones, tb_ref[...], NT, precision=lax.Precision.HIGHEST, preferred_element_type=F32
        )
        for h in range(2):
            packed[...] = jnp.zeros_like(packed)
            for k in range(9):
                packed[32 * k : 32 * k + 32, 0:64] = both[32 * h : 32 * h + 32, 64 * k : 64 * k + 64]
            for k in range(16):
                piece = both[64 + 32 * h : 96 + 32 * h, 32 * k : 32 * k + 32]
                stage[pl.ds(k, 32, stride=16), :] = jnp.pad(piece, ((0, 0), (0, 96)))
            packed[0:512, 64:96] = stage[:, 0:32]
            for c in range(4):
                rows_c = first[pl.ds(c, 64, stride=4), :]
                packed[288 : 352, 16 * c : 16 * c + 16] = rows_c[:, 16 * h : 16 * h + 16]
            packed[352 : 353, 0:16] = bias[0:1, 16 * h : 16 * h + 16]
            packed[353 : 354, 0:32] = bias[0:1, 32 + 32 * h : 64 + 32 * h]
            packed[354 : 355, 0:32] = bias[0:1, 96 + 32 * h : 128 + 32 * h]
            packed[355 : 356, 0:1] = jnp.sum(loss_ref[...], axis=1, keepdims=True)
            for k in range(4):
                packed[384 + k : 385 + k, 0:64] = sum1_ref[0:1, 256 * h + 64 * k : 256 * h + 64 * k + 64]
            for k in range(8):
                at = 64 * k
                size = min(64, count - at)
                packed[388 + k : 389 + k, 0:size] = sum2_ref[0:1, count * h + at : count * h + at + size]
            for o in range(owners):
                at = SLICE * ((o % 4) * (owners // 4) + o // 4)
                packed[pl.ds(at + lax.rem(batch, SLICE), 1), 96:128] = outgoing[o : o + 1, :]
            pack[half_rows * h : half_rows * h + half_rows, :] = packed[...].astype(BF16)
        for k in range(1, 8):
            to_near(k).start()
        last_part(0)
        total[...] = pack[rows_of(group, block), :].astype(F32)
        for k in range(1, 8):
            to_near(k).wait()
            total[...] += arrived[lax.rem(group + 8 - k, 8)].astype(F32)
        if short:
            crossed[high] = total[...].astype(BF16)
            for k in range(1, high_count):
                to_far(k).start()
            last_part(1)
            complete(last_phase - 1)
            for copy in transfers(last_phase):
                copy.start()
            for k in range(1, high_count):
                to_far(k).wait()
            ours = crossed[0].astype(F32)
            for k in range(1, high_count):
                ours = ours + crossed[k].astype(F32)
            total[...] = ours
            for k in range(high_count):
                gathered[low * high_count + k] = ours[SLICE * k : SLICE * k + SLICE, :]
            own_ref[...] = total[rows_of(high, SLICE), :]
        else:
            for k in range(1, high_count):
                to_far(k).start()
            last_part(1)
            complete(last_phase - 1)
            for copy in transfers(last_phase):
                copy.start()
            share[...] = total[rows_of(high, SLICE), :]
            for k in range(1, high_count):
                to_far(k).wait()
                share[...] += crossed[lax.rem(high + high_count - k, high_count)]
            for k in range(1, high_count):
                back_far(k).start()
            gathered[place] = share[...]
            own_ref[...] = share[...]
            for k in range(1, high_count):
                back_far(k).wait()
        for k in range(1, 4):
            back_near(k).start()
        last_part(2)
        complete(last_phase)
        dense_copy().start()
        for k in range(1, 4):
            back_near(k).wait()
        sum_ref[...] = gathered[0:16]
        dense_copy().wait()
        for part in range(3):
            frames_copy(tile, part).wait()


def backward(tiles, anys, hg, lg, active, w1, w2, w3, owners, owner_count, capacity, losses, sum1, sum2):
    lanes = hg.shape[-1]
    small = (hg, lg, active, w1, w2, w3, owners, losses, sum1, sum2)
    totals = [(768, 160), (1024, 192), (1152, 256), (160, LANES), (3136, LANES), (512, LANES)]
    totals += [(576, LANES), (256, LANES)]
    pack_shape = (2 * SLICE * owner_count, LANES)
    dense_shape = (2048, 512)
    frames_shape = (84, 84, 2, lanes)
    high_count = owner_count // 4
    copies = 8 + 2 * high_count + 4
    transfers = 4 * (owner_count.bit_length() - 1)
    return pl.pallas_call(
        functools.partial(backward_kernel, capacity),
        grid=(lanes // LANES,),
        in_specs=[pl.BlockSpec((None,) + a.shape[1:], lambda i: (i, 0, 0, 0)) for a in tiles]
        + [pl.BlockSpec(memory_space=pl.ANY)] * len(anys)
        + [whole(a.shape) for a in small],
        out_specs=[pl.BlockSpec(memory_space=pl.ANY)] * 2 + [whole((16, SLICE, LANES)), whole((SLICE, LANES))],
        out_shape=[jax.ShapeDtypeStruct(s, BF16) for s in (frames_shape, dense_shape)]
        + [jax.ShapeDtypeStruct(s, F32) for s in ((16, SLICE, LANES), (SLICE, LANES))],
        scratch_shapes=[pltpu.VMEM(s, F32) for s in totals + [(pack_shape[0] // 2, LANES)]]
        + [
            pltpu.VMEM((128, 256), BF16),
            pltpu.VMEM((192, 960), BF16),
            pltpu.VMEM((11, 11 * 64, LANES), BF16),
            pltpu.VMEM((11, 11 * 64, LANES), BF16),
            pltpu.VMEM((22, 704, LANES), BF16),
            pltpu.VMEM((84, 168, LANES), BF16),
            pltpu.VMEM((224, 512), BF16),
            pltpu.SemaphoreType.DMA((3,)),
            pltpu.SemaphoreType.DMA,
            pltpu.VMEM((20, 640, LANES), BF16),
            pltpu.VMEM((20, 640, LANES), BF16),
            pltpu.VMEM((512, 512), BF16),
            pltpu.VMEM((16 * 224, 128), BF16),
            pltpu.SemaphoreType.DMA((2,)),
            pltpu.VMEM((44, 336, LANES), BF16),
            pltpu.VMEM((1568, lanes), BF16),
            pltpu.VMEM((3136, 512), BF16),
            pltpu.SemaphoreType.DMA,
            pltpu.VMEM(dense_shape, BF16),
            pltpu.VMEM(dense_shape, BF16),
            pltpu.VMEM(dense_shape, BF16),
            pltpu.SemaphoreType.DMA((2,)),
            pltpu.SemaphoreType.DMA,
            pltpu.SemaphoreType.DMA,
            pltpu.SemaphoreType.DMA((transfers,)),
            pltpu.SemaphoreType.DMA((transfers,)),
            pltpu.VMEM(pack_shape, BF16),
            pltpu.VMEM((8, high_count * SLICE, LANES), BF16),
            pltpu.VMEM((high_count * SLICE, LANES), F32),
            pltpu.VMEM((high_count, high_count * SLICE, LANES), BF16)
            if high_count <= 4
            else pltpu.VMEM((high_count, SLICE, LANES), F32),
            pltpu.VMEM((SLICE, LANES), F32),
            pltpu.VMEM((owner_count, SLICE, LANES), F32),
            pltpu.SemaphoreType.DMA((copies,)),
            pltpu.SemaphoreType.DMA((copies,)),
        ],
        compiler_params=pltpu.CompilerParams(
            collective_id=1, has_side_effects=True, vmem_limit_bytes=60 * 1024 * 1024
        ),
        cost_estimate=pl.CostEstimate(
            flops=3 * 7729152 * lanes, bytes_accessed=6 * 28224 * lanes, transcendentals=0
        ),
    )(*tiles, *anys, *small)


def last_kernel(
    owners,
    loss_scale,
    section_ref,
    frames_any,
    dense_ref,
    sum_ref,
    own_ref,
    out_any,
    one_ref,
    two_ref,
    k1_ref,
    k2_ref,
    k3_ref,
    o1_ref,
    o2_ref,
    o3_ref,
    d1_ref,
    d2_ref,
    loss_ref,
    table_ref,
    buffer,
    in_sems,
    out_sems,
):
    step = pl.program_id(0)
    parts = in_sems.shape[0]
    part_rows = frames_any.shape[0] // parts

    def copy_in(k):
        rows = pl.ds(part_rows * k, part_rows)
        return pltpu.make_async_copy(frames_any.at[rows], buffer.at[rows], in_sems.at[k])

    def copy_out(k):
        rows = pl.ds(part_rows * k, part_rows)
        return pltpu.make_async_copy(buffer.at[rows], out_any.at[rows], out_sems.at[k])

    @pl.when(step == 0)
    def _():
        for k in range(parts):
            copy_in(k).start()
        two_ref[0:464, :] = dense_ref[1568:2032, 0:256].astype(F32)
        two_ref[464:918, :] = dense_ref[1568:2022, 256:512].astype(F32)
        if owners == 16:
            mine = own_ref[pl.ds(pl.multiple_of(8 * section_ref[0], 8), 8), :]
            table_ref[0] = 0.5 * mine[:, 96 : 96 + table_ref.shape[2]]
        for c in range(4):
            k1_ref[64 * c : 64 * c + 64, :] = sum_ref[288:352, 16 * c : 16 * c + 16]
        k2_ref[...] = sum_ref[:, 64:96]
        k3_ref[...] = sum_ref[0:288, 0:64]
        o1_ref[...] = 0.5 * sum_ref[352:353, 0:16]
        o2_ref[...] = 0.5 * sum_ref[353:354, 0:32]
        o3_ref[...] = 0.5 * sum_ref[354:355, 0:32]
        loss_ref[...] = loss_scale * sum_ref[355:356, 0:1]
        for k in range(4):
            d1_ref[:, 64 * k : 64 * k + 64] = 0.5 * sum_ref[384 + k : 385 + k, 0:64]
        for k in range(8):
            size = min(64, 459 - 64 * k)
            d2_ref[:, 64 * k : 64 * k + size] = 0.5 * sum_ref[388 + k : 389 + k, 0:size]

        for k in range(parts):
            copy_in(k).wait()
            copy_out(k).start()

    at = pl.ds(pl.multiple_of(step * 784, 16), 784)
    one_ref[...] = dense_ref[at, :].astype(F32)

    @pl.when(step == pl.num_programs(0) - 1)
    def _():
        for k in range(parts):
            copy_out(k).wait()


def last(owners, capacity, section, frames, dense, sums, own):
    others = [(918, 256), (256, 16), (512, 32), (288, 64), (1, 16), (1, 32), (1, 32), (1, 256), (1, 459), (1, 1), (1, 8, capacity)]
    return pl.pallas_call(
        functools.partial(last_kernel, owners, 0.5 / (frames.shape[3] * owners)),
        grid=(2,),
        in_specs=[
            pl.BlockSpec(memory_space=pltpu.SMEM),
            pl.BlockSpec(memory_space=pl.ANY),
            whole(dense.shape),
            whole(sums.shape),
            whole(own.shape),
        ],
        out_specs=[pl.BlockSpec(memory_space=pl.ANY), pl.BlockSpec((784, 512), lambda i: (i, 0))]
        + [whole(a) for a in others],
        out_shape=[
            jax.ShapeDtypeStruct(frames.shape, BF16),
            jax.ShapeDtypeStruct((1568, 512), F32),
        ]
        + [jax.ShapeDtypeStruct(a, F32) for a in others],
        scratch_shapes=[
            pltpu.VMEM(frames.shape, BF16),
            pltpu.SemaphoreType.DMA((7,)),
            pltpu.SemaphoreType.DMA((7,)),
        ],
        compiler_params=pltpu.CompilerParams(vmem_limit_bytes=60 * 1024 * 1024),
        cost_estimate=pl.CostEstimate(flops=0, bytes_accessed=2**25, transcendentals=0),
    )(section, frames, dense, sums, own)


def shards(
    frames,
    next_frames,
    actions,
    next_actions,
    lengths,
    terminal,
    rewards,
    discounts,
    owners,
    conv_one_weight,
    conv_one_offset,
    conv_two_weight,
    conv_two_offset,
    conv_three_weight,
    conv_three_offset,
    dense_one_weight,
    dense_one_offset,
    dense_two_weight,
    dense_two_offset,
    target_conv_one_weight,
    target_conv_one_offset,
    target_conv_two_weight,
    target_conv_two_offset,
    target_conv_three_weight,
    target_conv_three_offset,
    target_dense_one_weight,
    target_dense_one_offset,
    target_dense_two_weight,
    target_dense_two_offset,
):
    section = lax.axis_index("section")
    owner_count = lax.axis_size("batch")
    rows = frames.shape[0]
    p1, p2, q1 = order_rows(4, 8), order_rows(32, 4), back_one_choice()

    def tower_weights(one, two, three, off_one, off_two, off_three):
        return (
            one.transpose(1, 2, 3, 0).reshape(256, 32),
            two.transpose(1, 2, 3, 0).reshape(512, 64),
            three.transpose(2, 3, 0, 1).reshape(9, 64, 64),
            off_one[None, :],
            off_two[None, :],
            off_three[None, :],
        )

    online = tower_weights(
        conv_one_weight, conv_two_weight, conv_three_weight, conv_one_offset, conv_two_offset, conv_three_offset
    )
    target = tower_weights(
        target_conv_one_weight,
        target_conv_two_weight,
        target_conv_three_weight,
        target_conv_one_offset,
        target_conv_two_offset,
        target_conv_three_offset,
    )
    x = frames.transpose(2, 3, 1, 0)
    x_next = next_frames.transpose(2, 3, 1, 0)
    section_row = section.reshape(1).astype(jnp.int32)
    vectors = [
        a.reshape(a.shape[0] // LANES, LANES)
        for a in (dense_one_offset, target_dense_one_offset, actions, next_actions, lengths, terminal)
    ]
    a1, s1, a2, s2, s3, feature, active, logit_grad, hidden_grad, row_loss, sum1, sum2 = head(
        x,
        x_next,
        dense_one_weight,
        target_dense_one_weight,
        (
            *online,
            *target,
            p1,
            p2,
            dense_two_weight.T,
            target_dense_two_weight.T,
            *vectors,
            dense_two_offset,
            target_dense_two_offset,
            rewards.T,
            discounts.T,
        ),
    )

    capacity = (rows + owner_count - 1) // owner_count + 1
    frames_grad, dense, sums, own = backward(
        (a2, s2, s3),
        (a1, s1, x, feature, dense_one_weight, p2, q1),
        hidden_grad,
        logit_grad,
        active,
        *online[:3],
        owners.T,
        owner_count,
        capacity,
        row_loss,
        sum1,
        sum2,
    )
    frames_grad, grad_dense_one, grad_dense_two, one, two, three, *rest = last(
        owner_count, capacity, section_row, frames_grad, dense, sums.reshape(16 * SLICE, LANES), own
    )
    off_one, off_two, off_three, dense_off_one, dense_off_two, loss, table = rest
    if owner_count != 16:
        groups = -(-owner_count // SLICE)
        table = 0.5 * own[:, 96 : 96 + groups * capacity].reshape(SLICE, groups, capacity)
        table = table.transpose(1, 0, 2).reshape(groups * SLICE, capacity)
        table = lax.dynamic_slice_in_dim(table, section * (owner_count // 2), owner_count // 2, 0)[None]
    return (
        loss[0, 0],
        frames_grad.transpose(3, 2, 0, 1),
        one.reshape(4, 8, 8, 16).transpose(3, 0, 1, 2),
        off_one[0],
        two.reshape(32, 4, 4, 32).transpose(0, 3, 1, 2),
        off_two[0],
        three.reshape(3, 3, 32, 64).transpose(2, 3, 0, 1),
        off_three[0],
        grad_dense_one,
        dense_off_one[0],
        grad_dense_two.T,
        dense_off_two[0],
        table,
    )


def solution(mesh):
    return jax.shard_map(
        shards,
        mesh=mesh,
        in_specs=(P("batch", None, None, None),) * 2
        + (P("batch"),) * 4
        + (P("batch", None),) * 3
        + (P(),) * 20,
        out_specs=(
            P(),
            P("batch", "section", None, None),
            P("section", None, None, None),
            P("section"),
            P("section", None, None, None),
            P("section"),
            P("section", None, None, None),
            P("section"),
            P("section", None),
            P("section"),
            P("section", None),
            P("section"),
            P("batch", "section", None),
        ),
        check_vma=False,
    )
```

```python
import functools

import jax
import jax.numpy as jnp
import numpy as np
from jax import lax
from jax.experimental import pallas as pl
from jax.experimental.pallas import tpu as pltpu
from jax.sharding import PartitionSpec as P

ACTIONS = 18
ATOMS = 51
NSTEP = 3
LANES = 128
SLICE = 32
ROW_CHUNKS = ((0, 12), (12, 24), (24, 36), (36, 52), (52, 68), (68, 84))
MESH = pl.DeviceIdType.MESH
support_low = -10.0
support_high = 10.0
F32 = jnp.float32
BF16 = jnp.bfloat16
NT = (((1,), (1,)), ((), ()))


def nn_dot(a, b):
    return jnp.dot(a, b, preferred_element_type=F32)


def nt_dot(a, b):
    return lax.dot_general(a, b, NT, preferred_element_type=F32)


def stack(parts):
    return jnp.concatenate(parts, axis=0)


def beside(parts):
    return jnp.concatenate(parts, axis=1)


def eye(size):
    rows = lax.broadcasted_iota(jnp.int32, (size, size), 0)
    cols = lax.broadcasted_iota(jnp.int32, (size, size), 1)
    return jnp.where(rows == cols, 1.0, 0.0).astype(BF16)


def order_rows(channels, extent):
    count = channels * extent * extent
    chosen = np.zeros((count, count), np.float32)
    for c in range(channels):
        for u in range(extent):
            for v in range(extent):
                chosen[(u * extent + v) * channels + c, (c * extent + u) * extent + v] = 1.0
    return jnp.asarray(chosen, BF16)


def back_one_choice():
    chosen = np.zeros((2, 8, 4, 28, 2, 128), np.float32)
    for dp in range(2):
        for dq in range(8):
            for i in range(4):
                for x in range(28):
                    u, v = i + 4 * (1 - dp), x + 4 - 4 * dq
                    if 0 <= v < 8:
                        for ch in range(2):
                            chosen[dp, dq, i, x, ch, ch * 64 + u * 8 + v] = 1.0
    return jnp.asarray(chosen.reshape(16 * 224, 128), BF16)


def lane_bias(row, size):
    return nt_dot(eye(size), jnp.broadcast_to(row, (LANES, size)))


def activate(h):
    t = jnp.tanh(h)
    m = h * t
    return h + m, (1.0 + t) * ((1.0 + h) - m)


def in_turn(jobs):
    waiting = None
    for first, then in jobs:
        value = first()
        if waiting is not None:
            waiting[0](waiting[1])
        waiting = (then, value)
    waiting[0](waiting[1])


def whole(shape):
    return pl.BlockSpec(shape, lambda i, *_: (0,) * len(shape))


def by_lane(shape):
    return pl.BlockSpec(shape[:-1] + (LANES,), lambda i, *_: (0,) * (len(shape) - 1) + (i,))


def lane_column(row):
    size = row.shape[1]
    parts = []
    for at in range(0, size, LANES):
        step = min(LANES, size - at)
        parts.append(lane_bias(row[:, at : at + step], step))
    return stack(parts)


def softmax_terms(v):
    top = jnp.max(v, axis=0, keepdims=True)
    e = jnp.exp(v - top)
    total = jnp.sum(e, axis=0, keepdims=True)
    return e / total, v - top - jnp.log(total)


def head_kernel(
    x_any,
    y_any,
    dense_any,
    target_dense_any,
    w1_ref,
    w2_ref,
    w3_ref,
    o1_ref,
    o2_ref,
    o3_ref,
    v1_ref,
    v2_ref,
    v3_ref,
    q1_ref,
    q2_ref,
    q3_ref,
    p1_ref,
    p2_ref,
    out_ref,
    target_out_ref,
    b1_ref,
    d1_ref,
    action_ref,
    later_action_ref,
    length_ref,
    terminal_ref,
    b2_ref,
    d2_ref,
    rewards_ref,
    discounts_ref,
    a1_any,
    s1_any,
    a2_any,
    s2_any,
    s3_any,
    f_any,
    active_ref,
    lg_ref,
    hg_ref,
    loss_ref,
    sum1_ref,
    sum2_ref,
    wt1,
    wt2,
    wt3,
    wt4,
    c1,
    c2,
    c3,
    c4,
    fs,
    fb,
    xbuf,
    a1,
    s1,
    a2,
    s2,
    s3,
    wd,
    wdt,
    pre,
    hidden,
    late,
    back,
    logits,
    logits_later,
    lgs,
    probs,
    position,
    x_sems,
    out_sems,
    wd_sem,
    sent,
    came,
):
    section, batch = lax.axis_index("section"), lax.axis_index("batch")
    step, steps = pl.program_id(0), pl.num_programs(0)
    lanes = hidden.shape[1]
    tiles = lanes // LANES
    targets = tiles - 1
    online = step >= targets
    slot = lax.rem(step, 2)
    height, width, stacked, _ = x_any.shape

    def lanes_of(index):
        return pl.ds(pl.multiple_of(index * LANES, LANES), LANES)

    def x_copy(source, tile, at, k):
        place = lax.rem(at, 2)
        first, last = ROW_CHUNKS[k]
        pixels = source.reshape(height, width * stacked, lanes)
        return pltpu.make_async_copy(
            pixels.at[first:last, :, lanes_of(tile)], xbuf.at[place, first:last], x_sems.at[place, k]
        )

    def start_x(at):
        @pl.when(at < targets)
        def _():
            for k in range(len(ROW_CHUNKS)):
                x_copy(y_any, jnp.minimum(at, targets - 1) + section, at, k).start()

        @pl.when((at >= targets) & (at < steps))
        def _():
            for k in range(len(ROW_CHUNKS)):
                x_copy(x_any, jnp.clip(at - targets, 0, tiles - 1), at, k).start()

    tile = jnp.maximum(step - targets, 0)
    outs = ((a1, a1_any), (s1, s1_any), (a2, a2_any), (s2, s2_any), (s3, s3_any), (fb, f_any))

    def out_copy(k, at):
        source, into = outs[k]
        place = into.at[:, lanes_of(at)] if k == 5 else into.at[at]
        return pltpu.make_async_copy(source, place, out_sems.at[k])

    def wait_outs(which):
        @pl.when(step > targets)
        def _():
            for k in which:
                out_copy(k, jnp.maximum(tile - 1, 0)).wait()

    def start_outs(which):
        @pl.when(online)
        def _():
            for k in which:
                out_copy(k, tile).start()

    def swap():
        return pltpu.make_async_remote_copy(
            src_ref=late.at[:, lanes_of((tiles - 1) * section)],
            dst_ref=late.at[:, lanes_of((tiles - 1) * section)],
            send_sem=sent,
            recv_sem=came,
            device_id=(1 - section, batch),
            device_id_type=MESH,
        )

    def dense_copy(source):
        return pltpu.make_async_copy(source, wd, wd_sem)

    @pl.when(step == 0)
    def _():
        barrier = pltpu.get_barrier_semaphore()
        pl.semaphore_signal(barrier, inc=1, device_id=(1 - section, batch), device_id_type=MESH)
        start_x(step)
        dense_copy(target_dense_any).start()

    start_x(step + 1)

    def prepare(one_ref, two_ref, three_ref, off_one, off_two, off_three):
        wt1[...] = jnp.zeros_like(wt1)
        wt2[...] = jnp.zeros_like(wt2)
        wt3[...] = jnp.zeros_like(wt3)
        base = nt_dot(eye(32), nn_dot(p1_ref[...], one_ref[...]).astype(BF16))
        base = (0.5 * base).astype(BF16)
        for t in range(5):
            for u in range(8):
                wt1[32 * t : 32 * t + 32, 96 * u + 16 * t : 96 * u + 16 * t + 32] = base[:, 32 * u : 32 * u + 32]
        base = nt_dot(eye(64), nn_dot(p2_ref[...], two_ref[...]).astype(BF16))
        base = (0.5 * base).astype(BF16)
        for t in range(3):
            for u in range(4):
                wt2[64 * t : 64 * t + 64, 256 * u + 64 * t : 256 * u + 64 * t + 128] = base[:, 128 * u : 128 * u + 128]
        for u in range(3):
            for v in range(3):
                piece = (0.5 * three_ref[3 * u + v].astype(F32)).astype(BF16)
                wt4[:, 192 * u + 64 * v : 192 * u + 64 * v + 64] = piece
                for t in range(2):
                    at = 256 * u + 64 * t + 64 * v
                    wt3[64 * t : 64 * t + 64, at : at + 64] = piece
        c1[...] = stack([0.5 * lane_bias(off_one[...], 32)] * 5)
        c2[...] = stack([0.5 * lane_bias(off_two[...], 64)] * 3)
        column = 0.5 * lane_bias(off_three[...], 64)
        c3[...] = stack([column] * 2)
        c4[...] = column

    @pl.when(step == 0)
    def _():
        prepare(v1_ref, v2_ref, v3_ref, q1_ref, q2_ref, q3_ref)

    @pl.when(step == targets)
    def _():
        prepare(w1_ref, w2_ref, w3_ref, o1_ref, o2_ref, o3_ref)

    def put(bias, act, slope, places):
        def then(value):
            for k, (row, at, size) in enumerate(places):
                a, s = activate(value[:, LANES * k : LANES * k + LANES] + bias[...])
                act[row, at : at + size, :] = a.astype(BF16)
                slope[row, at : at + size, :] = s.astype(BF16)

        return then

    def strips_one(i, s):
        def dot():
            cols = [
                stack([xbuf[slot, 8 * i + 4 * k + u, 80 * s : 80 * s + 96, :] for u in range(8)])
                for k in range(2)
            ]
            return nn_dot(wt1[...], beside(cols))

        return dot, put(c1, a1, s1, [(2 * i + k, 160 * s, 160) for k in range(2)])

    wait_outs((0, 1))
    for k, pairs in enumerate((range(0, 4), range(4, 10))):
        for n in range(3 * k, 3 * k + 3):
            x_copy(x_any, tile, step, n).wait()
        in_turn([strips_one(i, s) for i in pairs for s in range(4)])
    start_outs((0, 1))
    wait_outs((2, 3, 4, 5))

    def strips_two(places):
        def dot():
            cols = [
                stack([a1[2 * p + u, 192 * s : 192 * s + 256, :] for u in range(4)])
                for p, s in places
            ]
            return nn_dot(wt2[...], beside(cols))

        return dot, put(c2, a2, s2, [(p, 192 * s, 192) for p, s in places])

    def strips_three(places, weight, bias, count):
        def dot():
            cols = [
                stack([a2[p + u, 64 * q : 64 * q + 64 * count + 128, :] for u in range(3)])
                for p, q in places
            ]
            return nn_dot(weight[...], beside(cols))

        def then(value):
            for k, (p, q) in enumerate(places):
                a, s = activate(value[:, LANES * k : LANES * k + LANES] + bias[...])
                for t in range(count):
                    fs[pl.ds(7 * p + q + t, 64, stride=49), :] = a[64 * t : 64 * t + 64, :]
                s3[p, 64 * q : 64 * q + 64 * count, :] = s.astype(BF16)

        return dot, then

    two = [(2 * i + k, s) for i in range(4) for s in range(3) for k in range(2)]
    two += [(8, s) for s in range(3)]
    three = [(p, q) for p in range(7) for q in (0, 2, 4)]
    ends = [(p, 6) for p in range(7)]
    in_turn(
        [strips_two(two[k : k + 2]) for k in range(0, len(two), 2)]
        + [strips_three(three[k : k + 2], wt3, c3, 2) for k in range(0, len(three), 2)]
        + [strips_three(ends[k : k + 2], wt4, c4, 1) for k in range(0, len(ends), 2)]
    )
    fb[...] = fs[...].astype(BF16)
    start_outs((2, 3, 4, 5))

    def turn(source):
        dense_copy(source).wait()
        unit = eye(512)
        for at in range(0, wd.shape[0], 256):
            size = min(256, wd.shape[0] - at)
            wdt[:, at : at + size] = nt_dot(unit, wd[at : at + size, :]).astype(BF16)

    @pl.when(step == 0)
    def _():
        turn(target_dense_any)
        dense_copy(dense_any).start()

    @pl.when(step == targets)
    def _():
        turn(dense_any)

    def column(rows_ref):
        return stack([lane_bias(rows_ref[k : k + 1, :], LANES) for k in range(rows_ref.shape[0])])

    pre[...] = nn_dot(wdt[...], fb[...])

    @pl.when(step < targets)
    def _():
        later, _ = activate(0.5 * (pre[...] + column(d1_ref)))
        late[:, lanes_of(jnp.minimum(step, targets - 1) + section)] = later.astype(BF16)

    @pl.when(step == targets - 1)
    def _():
        pl.semaphore_wait(pltpu.get_barrier_semaphore(), 1)
        swap().start()

    @pl.when(online)
    def _():
        hidden[:, lanes_of(tile)] = pre[...] + column(b1_ref)

    @pl.when(step == steps - 1)
    def _():
        count = out_ref.shape[0]
        back[...] = jnp.zeros_like(back)
        lgs[...] = jnp.zeros_like(lgs)
        for at in range(0, count, 256):
            size = min(256, count - at)
            back[:, at : at + size] = nt_dot(eye(512), out_ref[at : at + size, :]).astype(BF16)

        def wide(ref):
            return beside([lane_column(ref[...].reshape(1, count))] * tiles)

        active, slope = activate(0.5 * hidden[...])
        active = active.astype(BF16)
        active_ref[...] = active
        logits[...] = nn_dot(out_ref[...], active) + wide(b2_ref)
        swap().wait()
        logits_later[...] = nn_dot(target_out_ref[...], late[...]) + wide(d2_ref)

        def row(ref):
            return beside([ref[k : k + 1, :] for k in range(tiles)])

        action, later_action = row(action_ref), row(later_action_ref)
        length, terminal = row(length_ref), row(terminal_ref)

        def pick(ref, ids):
            total = jnp.zeros((ATOMS, lanes), F32)
            for a in range(ACTIONS):
                total = total + jnp.where(ids == a, ref[ATOMS * a : ATOMS * a + ATOMS, :], 0.0)
            return total

        soft, log_soft = softmax_terms(pick(logits, action))
        returns = jnp.zeros((1, lanes), F32)
        bootstrap = jnp.zeros((1, lanes), F32)
        product = jnp.ones((1, lanes), F32)
        for k in range(NSTEP):
            returns = returns + jnp.where(length > k, product * rewards_ref[k : k + 1, :], 0.0)
            product = product * discounts_ref[k : k + 1, :]
            bootstrap = bootstrap + jnp.where(length == k + 1, product, 0.0)
        bootstrap = bootstrap * (1.0 - terminal.astype(F32))
        spacing = (support_high - support_low) / (ATOMS - 1)
        ids = lax.broadcasted_iota(jnp.int32, (ATOMS, lanes), 0).astype(F32)
        shifted = jnp.clip(returns + bootstrap * (support_low + spacing * ids), support_low, support_high)
        position[...] = (shifted - support_low) / spacing
        probs[...], _ = softmax_terms(pick(logits_later, later_action))
        mass = jnp.zeros((ATOMS, lanes), F32)
        for j in range(ATOMS):
            weight = jnp.maximum(0.0, 1.0 - jnp.abs(position[j : j + 1, :] - ids))
            mass = mass + probs[j : j + 1, :] * weight
        loss_ref[...] = -jnp.sum(mass * log_soft, axis=0, keepdims=True)
        chosen_grad = jnp.sum(mass, axis=0, keepdims=True) * soft - mass
        for a in range(ACTIONS):
            lgs[ATOMS * a : ATOMS * a + ATOMS, :] = jnp.where(action == a, chosen_grad, 0.0)
        lg = lgs[...].astype(BF16)
        lg_ref[...] = lg[0:count]
        hg = (nn_dot(back[...], lg) * (0.5 * slope)).astype(BF16)
        hg_ref[...] = hg
        ones = jnp.ones((8, lanes), BF16)
        sum1_ref[...] = nt_dot(ones, hg)
        sum2_ref[...] = nt_dot(ones, lg[0:count])
        for k in range(len(outs)):
            out_copy(k, tile).wait()


def head(x, y, dense_one, target_dense_one, small):
    lanes = x.shape[3]
    count = small[14].shape[0]
    tiles = lanes // LANES
    outs = [(20, 640), (20, 640), (9, 576), (9, 576), (7, 448)]
    outs = [(tiles,) + shape + (LANES,) for shape in outs] + [(3136, lanes)]
    rest = [((512, lanes), BF16), ((count, lanes), BF16), ((512, lanes), BF16), ((1, lanes), F32)]
    rest += [((8, 512), F32), ((8, count), F32)]
    anywhere = pl.BlockSpec(memory_space=pl.ANY)
    buffers = [
        ((160, 768), BF16),
        ((192, 1024), BF16),
        ((128, 768), BF16),
        ((64, 576), BF16),
        ((160, LANES), F32),
        ((192, LANES), F32),
        ((128, LANES), F32),
        ((64, LANES), F32),
        ((3136, LANES), F32),
        ((3136, LANES), BF16),
        ((2, 84, 336, LANES), BF16),
        ((20, 640, LANES), BF16),
        ((20, 640, LANES), BF16),
        ((9, 576, LANES), BF16),
        ((9, 576, LANES), BF16),
        ((7, 448, LANES), BF16),
        ((3136, 512), BF16),
        ((512, 3136), BF16),
        ((512, LANES), F32),
        ((512, lanes), F32),
        ((512, lanes), BF16),
        ((512, 1024), BF16),
        ((count, lanes), F32),
        ((count, lanes), F32),
        ((1024, lanes), F32),
        ((ATOMS, lanes), F32),
        ((ATOMS, lanes), F32),
    ]
    return pl.pallas_call(
        head_kernel,
        grid=(2 * (lanes // LANES) - 1,),
        in_specs=[anywhere] * 4 + [whole(a.shape) for a in small],
        out_specs=[anywhere] * len(outs) + [whole(s) for s, _ in rest],
        out_shape=[jax.ShapeDtypeStruct(s, BF16) for s in outs]
        + [jax.ShapeDtypeStruct(s, t) for s, t in rest],
        scratch_shapes=[pltpu.VMEM(s, t) for s, t in buffers]
        + [
            pltpu.SemaphoreType.DMA((2, len(ROW_CHUNKS))),
            pltpu.SemaphoreType.DMA((len(outs),)),
            pltpu.SemaphoreType.DMA,
            pltpu.SemaphoreType.DMA,
            pltpu.SemaphoreType.DMA,
        ],
        compiler_params=pltpu.CompilerParams(
            collective_id=0, has_side_effects=True, vmem_limit_bytes=60 * 1024 * 1024
        ),
        cost_estimate=pl.CostEstimate(
            flops=5 * 2 * 9785600 * LANES, bytes_accessed=2**26, transcendentals=0
        ),
    )(x, y, dense_one, target_dense_one, *small)


def backward_kernel(
    capacity,
    a2_ref,
    s2_ref,
    s3_ref,
    a1_any,
    s1_any,
    x_any,
    f_any,
    dense_weight_any,
    p2_any,
    q1_any,
    hg_ref,
    lg_ref,
    active_ref,
    w1_ref,
    w2_ref,
    w3_ref,
    owner_ref,
    loss_ref,
    sum1_ref,
    sum2_ref,
    frames_any,
    dense_any,
    sum_ref,
    own_ref,
    t1_ref,
    t2_ref,
    t3_ref,
    tb_ref,
    fcs,
    stage,
    turned,
    first,
    packed,
    wb2,
    wb3,
    g2,
    g3,
    g1,
    frames,
    wb1,
    frame_sems,
    dense_sem,
    a1_ref,
    s1_ref,
    p2_ref,
    q1_ref,
    choice_sems,
    xbuf,
    fbuf,
    dense_weight_ref,
    weight_sem,
    slab,
    landed,
    shared,
    a_sems,
    x_sem,
    f_sem,
    sent,
    came,
    pack,
    arrived,
    total,
    crossed,
    share,
    gathered,
    left,
    reached,
):
    section, batch = lax.axis_index("section"), lax.axis_index("batch")
    owners = lax.axis_size("batch")
    bits = owners.bit_length() - 1
    tile = pl.program_id(0)
    last_tile = pl.num_programs(0) - 1

    dense_rows = slab.shape[0]
    bit = [lax.rem(batch // (1 << k), 2) for k in range(bits)]
    colours = 2 if bits < 7 else 1
    region = dense_rows // (2 * colours)
    orders = [list(range(1, bits)) for _ in range(colours)]
    orders[-1] = orders[-1][(bits - 1) // 2 :] + orders[-1][: (bits - 1) // 2]
    base = (dense_rows // 2) * bit[0]
    bases = []
    for c in range(colours):
        starts = [base + c * region]
        for m, k in enumerate(orders[c]):
            starts.append(starts[-1] + (region >> (m + 1)) * bit[k])
        bases.append(starts)

    def rows_at(start, size):
        return pl.ds(pl.multiple_of(start, 16), size)

    def moves(phase):
        if phase in (0, 2 * bits - 1):
            half = dense_rows // 2
            if phase:
                return [(0, base, half, None, None)]
            return [(0, half * (1 - bit[0]), half, 0, base)]
        found = []
        for c in range(colours):
            m = phase - 1 if phase < bits else 2 * bits - 2 - phase
            size = region >> (m + 1)
            k, start = orders[c][m], bases[c][m]
            if phase < bits:
                place = dense_rows // 2 + (c + 1) * region - 2 * size
                found.append((k, start + size * (1 - bit[k]), size, place, bases[c][m + 1]))
            else:
                found.append((k, bases[c][m + 1], size, None, None))
        return found

    def transfers(phase):
        copies = []
        for c, (k, start, size, place, _) in enumerate(moves(phase)):
            if phase < bits:
                source, into = slab.at[rows_at(start, size), :], landed.at[pl.ds(place, size), :]
            else:
                source = into = shared.at[rows_at(start, size), :]
            copies.append(
                pltpu.make_async_remote_copy(
                    src_ref=source,
                    dst_ref=into,
                    send_sem=sent.at[2 * phase + c],
                    recv_sem=came.at[2 * phase + c],
                    device_id=(section, batch + (1 << k) * (1 - 2 * bit[k])),
                    device_id_type=MESH,
                )
            )
        return copies

    def complete(phase):
        for copy, (_, _, size, place, to) in zip(transfers(phase), moves(phase)):
            copy.wait()
            if phase < bits:
                step = min(size, 64)

                def add(n, carry, step=step, place=place, to=to):
                    at = rows_at(to + step * n, step)
                    more = landed[pl.ds(pl.multiple_of(place + step * n, 16), step), :]
                    slab[at, :] = (slab[at, :].astype(F32) + more.astype(F32)).astype(BF16)
                    return carry

                lax.fori_loop(0, size // step, add, 0)
        if phase == bits - 1:
            for c in range(colours):
                own = rows_at(bases[c][-1], region >> (bits - 1))
                shared[own, :] = slab[own, :]

    starts = [0, 1, 2, 3, 5, 6, 8]
    if bits != 4:
        starts = [9 * phase // (2 * bits - 1) for phase in range(2 * bits - 1)]
    last_phase = 2 * bits - 1

    def slot(index):
        for phase, at in enumerate(starts):
            if phase > 0 and at % 3 == index:

                @pl.when(tile == at // 3)
                def _(phase=phase):
                    complete(phase - 1)
                    for copy in transfers(phase):
                        copy.start()

    high_count = owners // 4
    block = high_count * SLICE
    low, high = lax.rem(batch, 4), batch // 4
    group = section * 4 + low
    place = low * high_count + high

    def near(k):
        index = lax.rem(group + k, 8)
        return index, (index // 4, high * 4 + lax.rem(index, 4))

    def far(k):
        index = lax.rem(high + k, high_count)
        return index, (section, index * 4 + low)

    def send(source, into, device, number):
        return pltpu.make_async_remote_copy(
            src_ref=source,
            dst_ref=into,
            send_sem=left.at[number],
            recv_sem=reached.at[number],
            device_id=device,
            device_id_type=MESH,
        )

    def rows_of(index, size):
        return pl.ds(pl.multiple_of(index * size, size), size)

    def to_near(k):
        index, device = near(k)
        return send(pack.at[rows_of(index, block), :], arrived.at[group], device, k)

    short = high_count <= 4

    def to_far(k):
        index, device = far(k)
        source = crossed.at[high] if short else total.at[rows_of(index, SLICE), :]
        return send(source, crossed.at[high], device, 8 + k)

    def back_far(k):
        return send(share, gathered.at[place], far(k)[1], 8 + high_count + k)

    def back_near(k):
        ours = gathered.at[pl.ds(low * high_count, high_count)]
        device = (section, high * 4 + lax.rem(low + k, 4))
        return send(ours, ours, device, 8 + 2 * high_count + k)

    def a_copy(at, k):
        source, into = ((a1_any, a1_ref), (s1_any, s1_ref))[k]
        return pltpu.make_async_copy(source.at[at], into, a_sems.at[k])

    def dense_copy():
        return pltpu.make_async_copy(shared, dense_any, dense_sem)

    height, width, stacked, lane_count = x_any.shape
    pixels = x_any.reshape(height, width * stacked, lane_count)

    def x_copy():
        return pltpu.make_async_copy(
            pixels.at[pl.ds(40 * section, 44), :, pl.ds(pl.multiple_of(tile * LANES, LANES), LANES)],
            xbuf,
            x_sem,
        )

    def f_copy():
        half = fbuf.shape[0]
        return pltpu.make_async_copy(f_any.at[rows_at(half * section, half), :], fbuf, f_sem)

    def choice_copy(k):
        source, into = ((p2_any, p2_ref), (q1_any, q1_ref))[k]
        return pltpu.make_async_copy(source, into, choice_sems.at[k])

    def weight_copy():
        return pltpu.make_async_copy(dense_weight_any, dense_weight_ref, weight_sem)

    @pl.when(tile == 0)
    def _():
        f_copy().start()
        barrier = pltpu.get_barrier_semaphore()
        for k in range(1, 8):
            pl.semaphore_signal(barrier, inc=1, device_id=near(k)[1], device_id_type=MESH)
        for k in range(1, high_count):
            pl.semaphore_signal(barrier, inc=1, device_id=far(k)[1], device_id_type=MESH)
        f_copy().wait()
        for k in range(2):
            choice_copy(k).start()
        weight_copy().start()
        for k in range(2):
            a_copy(tile, k).start()

        def dense_one(start, stop):
            for at in range(start, stop, 256):
                rows = slice(at, min(at + 256, stop))
                slab[rows, :] = nt_dot(fbuf[rows, :], hg_ref[...]).astype(BF16)

        def upper_half():
            slab[1568:dense_rows, :] = jnp.zeros((dense_rows - 1568, 512), BF16)
            mine = active_ref[pl.ds(pl.multiple_of(256 * section, 256), 256), :]
            slab[1568:2032, 0:256] = nt_dot(lg_ref[0:464, :], mine).astype(BF16)
            slab[1568:2022, 256:512] = nt_dot(lg_ref[464:918, :], mine).astype(BF16)
            dense_one(1024, 1568)

        @pl.when(bit[0] == 0)
        def _():
            upper_half()

        @pl.when(bit[0] == 1)
        def _():
            dense_one(0, 1024)

        pl.semaphore_wait(barrier, 6 + high_count)
        for copy in transfers(0):
            copy.start()

        @pl.when(bit[0] == 0)
        def _():
            dense_one(0, 1024)

        @pl.when(bit[0] == 1)
        def _():
            upper_half()

        for ref in (t1_ref, t2_ref, t3_ref, tb_ref, wb1, wb2, wb3):
            ref[...] = jnp.zeros_like(ref)
        for ref, edge, width in ((g1, 1, 32), (g2, 1, 64), (g3, 2, 64)):
            side = jnp.zeros((edge * width, LANES), BF16)
            for r in range(ref.shape[0]):
                if edge <= r < ref.shape[0] - edge:
                    ref[r, 0 : edge * width, :] = side
                    ref[r, ref.shape[1] - edge * width :, :] = side
                else:
                    ref[r] = jnp.zeros((ref.shape[1], LANES), BF16)
        for k in range(2):
            choice_copy(k).wait()
        rows = (0.5 * nn_dot(p2_ref[...], w2_ref[...])).astype(BF16)
        for dp in range(2):
            for dq in range(2):
                for b in range(2):
                    for x in range(2):
                        u, v = b + 2 * (1 - dp), x + 2 * (1 - dq)
                        to, at, of = 32 * (2 * b + x), 64 * (2 * dp + dq), 32 * (4 * u + v)
                        wb2[to : to + 32, at : at + 64] = rows[of : of + 32, :]
        for u in range(3):
            for v in range(3):
                piece = (0.5 * nt_dot(eye(64), w3_ref[3 * u + v])).astype(BF16)
                for t in range(3):
                    at = 320 * (2 - u) + 64 * (t + 2 - v)
                    wb3[64 * t : 64 * t + 64, at : at + 64] = piece
        half = w1_ref[pl.ds(pl.multiple_of(section * 128, 128), 128), :]
        pieces = nn_dot(q1_ref[...], half).astype(BF16)
        for k in range(16):
            wb1[:, 32 * k : 32 * k + 32] = pieces[224 * k : 224 * k + 224, :]
        weight_copy().wait()

    slot(0)
    x_copy().start()

    def sums(value, size):
        total = value[0:size]
        for at in range(size, value.shape[0], size):
            total = total + value[at : at + size]
        return total

    hg = hg_ref[:, pl.ds(pl.multiple_of(tile * LANES, LANES), LANES)]

    def feature_grad(n, carry):
        at = pl.ds(pl.multiple_of(448 * n, 448), 448)
        fcs[at, :] = 0.5 * nn_dot(dense_weight_ref[at, :], hg).astype(BF16).astype(F32)
        return carry

    lax.fori_loop(0, 7, feature_grad, 0, unroll=True)

    def cot_three(p, carry):
        cot = stack([fcs[pl.ds(7 * p + q, 64, stride=49), :] for q in range(7)])
        g = cot * s3_ref[p].astype(F32)
        g3[p + 2, 128:576, :] = g.astype(BF16)
        tb_ref[96:160, :] += sums(g, 64)
        return carry

    lax.fori_loop(0, 7, cot_three, 0, unroll=True)

    blocks, cots = [], []
    nothing = jnp.zeros((64, LANES), BF16)
    for n in range(4):
        p = 4 * section + n
        rows = [jnp.minimum(p + u, 8) for u in range(3)]
        blocks.append(stack([a2_ref[r, 0:384, :] for r in rows]))
        blocks.append(stack([part for r in rows for part in (a2_ref[r, 256:576, :], nothing)]))
        cots += [g3[p + 2, 128:384, :], g3[p + 2, 384:640, :]]
    t3_ref[...] += nt_dot(beside(blocks), beside(cots))


    def patch_three(y, s):
        return stack([g3[y + d, 192 * s : 192 * s + 320, :] for d in range(3)])

    def strips_two(places):
        def dot():
            return nn_dot(wb3[...], beside([patch_three(y, s) for y, s in places]))

        def then(value):
            for k, (y, s) in enumerate(places):
                slope = s2_ref[y, 192 * s : 192 * s + 192, :].astype(F32)
                g = value[:, LANES * k : LANES * k + LANES] * slope
                g2[y + 1, 64 + 192 * s : 256 + 192 * s, :] = g.astype(BF16)
                tb_ref[32:96, :] += sums(g, 64)

        return dot, then

    pairs = [(2 * i, s) for i in range(4) for s in range(3)]
    in_turn(
        [strips_two([(y, s), (y + 1, s)]) for y, s in pairs]
        + [strips_two([(8, 0), (8, 1)]), strips_two([(8, 2)])]
    )

    slot(1)
    a_copy(tile, 0).wait()
    a_copy(tile, 1).wait()

    blocks, cots = [], []
    for n in range(5):
        p = 5 * section + n
        rows = [jnp.minimum(2 * p + u, 19) for u in range(4)]
        for q in range(3):
            blocks.append(stack([a1_ref[r, 192 * q : 192 * q + 256, :] for r in rows]))
            cots.append(g2[p + 1, 64 + 192 * q : 256 + 192 * q, :])
    t2_ref[...] += nt_dot(beside(blocks), beside(cots))


    def back_two(i):
        def strip(s):
            def dot():
                cols = [
                    stack([g2[2 * i + k + d, 64 * s : 64 * s + 128, :] for d in range(2)])
                    for k in range(2)
                ]
                return nn_dot(wb2[...], beside(cols))

            def then(v):
                total = jnp.zeros((32, LANES), F32)
                for k in range(2):
                    for b in range(2):
                        row = 4 * i + 2 * k + b
                        slope = s1_ref[row, 64 * s : 64 * s + 64, :].astype(F32)
                        g = v[64 * b : 64 * b + 64, LANES * k : LANES * k + LANES] * slope
                        g1[row + 1, 32 + 64 * s : 96 + 64 * s, :] = g.astype(BF16)
                        total = total + sums(g, 32)
                tb_ref[0:32, :] += total

            return dot, then

        return [strip(s) for s in range(10)]

    in_turn([job for i in range(5) for job in back_two(i)])
    slot(2)

    @pl.when(tile < last_tile)
    def _():
        for k in range(2):
            a_copy(tile + 1, k).start()

    x_copy().wait()

    for first_row in (0, 5):
        blocks, cots = [], []
        for n in range(first_row, first_row + 5):
            for q in range(4):
                blocks.append(stack([xbuf[4 * n + u, 80 * q : 80 * q + 96, :] for u in range(8)]))
                cots.append(g1[10 * section + n + 1, 32 + 160 * q : 192 + 160 * q, :])
        t1_ref[...] += nt_dot(beside(blocks), beside(cots))


    height, width, channels, lane_count = frames_any.shape
    out_pixels = frames_any.reshape(height, width * channels, lane_count)

    def frames_copy(at, part):
        lanes = pl.ds(pl.multiple_of(at * LANES, LANES), LANES)
        rows = pl.ds(28 * part, 28)
        return pltpu.make_async_copy(frames.at[rows], out_pixels.at[rows, :, lanes], frame_sems.at[part])

    def frames_part(part):
        def strips(places):
            def dot():
                cols = [
                    stack([g1[7 * part + a + d, 224 * s : 224 * s + 256, :] for d in range(2)])
                    for a, s in places
                ]
                return nn_dot(wb1[...], beside(cols))

            def then(v):
                for k, (a, s) in enumerate(places):
                    for i in range(4):
                        frames[28 * part + 4 * a + i, 56 * s : 56 * s + 56, :] = v[
                            56 * i : 56 * i + 56, LANES * k : LANES * k + LANES
                        ].astype(BF16)

            return dot, then

        places = [(a, s) for a in range(7) for s in range(3)]
        in_turn([strips(places[k : k + 2]) for k in range(0, len(places), 2)])

    @pl.when(tile < last_tile)
    def _():
        def one_part(part, carry):
            @pl.when(tile > 0)
            def _():
                frames_copy(tile - 1, part).wait()

            frames_part(part)
            frames_copy(tile, part).start()
            return carry

        lax.fori_loop(0, 3, one_part, 0)

    def last_part(part):
        frames_copy(tile - 1, part).wait()
        frames_part(part)
        frames_copy(tile, part).start()

    @pl.when(tile == last_tile)
    def _():
        rows = owner_ref.shape[1]
        half_rows = SLICE * owners
        owner_hot = owner_ref[...] == lax.broadcasted_iota(jnp.int32, (owners, rows), 0)
        owner_hot = jnp.where(owner_hot, 1.0, 0.0)
        before = lax.broadcasted_iota(jnp.int32, (rows, rows), 0)
        before = before < lax.broadcasted_iota(jnp.int32, (rows, rows), 1)
        before = nn_dot(owner_hot.astype(BF16), jnp.where(before, 1.0, 0.0).astype(BF16))
        slots = jnp.sum(before * owner_hot, axis=0, keepdims=True)
        slot_ids = lax.broadcasted_iota(jnp.int32, (32, rows), 0)
        slot_ids = slot_ids - capacity * (batch // SLICE)
        slot_hot = jnp.where(slots.astype(jnp.int32) == slot_ids, 1.0, 0.0).astype(BF16)
        outgoing = nt_dot((owner_hot * loss_ref[...]).astype(BF16), slot_hot)
        count = sum2_ref.shape[1] // 2
        for k in range(9):
            u, v = k // 3, k % 3
            pieces = [
                t3_ref[384 * u + 64 * (q + v) : 384 * u + 64 * (q + v) + 64, 64 * q : 64 * q + 64]
                for q in range(4)
            ]
            turned[64 * k : 64 * k + 64, 0:64] = functools.reduce(jnp.add, pieces)
        for k in range(16):
            u, v = k // 4, k % 4
            pieces = [
                t2_ref[256 * u + 32 * (2 * q + v) : 256 * u + 32 * (2 * q + v) + 32, 64 * q : 64 * q + 64]
                for q in range(3)
            ]
            turned[32 * k : 32 * k + 32, 64:128] = functools.reduce(jnp.add, pieces)
        for u in range(8):
            pieces = [
                t1_ref[96 * u + 16 * q : 96 * u + 16 * q + 32, 32 * q : 32 * q + 32] for q in range(5)
            ]
            first[32 * u : 32 * u + 32, 0:32] = functools.reduce(jnp.add, pieces)
        both = jnp.transpose(turned[...])
        ones = jnp.ones((8, LANES), F32)
        bias = lax.dot_general(
            ones, tb_ref[...], NT, precision=lax.Precision.HIGHEST, preferred_element_type=F32
        )
        for h in range(2):
            packed[...] = jnp.zeros_like(packed)
            for k in range(9):
                packed[32 * k : 32 * k + 32, 0:64] = both[32 * h : 32 * h + 32, 64 * k : 64 * k + 64]
            for k in range(16):
                piece = both[64 + 32 * h : 96 + 32 * h, 32 * k : 32 * k + 32]
                stage[pl.ds(k, 32, stride=16), :] = jnp.pad(piece, ((0, 0), (0, 96)))
            packed[0:512, 64:96] = stage[:, 0:32]
            for c in range(4):
                rows_c = first[pl.ds(c, 64, stride=4), :]
                packed[288 : 352, 16 * c : 16 * c + 16] = rows_c[:, 16 * h : 16 * h + 16]
            packed[352 : 353, 0:16] = bias[0:1, 16 * h : 16 * h + 16]
            packed[353 : 354, 0:32] = bias[0:1, 32 + 32 * h : 64 + 32 * h]
            packed[354 : 355, 0:32] = bias[0:1, 96 + 32 * h : 128 + 32 * h]
            packed[355 : 356, 0:1] = jnp.sum(loss_ref[...], axis=1, keepdims=True)
            for k in range(4):
                packed[384 + k : 385 + k, 0:64] = sum1_ref[0:1, 256 * h + 64 * k : 256 * h + 64 * k + 64]
            for k in range(8):
                at = 64 * k
                size = min(64, count - at)
                packed[388 + k : 389 + k, 0:size] = sum2_ref[0:1, count * h + at : count * h + at + size]
            for o in range(owners):
                at = SLICE * ((o % 4) * (owners // 4) + o // 4)
                packed[pl.ds(at + lax.rem(batch, SLICE), 1), 96:128] = outgoing[o : o + 1, :]
            pack[half_rows * h : half_rows * h + half_rows, :] = packed[...].astype(BF16)
        for k in range(1, 8):
            to_near(k).start()
        last_part(0)
        total[...] = pack[rows_of(group, block), :].astype(F32)
        for k in range(1, 8):
            to_near(k).wait()
            total[...] += arrived[lax.rem(group + 8 - k, 8)].astype(F32)
        if short:
            crossed[high] = total[...].astype(BF16)
            for k in range(1, high_count):
                to_far(k).start()
            last_part(1)
            complete(last_phase - 1)
            for copy in transfers(last_phase):
                copy.start()
            for k in range(1, high_count):
                to_far(k).wait()
            ours = crossed[0].astype(F32)
            for k in range(1, high_count):
                ours = ours + crossed[k].astype(F32)
            total[...] = ours
            for k in range(high_count):
                gathered[low * high_count + k] = ours[SLICE * k : SLICE * k + SLICE, :]
            own_ref[...] = total[rows_of(high, SLICE), :]
        else:
            for k in range(1, high_count):
                to_far(k).start()
            last_part(1)
            complete(last_phase - 1)
            for copy in transfers(last_phase):
                copy.start()
            share[...] = total[rows_of(high, SLICE), :]
            for k in range(1, high_count):
                to_far(k).wait()
                share[...] += crossed[lax.rem(high + high_count - k, high_count)]
            for k in range(1, high_count):
                back_far(k).start()
            gathered[place] = share[...]
            own_ref[...] = share[...]
            for k in range(1, high_count):
                back_far(k).wait()
        for k in range(1, 4):
            back_near(k).start()
        last_part(2)
        complete(last_phase)
        dense_copy().start()
        for k in range(1, 4):
            back_near(k).wait()
        sum_ref[...] = gathered[0:16]
        dense_copy().wait()
        for part in range(3):
            frames_copy(tile, part).wait()


def backward(tiles, anys, hg, lg, active, w1, w2, w3, owners, owner_count, capacity, losses, sum1, sum2):
    lanes = hg.shape[-1]
    small = (hg, lg, active, w1, w2, w3, owners, losses, sum1, sum2)
    totals = [(768, 160), (1024, 192), (1152, 256), (160, LANES), (3136, LANES), (512, LANES)]
    totals += [(576, LANES), (256, LANES)]
    pack_shape = (2 * SLICE * owner_count, LANES)
    dense_shape = (2048, 512)
    frames_shape = (84, 84, 2, lanes)
    high_count = owner_count // 4
    copies = 8 + 2 * high_count + 4
    transfers = 4 * (owner_count.bit_length() - 1)
    return pl.pallas_call(
        functools.partial(backward_kernel, capacity),
        grid=(lanes // LANES,),
        in_specs=[pl.BlockSpec((None,) + a.shape[1:], lambda i: (i, 0, 0, 0)) for a in tiles]
        + [pl.BlockSpec(memory_space=pl.ANY)] * len(anys)
        + [whole(a.shape) for a in small],
        out_specs=[pl.BlockSpec(memory_space=pl.ANY)] * 2 + [whole((16, SLICE, LANES)), whole((SLICE, LANES))],
        out_shape=[jax.ShapeDtypeStruct(s, BF16) for s in (frames_shape, dense_shape)]
        + [jax.ShapeDtypeStruct(s, F32) for s in ((16, SLICE, LANES), (SLICE, LANES))],
        scratch_shapes=[pltpu.VMEM(s, F32) for s in totals + [(pack_shape[0] // 2, LANES)]]
        + [
            pltpu.VMEM((128, 256), BF16),
            pltpu.VMEM((192, 960), BF16),
            pltpu.VMEM((11, 11 * 64, LANES), BF16),
            pltpu.VMEM((11, 11 * 64, LANES), BF16),
            pltpu.VMEM((22, 704, LANES), BF16),
            pltpu.VMEM((84, 168, LANES), BF16),
            pltpu.VMEM((224, 512), BF16),
            pltpu.SemaphoreType.DMA((3,)),
            pltpu.SemaphoreType.DMA,
            pltpu.VMEM((20, 640, LANES), BF16),
            pltpu.VMEM((20, 640, LANES), BF16),
            pltpu.VMEM((512, 512), BF16),
            pltpu.VMEM((16 * 224, 128), BF16),
            pltpu.SemaphoreType.DMA((2,)),
            pltpu.VMEM((44, 336, LANES), BF16),
            pltpu.VMEM((1568, lanes), BF16),
            pltpu.VMEM((3136, 512), BF16),
            pltpu.SemaphoreType.DMA,
            pltpu.VMEM(dense_shape, BF16),
            pltpu.VMEM(dense_shape, BF16),
            pltpu.VMEM(dense_shape, BF16),
            pltpu.SemaphoreType.DMA((2,)),
            pltpu.SemaphoreType.DMA,
            pltpu.SemaphoreType.DMA,
            pltpu.SemaphoreType.DMA((transfers,)),
            pltpu.SemaphoreType.DMA((transfers,)),
            pltpu.VMEM(pack_shape, BF16),
            pltpu.VMEM((8, high_count * SLICE, LANES), BF16),
            pltpu.VMEM((high_count * SLICE, LANES), F32),
            pltpu.VMEM((high_count, high_count * SLICE, LANES), BF16)
            if high_count <= 4
            else pltpu.VMEM((high_count, SLICE, LANES), F32),
            pltpu.VMEM((SLICE, LANES), F32),
            pltpu.VMEM((owner_count, SLICE, LANES), F32),
            pltpu.SemaphoreType.DMA((copies,)),
            pltpu.SemaphoreType.DMA((copies,)),
        ],
        compiler_params=pltpu.CompilerParams(
            collective_id=1, has_side_effects=True, vmem_limit_bytes=60 * 1024 * 1024
        ),
        cost_estimate=pl.CostEstimate(
            flops=3 * 7729152 * lanes, bytes_accessed=6 * 28224 * lanes, transcendentals=0
        ),
    )(*tiles, *anys, *small)


def last_kernel(
    owners,
    loss_scale,
    section_ref,
    frames_any,
    dense_ref,
    sum_ref,
    own_ref,
    out_any,
    one_ref,
    two_ref,
    k1_ref,
    k2_ref,
    k3_ref,
    o1_ref,
    o2_ref,
    o3_ref,
    d1_ref,
    d2_ref,
    loss_ref,
    table_ref,
    buffer,
    in_sems,
    out_sems,
):
    step = pl.program_id(0)
    parts = in_sems.shape[0]
    part_rows = frames_any.shape[0] // parts

    def copy_in(k):
        rows = pl.ds(part_rows * k, part_rows)
        return pltpu.make_async_copy(frames_any.at[rows], buffer.at[rows], in_sems.at[k])

    def copy_out(k):
        rows = pl.ds(part_rows * k, part_rows)
        return pltpu.make_async_copy(buffer.at[rows], out_any.at[rows], out_sems.at[k])

    @pl.when(step == 0)
    def _():
        for k in range(parts):
            copy_in(k).start()
        two_ref[0:464, :] = dense_ref[1568:2032, 0:256].astype(F32)
        two_ref[464:918, :] = dense_ref[1568:2022, 256:512].astype(F32)
        if owners == 16:
            mine = own_ref[pl.ds(pl.multiple_of(8 * section_ref[0], 8), 8), :]
            table_ref[0] = 0.5 * mine[:, 96 : 96 + table_ref.shape[2]]
        for c in range(4):
            k1_ref[64 * c : 64 * c + 64, :] = sum_ref[288:352, 16 * c : 16 * c + 16]
        k2_ref[...] = sum_ref[:, 64:96]
        k3_ref[...] = sum_ref[0:288, 0:64]
        o1_ref[...] = 0.5 * sum_ref[352:353, 0:16]
        o2_ref[...] = 0.5 * sum_ref[353:354, 0:32]
        o3_ref[...] = 0.5 * sum_ref[354:355, 0:32]
        loss_ref[...] = loss_scale * sum_ref[355:356, 0:1]
        for k in range(4):
            d1_ref[:, 64 * k : 64 * k + 64] = 0.5 * sum_ref[384 + k : 385 + k, 0:64]
        for k in range(8):
            size = min(64, 459 - 64 * k)
            d2_ref[:, 64 * k : 64 * k + size] = 0.5 * sum_ref[388 + k : 389 + k, 0:size]

        for k in range(parts):
            copy_in(k).wait()
            copy_out(k).start()

    at = pl.ds(pl.multiple_of(step * 784, 16), 784)
    one_ref[...] = dense_ref[at, :].astype(F32)

    @pl.when(step == pl.num_programs(0) - 1)
    def _():
        for k in range(parts):
            copy_out(k).wait()


def last(owners, capacity, section, frames, dense, sums, own):
    others = [(918, 256), (256, 16), (512, 32), (288, 64), (1, 16), (1, 32), (1, 32), (1, 256), (1, 459), (1, 1), (1, 8, capacity)]
    return pl.pallas_call(
        functools.partial(last_kernel, owners, 0.5 / (frames.shape[3] * owners)),
        grid=(2,),
        in_specs=[
            pl.BlockSpec(memory_space=pltpu.SMEM),
            pl.BlockSpec(memory_space=pl.ANY),
            whole(dense.shape),
            whole(sums.shape),
            whole(own.shape),
        ],
        out_specs=[pl.BlockSpec(memory_space=pl.ANY), pl.BlockSpec((784, 512), lambda i: (i, 0))]
        + [whole(a) for a in others],
        out_shape=[
            jax.ShapeDtypeStruct(frames.shape, BF16),
            jax.ShapeDtypeStruct((1568, 512), F32),
        ]
        + [jax.ShapeDtypeStruct(a, F32) for a in others],
        scratch_shapes=[
            pltpu.VMEM(frames.shape, BF16),
            pltpu.SemaphoreType.DMA((7,)),
            pltpu.SemaphoreType.DMA((7,)),
        ],
        compiler_params=pltpu.CompilerParams(vmem_limit_bytes=60 * 1024 * 1024),
        cost_estimate=pl.CostEstimate(flops=0, bytes_accessed=2**25, transcendentals=0),
    )(section, frames, dense, sums, own)


def shards(
    frames,
    next_frames,
    actions,
    next_actions,
    lengths,
    terminal,
    rewards,
    discounts,
    owners,
    conv_one_weight,
    conv_one_offset,
    conv_two_weight,
    conv_two_offset,
    conv_three_weight,
    conv_three_offset,
    dense_one_weight,
    dense_one_offset,
    dense_two_weight,
    dense_two_offset,
    target_conv_one_weight,
    target_conv_one_offset,
    target_conv_two_weight,
    target_conv_two_offset,
    target_conv_three_weight,
    target_conv_three_offset,
    target_dense_one_weight,
    target_dense_one_offset,
    target_dense_two_weight,
    target_dense_two_offset,
):
    section = lax.axis_index("section")
    owner_count = lax.axis_size("batch")
    rows = frames.shape[0]
    p1, p2, q1 = order_rows(4, 8), order_rows(32, 4), back_one_choice()

    def tower_weights(one, two, three, off_one, off_two, off_three):
        return (
            one.transpose(1, 2, 3, 0).reshape(256, 32),
            two.transpose(1, 2, 3, 0).reshape(512, 64),
            three.transpose(2, 3, 0, 1).reshape(9, 64, 64),
            off_one[None, :],
            off_two[None, :],
            off_three[None, :],
        )

    online = tower_weights(
        conv_one_weight, conv_two_weight, conv_three_weight, conv_one_offset, conv_two_offset, conv_three_offset
    )
    target = tower_weights(
        target_conv_one_weight,
        target_conv_two_weight,
        target_conv_three_weight,
        target_conv_one_offset,
        target_conv_two_offset,
        target_conv_three_offset,
    )
    x = frames.transpose(2, 3, 1, 0)
    x_next = next_frames.transpose(2, 3, 1, 0)
    section_row = section.reshape(1).astype(jnp.int32)
    vectors = [
        a.reshape(a.shape[0] // LANES, LANES)
        for a in (dense_one_offset, target_dense_one_offset, actions, next_actions, lengths, terminal)
    ]
    a1, s1, a2, s2, s3, feature, active, logit_grad, hidden_grad, row_loss, sum1, sum2 = head(
        x,
        x_next,
        dense_one_weight,
        target_dense_one_weight,
        (
            *online,
            *target,
            p1,
            p2,
            dense_two_weight.T,
            target_dense_two_weight.T,
            *vectors,
            dense_two_offset,
            target_dense_two_offset,
            rewards.T,
            discounts.T,
        ),
    )

    capacity = (rows + owner_count - 1) // owner_count + 1
    frames_grad, dense, sums, own = backward(
        (a2, s2, s3),
        (a1, s1, x, feature, dense_one_weight, p2, q1),
        hidden_grad,
        logit_grad,
        active,
        *online[:3],
        owners.T,
        owner_count,
        capacity,
        row_loss,
        sum1,
        sum2,
    )
    frames_grad, grad_dense_one, grad_dense_two, one, two, three, *rest = last(
        owner_count, capacity, section_row, frames_grad, dense, sums.reshape(16 * SLICE, LANES), own
    )
    off_one, off_two, off_three, dense_off_one, dense_off_two, loss, table = rest
    if owner_count != 16:
        groups = -(-owner_count // SLICE)
        table = 0.5 * own[:, 96 : 96 + groups * capacity].reshape(SLICE, groups, capacity)
        table = table.transpose(1, 0, 2).reshape(groups * SLICE, capacity)
        table = lax.dynamic_slice_in_dim(table, section * (owner_count // 2), owner_count // 2, 0)[None]
    return (
        loss[0, 0],
        frames_grad.transpose(3, 2, 0, 1),
        one.reshape(4, 8, 8, 16).transpose(3, 0, 1, 2),
        off_one[0],
        two.reshape(32, 4, 4, 32).transpose(0, 3, 1, 2),
        off_two[0],
        three.reshape(3, 3, 32, 64).transpose(2, 3, 0, 1),
        off_three[0],
        grad_dense_one,
        dense_off_one[0],
        grad_dense_two.T,
        dense_off_two[0],
        table,
    )


def solution(mesh):
    return jax.shard_map(
        shards,
        mesh=mesh,
        in_specs=(P("batch", None, None, None),) * 2
        + (P("batch"),) * 4
        + (P("batch", None),) * 3
        + (P(),) * 20,
        out_specs=(
            P(),
            P("batch", "section", None, None),
            P("section", None, None, None),
            P("section"),
            P("section", None, None, None),
            P("section"),
            P("section", None, None, None),
            P("section"),
            P("section", None),
            P("section"),
            P("section", None),
            P("section"),
            P("batch", "section", None),
        ),
        check_vma=False,
    )
```
